32 devices in a mesh: seq: 4 (over x, core), fsdp: 8 (over z, y).
Axes of the slice: x: 2, y: 2, z: 4, core: 2. Of those that a mesh axis runs over, the one named last changes fastest.
Arguments:
- tokens: bfloat16 [8, 2048, 1152], P('fsdp', 'seq'), may hold values from -6 to 6
- patch_mask: int32 [8, 2048], P('fsdp', 'seq'), may hold values from 0 to 1, as said below
- gain_one: bfloat16 [1152], P('seq'), may hold values from 0.25 to 1.75
- shift_one: bfloat16 [1152], P('seq'), may hold values from -3 to 3
- w_query: bfloat16 [1152, 1152], P('fsdp', 'seq'), may hold values from -0.25 to 0.25
- b_query: bfloat16 [1152], P('seq'), may hold values from -3 to 3
- w_key: bfloat16 [1152, 1152], P('fsdp', 'seq'), may hold values from -0.25 to 0.25
- w_value: bfloat16 [1152, 1152], P('fsdp', 'seq'), may hold values from -0.1875 to 0.1875
- b_value: bfloat16 [1152], P('seq'), may hold values from -3 to 3
- w_output: bfloat16 [1152, 1152], P('fsdp', 'seq'), may hold values from -1.5 to 1.5
- b_output: bfloat16 [1152], P('seq'), may hold values from -3 to 3
- gain_two: bfloat16 [1152], P('seq'), may hold values from 0.25 to 1.75
- shift_two: bfloat16 [1152], P('seq'), may hold values from -3 to 3
- w_up: bfloat16 [1152, 4304], P('fsdp', 'seq'), may hold values from -0.1875 to 0.1875
- b_up: bfloat16 [4304], P('seq'), may hold values from -3 to 3
- w_down: bfloat16 [4304, 1152], P('fsdp', 'seq'), may hold values from -0.09375 to 0.09375
- b_down: bfloat16 [1152], P('seq'), may hold values from -3 to 3
- cotangent: bfloat16 [8, 2048, 1152], P('fsdp', 'seq'), may hold values from -6 to 6
Outputs:
- layer_out: bfloat16 [8, 2048, 1152], P('fsdp', 'seq')
- grad_tokens: bfloat16 [8, 2048, 1152], P('fsdp', 'seq')
- grad_gain_one: float32 [1152], P('seq')
- grad_shift_one: float32 [1152], P('seq')
- grad_w_query: float32 [1152, 1152], P('fsdp', 'seq')
- grad_b_query: float32 [1152], P('seq')
- grad_w_key: float32 [1152, 1152], P('fsdp', 'seq')
- grad_w_value: float32 [1152, 1152], P('fsdp', 'seq')
- grad_b_value: float32 [1152], P('seq')
- grad_w_output: float32 [1152, 1152], P('fsdp', 'seq')
- grad_b_output: float32 [1152], P('seq')
- grad_gain_two: float32 [1152], P('seq')
- grad_shift_two: float32 [1152], P('seq')
- grad_w_up: float32 [1152, 4304], P('fsdp', 'seq')
- grad_b_up: float32 [4304], P('seq')
- grad_w_down: float32 [4304, 1152], P('fsdp', 'seq')
- grad_b_down: float32 [1152], P('seq')
The draws below stay inside these ranges and needn't reach their ends.
Inputs may be any that keep to these rules, and one draw needn't show every extreme that they name: `patch_mask`: in every image the ones form a prefix of 1984 or more positions and the rest are zeros.
All inputs are finite; a program needn't handle non-finite values.
Results may differ from the reference program's by a relative error of at most 0.018.
Values may be sent and summed in bfloat16 or wider, within the bound.
No kernel may reach another device: no remote copies, remote signals or barrier semaphores. Data moves between devices by JAX's collectives and lax.ppermute only.
A program may use at most 192 MiB of HBM per device.

```python
import jax
import jax.numpy as jnp
from jax import lax

D = 1152
H = 16
FF = 4304
LEN = 2048
HEAD = 72
IMAGES = 8


def draw_patch_mask(key, part):
    key = jax.random.fold_in(key, 7)
    counts = jax.random.randint(key, (IMAGES, 1), LEN - LEN // 32, LEN + 1)
    places = lax.broadcasted_iota(jnp.int32, (IMAGES, LEN), 1)
    return (places < counts).astype(jnp.int32)


def block_scale(key, extent, pieces, smallest, largest):
    def one(axis_at, blocks):
        draws = jax.random.uniform(jax.random.fold_in(jax.random.fold_in(key, 6), axis_at), (blocks,), jnp.float32, smallest / len(pieces), largest / len(pieces))
        return jnp.repeat(jnp.exp(draws), extent[axis_at] // blocks).reshape((-1,) + (1,) * (len(extent) - axis_at - 1))

    level = one(*pieces[0])
    for cut in pieces[1:]:
        level = level * one(*cut)
    return level


def bell_draw(own_key, shape, scale, reach, shards=(), kind=jnp.bfloat16):
    array = scale * jax.random.normal(own_key, shape, jnp.float32)
    if shards:
        array = array * block_scale(own_key, shape, shards, -0.22, 0.18)
    return jnp.clip(array, -reach, reach).astype(kind)


def setup_inputs(seed: int = 0) -> dict:
    splits = jax.random.split(jax.random.key(seed), 19)
    return {
        "tokens": bell_draw(splits[0], (IMAGES, LEN, D), 1.0, 6.0, ((0, 8), (1, 4))),
        "patch_mask": draw_patch_mask(jax.random.fold_in(splits[18], 71), 0),
        "gain_one": jnp.clip(1.0 + 0.15 * jax.random.normal(splits[2], (D,), jnp.float32), 0.25, 1.75).astype(jnp.bfloat16),
        "shift_one": bell_draw(splits[3], (D,), 0.3, 3.0, ((0, 4),)),
        "w_query": bell_draw(splits[4], (D, D), (D // 2) ** -0.5, 0.25, ((0, 8), (1, 4))),
        "b_query": bell_draw(splits[5], (D,), 0.3, 3.0, ((0, 4),)),
        "w_key": bell_draw(splits[6], (D, D), (D // 2) ** -0.5, 0.25, ((0, 8), (1, 4))),
        "w_value": bell_draw(splits[7], (D, D), D ** -0.5, 0.1875, ((0, 8), (1, 4))),
        "b_value": bell_draw(splits[8], (D,), 0.3, 3.0, ((0, 4),)),
        "w_output": bell_draw(splits[9], (D, D), (max(1, D * 32 // LEN)) ** -0.5, 1.5, ((0, 8), (1, 4))),
        "b_output": bell_draw(splits[10], (D,), 0.3, 3.0, ((0, 4),)),
        "gain_two": jnp.clip(1.0 + 0.15 * jax.random.normal(splits[11], (D,), jnp.float32), 0.25, 1.75).astype(jnp.bfloat16),
        "shift_two": bell_draw(splits[12], (D,), 0.3, 3.0, ((0, 4),)),
        "w_up": bell_draw(splits[13], (D, FF), D ** -0.5, 0.1875, ((0, 8), (1, 4))),
        "b_up": bell_draw(splits[14], (FF,), 0.3, 3.0, ((0, 4),)),
        "w_down": bell_draw(splits[15], (FF, D), FF ** -0.5, 0.09375, ((0, 8), (1, 4))),
        "b_down": bell_draw(splits[16], (D,), 0.3, 3.0, ((0, 4),)),
        "cotangent": bell_draw(splits[17], (IMAGES, LEN, D), 1.0, 6.0, ((0, 8), (1, 4))),
    }


EPS = 1e-06
ROOT = 0.7978845608028654
CUBIC = 0.044715
NEG = -1e+30
HIGH = lax.Precision.HIGHEST

@jax.custom_vjp
def low(v):
    return lax.optimization_barrier(v.astype(jnp.bfloat16)).astype(jnp.float32)

@jax.custom_vjp
def low_back(v):
    return v

def low_keep(v):
    return (low(v), None)

def low_pass(kept, grad):
    return (grad,)

def back_keep(v):
    return (v, None)

def back_low(kept, grad):
    return (low(grad),)
low.defvjp(low_keep, low_pass)
low_back.defvjp(back_keep, back_low)

def norm_rows(value, gain, shift):
    mean = lax.optimization_barrier(jnp.mean(value, axis=-1, keepdims=True))
    centered = value - mean
    variance = lax.optimization_barrier(jnp.mean(centered * centered, axis=-1, keepdims=True))
    return centered * lax.rsqrt(variance + EPS) * gain + shift

def gelu_tanh(value):
    inner = jnp.tanh(ROOT * (value + CUBIC * value * value * value))
    return 0.5 * value * (1.0 + inner)

def attend(query, keys, values, key_ok):
    count, length = (query.shape[0], query.shape[1])
    span = min(512, length)
    scale = HEAD ** (-0.5)

    def one_block(query_block):
        scores = low_back(jnp.einsum('gqhd,gkhd->ghqk', query_block, keys, precision=HIGH) * scale)
        scores = jnp.where(key_ok, scores, NEG)
        top = lax.optimization_barrier(jnp.max(scores, axis=-1, keepdims=True))
        weights = jnp.exp(scores - top)
        probs = low(weights / lax.optimization_barrier(jnp.sum(weights, axis=-1, keepdims=True)))
        return jnp.einsum('ghqk,gkhd->gqhd', probs, values, precision=HIGH)
    blocks = jnp.moveaxis(query.reshape(count, length // span, span, H, HEAD), 1, 0)
    mixed = lax.map(jax.checkpoint(one_block), blocks)
    return jnp.moveaxis(mixed, 0, 1).reshape(count, length, H * HEAD)

def layer(tokens, params, key_ok):
    gain_one, shift_one, w_query, b_query, w_key, w_value, b_value, w_output, b_output, gain_two, shift_two, w_up, b_up, w_down, b_down = params
    count, length = (tokens.shape[0], tokens.shape[1])
    h_one = low(norm_rows(tokens, gain_one, shift_one))
    query = low_back(low(jnp.einsum('gsd,de->gse', h_one, w_query, precision=HIGH) + b_query))
    keys = low_back(low(jnp.einsum('gsd,de->gse', h_one, w_key, precision=HIGH)))
    values = low_back(low(jnp.einsum('gsd,de->gse', h_one, w_value, precision=HIGH) + b_value))
    mixed = attend(query.reshape(count, length, H, HEAD), keys.reshape(count, length, H, HEAD), values.reshape(count, length, H, HEAD), key_ok)
    mixed = low_back(low(mixed))
    attn_out = low_back(jnp.einsum('gse,ed->gsd', mixed, w_output, precision=HIGH) + b_output)
    residual = tokens + attn_out
    h_two = low(norm_rows(residual, gain_two, shift_two))
    hidden = low_back(jnp.einsum('gsd,df->gsf', h_two, w_up, precision=HIGH) + b_up)
    activated = low(gelu_tanh(hidden))
    return residual + low_back(jnp.einsum('gsf,fd->gsd', activated, w_down, precision=HIGH) + b_down)

def reference(tokens, patch_mask, gain_one, shift_one, w_query, b_query, w_key, w_value, b_value, w_output, b_output, gain_two, shift_two, w_up, b_up, w_down, b_down, cotangent):
    params = tuple((piece.astype(jnp.float32) for piece in (gain_one, shift_one, w_query, b_query, w_key, w_value, b_value, w_output, b_output, gain_two, shift_two, w_up, b_up, w_down, b_down)))
    groups = tokens.shape[0] // 2
    inputs = tokens.reshape((groups, 2) + tokens.shape[1:])
    masks = patch_mask.reshape(groups, 2, patch_mask.shape[1])
    pulls = cotangent.reshape((groups, 2) + cotangent.shape[1:])

    def step(totals, items):
        group, mask_group, pull_group = items
        key_ok = (mask_group > 0)[:, None, None, :]

        def forward(inside, weights):
            return layer(inside, weights, key_ok)
        result, pull_back = jax.vjp(forward, group.astype(jnp.float32), params)
        grad_input, grad_params = pull_back(pull_group.astype(jnp.float32))
        totals = tuple((left + right for left, right in zip(totals, grad_params)))
        return (totals, (result.astype(jnp.bfloat16), grad_input.astype(jnp.bfloat16)))
    empty = tuple((jnp.zeros(piece.shape, jnp.float32) for piece in params))
    totals, (results, grads) = lax.scan(step, empty, (inputs, masks, pulls))
    return (results.reshape(tokens.shape), grads.reshape(tokens.shape), totals[0], totals[1], totals[2], totals[3], totals[4], totals[5], totals[6], totals[7], totals[8], totals[9], totals[10], totals[11], totals[12], totals[13], totals[14])
```

```python
import functools
import math

import jax
import jax.numpy as jnp
import numpy as np
from jax import lax
from jax.experimental import pallas as pl
from jax.experimental.pallas import tpu as pltpu
from jax.sharding import PartitionSpec as P

HEAD = 72
WIDE = 128
MASK_AT = HEAD
LSE_AT = HEAD + 1
SUM_AT = HEAD
CHUNKS = 2

EPS = 1e-06
ROOT = 0.7978845608028654
CUBIC = 0.044715
NEG = -1e30
LOG2E = math.log2(math.e)
SCALE = HEAD ** (-0.5)

BF = jnp.bfloat16
F32 = jnp.float32
NT = (((1,), (1,)), ((), ()))
NN = (((1,), (0,)), ((), ()))
VMEM_BYTES = 56 << 20


def mm(left, right, dims=NN):
    return lax.dot_general(left, right, dims, preferred_element_type=F32)


def cost(macs, moved, special=0):
    return pl.CostEstimate(flops=2 * macs, bytes_accessed=moved, transcendentals=special)


def swap(value, bit):
    count = lax.axis_size("seq")
    return lax.ppermute(value, "seq", [(i, i ^ bit) for i in range(count)])


def spread(value):
    count = lax.axis_size("seq")
    blocks = [None] * count
    blocks[0] = value
    have = [0]
    bit = count // 2
    while bit:
        for j in list(have):
            blocks[j | bit] = swap(blocks[j], bit)
            have.append(j | bit)
        bit //= 2
    return blocks


def collect(blocks):
    blocks = list(blocks)
    kind = blocks[0].dtype
    count = len(blocks)
    alive = list(range(count))
    bit = 1
    while bit < count:
        for j in reversed(alive):
            if j & bit:
                incoming = swap(blocks[j].astype(kind), bit)
                blocks[j ^ bit] = blocks[j ^ bit].astype(F32) + incoming.astype(F32)
        alive = [j for j in alive if not j & bit]
        bit *= 2
    return blocks[0]


def reorder(blocks, me):
    blocks = list(blocks)
    bit = 1
    while bit < len(blocks):
        odd = (me & bit) > 0
        blocks = [jnp.where(odd, blocks[j ^ bit], blocks[j]) for j in range(len(blocks))]
        bit *= 2
    return blocks


def ring_order():
    count = lax.axis_size("fsdp")
    if count == 8:
        return [0, 2, 4, 6, 7, 5, 3, 1]
    return list(range(count))


def ring_place():
    order = ring_order()
    table = np.zeros(len(order), np.int32)
    for at, device in enumerate(order):
        table[device] = at
    return jnp.asarray(table)[lax.axis_index("fsdp")]


def ring_shift(value, step):
    order = ring_order()
    count = len(order)
    return lax.ppermute(
        value, "fsdp", [(order[i], order[(i + step) % count]) for i in range(count)]
    )


def ring_owner(offset):
    order = ring_order()
    return jnp.asarray(order, jnp.int32)[(ring_place() + offset) % len(order)]


def ring_gather(value, flip):
    count = lax.axis_size("fsdp")
    found = [(0, value)]
    far = (count // 2, count - 1 - count // 2)
    for step, reach in ((1, far[flip]), (-1, far[1 - flip])):
        moving = value
        for k in range(1, reach + 1):
            moving = ring_shift(moving, step)
            found.append((-step * k, moving))
    index = jnp.stack([ring_owner(offset) for offset, _ in found])
    return place([block for _, block in found], index)


def place(blocks, index):
    count = len(blocks)

    def kernel(index_ref, *refs):
        target, sems = refs[count], refs[count + 1]
        copies = [
            pltpu.make_async_copy(refs[i], target.at[index_ref[i]], sems.at[i])
            for i in range(count)
        ]
        for copy in copies:
            copy.start()
        for copy in copies:
            copy.wait()

    block = blocks[0]
    return pl.pallas_call(
        kernel,
        grid_spec=pltpu.PrefetchScalarGridSpec(
            num_scalar_prefetch=1,
            grid=(1,),
            in_specs=[pl.BlockSpec(memory_space=pl.ANY)] * count,
            out_specs=pl.BlockSpec(memory_space=pl.ANY),
            scratch_shapes=[pltpu.SemaphoreType.DMA((count,))],
        ),
        out_shape=jax.ShapeDtypeStruct((count,) + block.shape, block.dtype),
        cost_estimate=cost(0, 2 * count * block.size * 2),
        name="place_blocks",
    )(index, *blocks)


def ring_reduce(take, flip):
    count = lax.axis_size("fsdp")
    far = (count // 2, count - 1 - count // 2)
    total = take(ring_owner(0)).astype(F32)
    for step, reach in ((1, far[flip]), (-1, far[1 - flip])):
        incoming = None
        for k in range(reach, 0, -1):
            part = take(ring_owner(step * k))
            if incoming is not None:
                part = (part.astype(F32) + incoming.astype(F32)).astype(BF)
            incoming = ring_shift(part, step)
        total = total + incoming.astype(F32)
    return total


def ring_sum(value):
    count = lax.axis_size("fsdp")
    bit = 1
    while bit < count:
        value = value + lax.ppermute(value, "fsdp", [(i, i ^ bit) for i in range(count)])
        bit *= 2
    return value


def norm_parts(value):
    mean = jnp.mean(value, axis=-1, keepdims=True)
    centered = value - mean
    inverse = lax.rsqrt(jnp.mean(centered * centered, axis=-1, keepdims=True) + EPS)
    return centered * inverse, inverse


def norm_back(grad_out, normed, inverse, gain):
    scaled = grad_out * gain
    first = jnp.mean(scaled, axis=-1, keepdims=True)
    second = jnp.mean(scaled * normed, axis=-1, keepdims=True)
    return inverse * (scaled - first - normed * second)


def three_parts(value):
    high = value.astype(BF).astype(F32)
    rest = value - high
    middle = rest.astype(BF).astype(F32)
    return high, middle, rest - middle


def put_parts(value, column, at):
    lane = lax.broadcasted_iota(jnp.int32, value.shape, 1)
    for i, part in enumerate(three_parts(column)):
        value = jnp.where(lane == at + i, -part, value)
    return value


def widen(rows, cols, dtype=BF):
    source = lax.broadcasted_iota(jnp.int32, (rows, cols), 0)
    target = lax.broadcasted_iota(jnp.int32, (rows, cols), 1)
    return ((source // HEAD) * WIDE + source % HEAD == target).astype(dtype)


def attend(qkv, wide_heads, chunk, kept):
    images, count, length, _ = qkv.shape
    heads = wide_heads // WIDE
    rows = length // CHUNKS
    keys = count * length
    flat = qkv.reshape(images, keys, 3 * wide_heads)

    def kernel(q_ref, kv_ref, *refs):
        mixed_ref, query_ref, exact_ref = refs[-3:]
        total = jnp.zeros((rows, heads * HEAD), F32)
        for e in range(heads):
            here = slice(e * WIDE, (e + 1) * WIDE)
            query = q_ref[0, 0, :, here]
            k = kv_ref[0, :, wide_heads + e * WIDE : wide_heads + (e + 1) * WIDE]
            v = kv_ref[0, :, 2 * wide_heads + e * WIDE : 2 * wide_heads + (e + 1) * WIDE]
            scores = mm(query, k, NT)
            top = jnp.max(scores, axis=-1, keepdims=True)
            weights = jnp.exp2(scores - top).astype(BF)
            mixed = mm(weights, v)
            summed = mixed[:, SUM_AT : SUM_AT + 1]
            mixed = mixed / summed
            log_total = top + jnp.log2(summed)
            exact_ref[0, 0, :, here] = mixed
            query_ref[0, 0, :, here] = put_parts(query.astype(F32), log_total, LSE_AT).astype(BF)
            source = lax.broadcasted_iota(jnp.int32, (WIDE, heads * HEAD), 0)
            target = lax.broadcasted_iota(jnp.int32, (WIDE, heads * HEAD), 1)
            pick = ((source < HEAD) & (source + e * HEAD == target)).astype(F32).astype(BF)
            total = total + mm(mixed.astype(BF), pick)
        mixed_ref[0, 0] = total.astype(BF)

    part = pl.BlockSpec((1, 1, rows, wide_heads), lambda i, b: (i, b, chunk, 0))
    shapes = [
        jax.ShapeDtypeStruct((images, count, rows, heads * HEAD), BF),
        jax.ShapeDtypeStruct((images, count, length, wide_heads), BF),
        jax.ShapeDtypeStruct((images, count, length, wide_heads), F32),
    ]
    outs = [pl.BlockSpec((1, 1, rows, heads * HEAD), lambda i, b: (i, b, 0, 0)), part, part]
    extra = list(kept)
    scores = images * count * rows * keys * heads
    return pl.pallas_call(
        kernel,
        grid=(images, count),
        in_specs=[part, pl.BlockSpec((1, keys, 3 * wide_heads), lambda i, b: (i, 0, 0))]
        + [pl.BlockSpec(memory_space=pl.ANY)] * len(extra),
        out_specs=outs,
        out_shape=shapes,
        input_output_aliases={2 + i: 1 + i for i in range(len(extra))},
        cost_estimate=cost(2 * scores * WIDE * 2, flat.size * 2 + 3 * images * keys * wide_heads, scores),
        compiler_params=pltpu.CompilerParams(vmem_limit_bytes=VMEM_BYTES),
        name="attend",
    )(qkv, flat, *extra)


def middle(mixed, tokens, cotangent, weights, chunk, kept):
    images, count, length, width = tokens.shape
    me, w_output, w_up, w_down, b_output, gain, shift, b_up = weights
    rows = length // CHUNKS
    own = mixed[0].shape[-1]
    hidden_count = w_up.shape[1]

    def kernel(me_ref, *refs):
        mixed_refs = refs[:count]
        tok_ref, cot_ref, wo_ref, up_ref, down_ref, bo_ref, g_ref, s_ref, bu_ref = refs[
            count : count + 9
        ]
        (
            h_ref,
            z_ref,
            du_ref,
            cat_ref,
            dh_ref,
            y_ref,
            x_ref,
            gb_ref,
        ) = refs[-8:]
        block = pl.program_id(1)
        x_one = tok_ref[0, 0].astype(F32) + bo_ref[...]
        pieces = []
        for i in range(count):
            piece = mixed_refs[i][0, 0]
            pieces.append(piece)
            x_one = x_one + mm(piece, wo_ref[me_ref[0] ^ i])
        cat_ref[0, 0] = jnp.concatenate(pieces, axis=-1)

        @pl.when(block == 0)
        def _():
            x_ref[0] = x_one

        normed, _ = norm_parts(x_one)
        h_two = (normed * g_ref[...] + s_ref[...]).astype(BF)
        h_ref[0, 0] = h_two
        hidden = mm(h_two, up_ref[...]) + bu_ref[...]
        grad_act = mm(cot_ref[0, 0], down_ref[...], NT)
        square = hidden * hidden
        inner = jnp.tanh(ROOT * (hidden + CUBIC * square * hidden))
        half = 0.5 * (1.0 + inner)
        z = (hidden * half).astype(BF)
        slope = half + 0.5 * hidden * (1.0 - inner * inner) * ROOT * (1.0 + 3.0 * CUBIC * square)
        wide_grad = grad_act * slope
        grad_hidden = wide_grad.astype(BF)
        z_ref[0, 0] = z
        du_ref[0, 0] = grad_hidden
        dh_ref[0, 0] = mm(grad_hidden, up_ref[...], NT).astype(BF)
        y_ref[0, 0] = mm(z, down_ref[...]).astype(BF)
        summed = jnp.sum(grad_hidden.astype(F32), axis=0, keepdims=True)
        first = (pl.program_id(0) == 0) & (block == 0)

        @pl.when(first)
        def _():
            gb_ref[...] = summed

        @pl.when(jnp.logical_not(first))
        def _():
            gb_ref[...] += summed

    def piece_spec(i):
        return pl.BlockSpec((1, 1, rows, own), lambda im, b, me_ref: (im, b ^ i, 0, 0))

    def whole_spec(array):
        return pl.BlockSpec(array.shape, lambda im, b, me_ref: (0,) * array.ndim)

    full = pl.BlockSpec((1, 1, rows, width), lambda im, b, me_ref: (im, b, chunk, 0))
    full_hidden = pl.BlockSpec((1, 1, rows, hidden_count), lambda im, b, me_ref: (im, b, chunk, 0))
    part = pl.BlockSpec((1, 1, rows, width), lambda im, b, me_ref: (im, b, 0, 0))
    constants = [w_output, w_up, w_down, b_output, gain, shift, b_up]
    extra = list(kept)
    inputs = [*mixed, tokens, cotangent, *constants, *extra]
    all_rows = images * count * rows
    return pl.pallas_call(
        kernel,
        grid_spec=pltpu.PrefetchScalarGridSpec(
            num_scalar_prefetch=1,
            grid=(images, count),
            in_specs=[piece_spec(i) for i in range(count)]
            + [full, full]
            + [whole_spec(array) for array in constants]
            + [pl.BlockSpec(memory_space=pl.ANY)] * len(extra),
            out_specs=[
                full,
                full_hidden,
                full_hidden,
                full,
                part,
                part,
                pl.BlockSpec((1, rows, width), lambda im, b, me_ref: (im, 0, 0)),
                pl.BlockSpec((1, hidden_count), lambda im, b, me_ref: (0, 0)),
            ],
        ),
        out_shape=[
            jax.ShapeDtypeStruct(tokens.shape, BF),
            jax.ShapeDtypeStruct((images, count, length, hidden_count), BF),
            jax.ShapeDtypeStruct((images, count, length, hidden_count), BF),
            jax.ShapeDtypeStruct(tokens.shape, BF),
            jax.ShapeDtypeStruct((images, count, rows, width), BF),
            jax.ShapeDtypeStruct((images, count, rows, width), BF),
            jax.ShapeDtypeStruct((images, rows, width), F32),
            jax.ShapeDtypeStruct((1, hidden_count), F32),
        ],
        input_output_aliases={1 + count + 9 + i: i for i in range(len(extra))},
        cost_estimate=cost(
            all_rows * width * (width + 4 * hidden_count) * 2,
            all_rows * (width * 16 + hidden_count * 4) + (w_output.size + 2 * w_up.size) * 2,
        ),
        compiler_params=pltpu.CompilerParams(vmem_limit_bytes=VMEM_BYTES),
        name="middle",
    )(me.reshape(1), *inputs)


def mixed_back(grad, w_wide, exact, chunk, kept):
    images, count, rows, width = grad.shape
    _, _, length, wide_heads = exact.shape
    heads = wide_heads // WIDE

    def kernel(grad_ref, w_ref, exact_ref, *refs):
        out_ref = refs[-1]
        result = mm(grad_ref[0, 0], w_ref[...], NT).astype(BF).astype(F32)
        for e in range(heads):
            here = slice(e * WIDE, (e + 1) * WIDE)
            mine = result[:, here]
            delta = jnp.sum(mine * exact_ref[0, 0, :, here], axis=-1, keepdims=True)
            out_ref[0, 0, :, here] = put_parts(mine, delta, SUM_AT).astype(BF)

    full = pl.BlockSpec((1, 1, rows, wide_heads), lambda im, b: (im, b, chunk, 0))
    extra = list(kept)
    return pl.pallas_call(
        kernel,
        grid=(images, count),
        in_specs=[
            pl.BlockSpec((1, 1, rows, width), lambda im, b: (im, b, 0, 0)),
            pl.BlockSpec(w_wide.shape, lambda im, b: (0, 0)),
            full,
        ]
        + [pl.BlockSpec(memory_space=pl.ANY)] * len(extra),
        out_specs=full,
        out_shape=jax.ShapeDtypeStruct(exact.shape, BF),
        input_output_aliases={3 + i: i for i in range(len(extra))},
        cost_estimate=cost(
            images * count * rows * width * wide_heads,
            images * count * rows * (width * 2 + wide_heads * 6) + w_wide.size * 2,
        ),
        compiler_params=pltpu.CompilerParams(vmem_limit_bytes=VMEM_BYTES),
        name="mixed_back",
    )(grad, w_wide, exact, *extra)


def attend_back(query, grad, qkv):
    images, keys, wide_heads = query.shape
    heads = wide_heads // WIDE
    rows = min(512, keys)
    span = min(512, keys)
    steps = keys // rows

    def kernel(q_ref, do_ref, k_ref, v_ref, dq_ref, dk_ref, dv_ref, kt, dk, dv):
        step = pl.program_id(2)

        @pl.when(step == 0)
        def _():
            kt[...] = k_ref[0].T
            dk[...] = jnp.zeros_like(dk)
            dv[...] = jnp.zeros_like(dv)

        q = q_ref[0]
        do = do_ref[0]
        turned = jnp.zeros((WIDE, rows), F32)
        for at in range(0, keys, span):
            here = slice(at, at + span)
            probs = jnp.exp2(mm(k_ref[0, here], q, NT))
            grad_scores = (probs * mm(v_ref[0, here], do, NT)).astype(BF)
            dv[here] += mm(probs.astype(BF), do)
            dk[here] += mm(grad_scores, q)
            turned = turned + mm(kt[:, here], grad_scores)
        dq_ref[0] = (turned.T * SCALE).astype(BF)

        @pl.when(step == steps - 1)
        def _():
            dk_ref[0] = (dk[...] * (1.0 / LOG2E)).astype(BF)
            dv_ref[0] = dv[...].astype(BF)

    row_spec = pl.BlockSpec((1, rows, WIDE), lambda i, e, b: (i, b, e))

    def all_spec(shift):
        return pl.BlockSpec((1, keys, WIDE), lambda i, e, b: (i, 0, e + shift))

    shape = jax.ShapeDtypeStruct((images, keys, wide_heads), BF)
    scores = images * heads * keys * keys
    return pl.pallas_call(
        kernel,
        grid=(images, heads, steps),
        in_specs=[row_spec, row_spec, all_spec(heads), all_spec(2 * heads)],
        out_specs=[row_spec, all_spec(0), all_spec(0)],
        out_shape=[shape] * 3,
        scratch_shapes=[
            pltpu.VMEM((WIDE, keys), BF),
            pltpu.VMEM((keys, WIDE), F32),
            pltpu.VMEM((keys, WIDE), F32),
        ],
        cost_estimate=cost(5 * scores * WIDE * 2, 7 * images * keys * wide_heads * 2, scores),
        compiler_params=pltpu.CompilerParams(vmem_limit_bytes=VMEM_BYTES),
        name="attend_back",
    )(query, grad, qkv, qkv)


def project_back(grads, w_wide):
    images, count, length, wide_heads = grads[0].shape
    width = w_wide.shape[0]

    def kernel(q_ref, k_ref, v_ref, w_ref, out_ref):
        total = jnp.zeros((length, width), F32)
        for i, ref in enumerate((q_ref, k_ref, v_ref)):
            total = total + mm(ref[0, 0], w_ref[:, i * wide_heads : (i + 1) * wide_heads], NT)
        out_ref[0, 0] = total.astype(BF)

    block = pl.BlockSpec((1, 1, length, wide_heads), lambda im, b: (im, b, 0, 0))
    return pl.pallas_call(
        kernel,
        grid=(images, count),
        in_specs=[block] * 3 + [pl.BlockSpec(w_wide.shape, lambda im, b: (0, 0))],
        out_specs=pl.BlockSpec((1, 1, length, width), lambda im, b: (im, b, 0, 0)),
        out_shape=jax.ShapeDtypeStruct((images, count, length, width), BF),
        cost_estimate=cost(
            images * count * length * width * wide_heads * 3,
            images * count * length * (wide_heads * 6 + width * 2) + w_wide.size * 2,
        ),
        compiler_params=pltpu.CompilerParams(vmem_limit_bytes=VMEM_BYTES),
        name="project_back",
    )(*grads, w_wide)


def local(
    tokens,
    patch_mask,
    gain_one,
    shift_one,
    w_query,
    b_query,
    w_key,
    w_value,
    b_value,
    w_output,
    b_output,
    gain_two,
    shift_two,
    w_up,
    b_up,
    w_down,
    b_down,
    cotangent,
):
    me = lax.axis_index("seq")
    count = lax.axis_size("seq")
    fcount = lax.axis_size("fsdp")
    images, length, width = tokens.shape
    own = w_query.shape[1]
    heads = own // HEAD
    wide_heads = heads * WIDE
    group = fcount // count
    rows = length // CHUNKS

    qkv_shard = jnp.concatenate([w_query, w_key, w_value], axis=1)
    small = jnp.concatenate(
        [patch_mask.astype(BF).reshape(-1)]
        + [gain_one, shift_one, b_output, gain_two, shift_two, b_down]
    )
    small = spread(small)
    qkv_rows = ring_gather(qkv_shard, 0).reshape(width, 3 * own)
    down_rows = ring_gather(w_down, 1)
    upper = ring_gather(jnp.concatenate([w_up, w_output], axis=1), 0)
    upper = upper.reshape(width, -1)
    up_mat = upper[:, : w_up.shape[1]]
    output_cols = upper[:, w_up.shape[1] :]

    patches = images * length
    valid = jnp.stack([block[:patches].reshape(images, length) for block in small], axis=1)
    bias_mask = jnp.where(valid > 0, 0.0, NEG).astype(F32)
    vectors = reorder([block[patches:].reshape(6, own) for block in small], me)
    vectors = jnp.concatenate(vectors, axis=1).astype(F32)
    g_one, s_one, b_out, g_two, s_two, b_dn = [vectors[i : i + 1] for i in range(6)]

    output_mat = jnp.concatenate(reorder(spread(output_cols), me), axis=1)
    output_mat = output_mat.reshape(count, own, width)

    def down_part(j):
        start = (me ^ j) * group
        return lax.dynamic_slice_in_dim(down_rows, start, group, 0)

    down_parts = [down_part(0)] + [swap(down_part(j), j) for j in range(1, count)]
    down_mat = jnp.concatenate(reorder(down_parts, me), axis=2).reshape(-1, width)

    expand = widen(own, wide_heads)
    w_wide = mm(qkv_rows, widen(3 * own, 3 * wide_heads)).astype(BF)
    own_rows = lax.dynamic_index_in_dim(output_mat, me, 0, keepdims=False)
    output_wide = mm(expand.T, own_rows).astype(BF)
    lane = np.arange(3 * wide_heads) % WIDE
    kind = np.arange(3 * wide_heads) // wide_heads
    factor = np.where(kind == 0, SCALE * LOG2E, 1.0).astype(np.float32)
    ones = (kind == 0) & (lane == MASK_AT)
    ones |= (kind == 1) & (lane >= LSE_AT) & (lane < LSE_AT + 3)
    ones |= (kind == 2) & (lane >= SUM_AT) & (lane < SUM_AT + 3)
    at_mask = ((kind == 1) & (lane == MASK_AT)).astype(np.float32)

    def widen_vector(vector):
        shaped = vector.astype(F32).reshape(heads, HEAD)
        return jnp.pad(shaped, ((0, 0), (0, WIDE - HEAD))).reshape(-1)

    def narrow(vector):
        return vector.reshape(heads, WIDE)[:, :HEAD].reshape(-1)

    bias_wide = jnp.concatenate(
        [widen_vector(b_query), jnp.zeros((wide_heads,), F32), widen_vector(b_value)]
    )
    bias_wide = bias_wide * factor + ones.astype(np.float32)
    weights = (me, output_mat, up_mat, down_mat, b_out, g_two, s_two, b_up.astype(F32)[None])

    def run(tokens, bias_mask, cotangent):
        images = tokens.shape[0]
        tok_all = jnp.stack(spread(tokens), axis=1)
        cot_all = jnp.stack(spread(cotangent), axis=1)
        normed, _ = norm_parts(tok_all.astype(F32))
        h_one = (normed * g_one + s_one).astype(BF)
        product = jnp.einsum("ijld,de->ijle", h_one, w_wide, preferred_element_type=F32)
        qkv = (product * factor + bias_wide + bias_mask[..., None] * at_mask).astype(BF)

        kept_attend, kept_middle = (), ()
        mixed_chunks = []
        for c in range(CHUNKS):
            mixed, *kept_attend = attend(qkv, wide_heads, c, kept_attend)
            mixed_chunks.append(spread(mixed))
        query_wide, mixed_exact = kept_attend
        hidden_parts, out_parts, x_parts = [], [], []
        up_bias_grad = 0.0
        for c in range(CHUNKS):
            *kept_middle, dh, y, x_own, gb = middle(
                mixed_chunks[c], tok_all, cot_all, weights, c, kept_middle
            )
            hidden_parts.append(collect([dh[:, j] for j in range(count)]))
            out_parts.append(y)
            x_parts.append(x_own)
            up_bias_grad = up_bias_grad + gb[0]
        h_two, activated, grad_hidden, mixed_all = kept_middle

        kept_back = ()
        grad_attn_all, grad_residual = [], []
        early = 0.0
        for c in range(CHUNKS):
            grad_norm = hidden_parts[c].astype(F32)
            normed_two, inverse_two = norm_parts(x_parts[c])
            cot_own = cotangent[:, c * rows : (c + 1) * rows].astype(F32)
            residual = cot_own + norm_back(grad_norm, normed_two, inverse_two, g_two)
            grad_attn = residual.astype(BF)
            grad_residual.append(residual)
            early = early + jnp.stack(
                [
                    jnp.sum(grad_norm * normed_two, axis=(0, 1)),
                    jnp.sum(grad_norm, axis=(0, 1)),
                    jnp.sum(grad_attn.astype(F32), axis=(0, 1)),
                    jnp.sum(cot_own, axis=(0, 1)),
                ]
            )
            stacked = jnp.stack(spread(grad_attn), axis=1)
            grad_attn_all.append(stacked)
            kept_back = (mixed_back(stacked, output_wide, mixed_exact, c, kept_back),)
        grad_mixed = kept_back[0]

        down_grad = jnp.einsum(
            "ijlf,ijld->fd", activated, cot_all, preferred_element_type=F32
        )
        up_grad = jnp.einsum("ijld,ijlf->df", h_two, grad_hidden, preferred_element_type=F32)
        grad_attn_all = jnp.concatenate(grad_attn_all, axis=2)
        grad_attn_cols = lax.dynamic_slice_in_dim(grad_attn_all, me * own, own, 3)
        output_grad = jnp.einsum(
            "ijle,ijld->ed", mixed_all, grad_attn_cols, preferred_element_type=F32
        )

        wide_shape = (images, count * length, wide_heads)
        grads = attend_back(
            query_wide.reshape(wide_shape),
            grad_mixed.reshape(wide_shape),
            qkv.reshape(images, count * length, 3 * wide_heads),
        )
        grads = [g.reshape(images, count, length, wide_heads) for g in grads]
        grad_h = project_back(grads, w_wide)
        grad_norm_one = collect([grad_h[:, j] for j in range(count)]).astype(F32)
        qkv_grad = [
            jnp.einsum("ijld,ijle->de", h_one, g, preferred_element_type=F32) for g in grads
        ]

        out_sum = collect(
            [jnp.concatenate([y[:, j] for y in out_parts], axis=1) for j in range(count)]
        )
        layer_out = (jnp.concatenate(x_parts, axis=1) + out_sum.astype(F32) + b_dn).astype(BF)
        normed_one, inverse_one = norm_parts(tokens.astype(F32))
        grad_tokens = (
            jnp.concatenate(grad_residual, axis=1)
            + norm_back(grad_norm_one, normed_one, inverse_one, g_one)
        ).astype(BF)
        late = jnp.stack(
            [
                jnp.sum(grad_norm_one * normed_one, axis=(0, 1)),
                jnp.sum(grad_norm_one, axis=(0, 1)),
            ]
        )
        bias_grads = [jnp.sum(grads[i].astype(F32), axis=(0, 1, 2)) for i in (0, 2)]
        sums = (down_grad, up_grad, output_grad, qkv_grad, early, up_bias_grad, late, bias_grads)
        return sums, (layer_out, grad_tokens)

    if images == 1:
        sums, (layer_out, grad_tokens) = run(tokens, bias_mask, cotangent)
    else:
        items = (tokens[:, None], bias_mask[:, None], cotangent[:, None])
        shapes = jax.eval_shape(lambda item: run(*item)[0], jax.tree.map(lambda a: a[0], items))
        empty = jax.tree.map(lambda a: jnp.zeros(a.shape, a.dtype), shapes)

        def step(totals, item):
            sums, results = run(*item)
            return jax.tree.map(jnp.add, totals, sums), results

        sums, (layer_out, grad_tokens) = lax.scan(step, empty, items)
        layer_out, grad_tokens = layer_out[:, 0], grad_tokens[:, 0]
    down_grad, up_grad, output_grad, qkv_grad, early, up_bias_grad, late, bias_grads = sums

    def relative(f):
        return ((f // group) ^ me) * group + f % group

    down_grad = down_grad.astype(BF).reshape(group, -1, width)

    def down_cols(j):
        return lax.dynamic_slice_in_dim(down_grad, (me ^ j) * own, own, 2)

    down_pieces = jnp.concatenate(
        [down_cols(0)] + [swap(down_cols(j), j) for j in range(1, count)], axis=0
    )
    final_down = ring_reduce(
        lambda f: lax.dynamic_index_in_dim(down_pieces, relative(f), 0, keepdims=False), 1
    )
    up_grad = up_grad.astype(BF).reshape(fcount, width // fcount, -1)
    final_up = ring_reduce(lambda f: lax.dynamic_index_in_dim(up_grad, f, 0, keepdims=False), 0)
    output_grad = output_grad.astype(BF).reshape(fcount, width // fcount, -1)
    final_output = ring_reduce(
        lambda f: lax.dynamic_index_in_dim(output_grad, relative(f), 0, keepdims=False), 1
    )
    qkv_grad = [mm(full.astype(BF), expand, NT).astype(BF) for full in qkv_grad]
    qkv_grad = jnp.concatenate(qkv_grad, axis=1).reshape(fcount, width // fcount, -1)
    final_qkv = ring_reduce(lambda f: lax.dynamic_index_in_dim(qkv_grad, f, 0, keepdims=False), 0)

    def to_owner(stack):
        kinds = stack.shape[0]
        parts = jnp.split(stack.reshape(kinds, count, own), count, axis=1)
        return collect(reorder([part[:, 0] for part in parts], me))

    early = to_owner(early)
    early = ring_sum(jnp.concatenate([early.reshape(-1), up_bias_grad]))
    late = to_owner(late)
    late = ring_sum(jnp.concatenate([late.reshape(-1)] + [narrow(g) for g in bias_grads]))
    gain_two_grad, shift_two_grad, b_output_grad, b_down_grad = [
        early[i * own : (i + 1) * own] for i in range(4)
    ]
    b_up_grad = early[4 * own :]
    gain_one_grad, shift_one_grad, b_query_grad, b_value_grad = [
        late[i * own : (i + 1) * own] for i in range(4)
    ]
    final_query, final_key, final_value = [
        final_qkv[:, i * own : (i + 1) * own] for i in range(3)
    ]
    return (
        layer_out,
        grad_tokens,
        gain_one_grad,
        shift_one_grad,
        final_query,
        b_query_grad,
        final_key,
        final_value,
        b_value_grad,
        final_output,
        b_output_grad,
        gain_two_grad,
        shift_two_grad,
        final_up,
        b_up_grad,
        final_down,
        b_down_grad,
    )


def solution(mesh):
    rows = P("fsdp", "seq", None)
    matrix = P("fsdp", "seq")
    vector = P("seq")
    return jax.shard_map(
        local,
        mesh=mesh,
        in_specs=(
            rows,
            matrix,
            vector,
            vector,
            matrix,
            vector,
            matrix,
            matrix,
            vector,
            matrix,
            vector,
            vector,
            vector,
            matrix,
            vector,
            matrix,
            vector,
            rows,
        ),
        out_specs=(
            rows,
            rows,
            vector,
            vector,
            matrix,
            vector,
            matrix,
            matrix,
            vector,
            matrix,
            vector,
            vector,
            vector,
            matrix,
            vector,
            matrix,
            vector,
        ),
        check_vma=False,
    )
```

```python
import functools
import math

import jax
import jax.numpy as jnp
import numpy as np
from jax import lax
from jax.experimental import pallas as pl
from jax.experimental.pallas import tpu as pltpu
from jax.sharding import PartitionSpec as P

HEAD = 72
WIDE = 128
MASK_AT = HEAD
LSE_AT = HEAD + 1
SUM_AT = HEAD
CHUNKS = 2

EPS = 1e-06
ROOT = 0.7978845608028654
CUBIC = 0.044715
NEG = -1e30
LOG2E = math.log2(math.e)
SCALE = HEAD ** (-0.5)

BF = jnp.bfloat16
F32 = jnp.float32
NT = (((1,), (1,)), ((), ()))
NN = (((1,), (0,)), ((), ()))
VMEM_BYTES = 56 << 20


def mm(left, right, dims=NN):
    return lax.dot_general(left, right, dims, preferred_element_type=F32)


def cost(macs, moved, special=0):
    return pl.CostEstimate(flops=2 * macs, bytes_accessed=moved, transcendentals=special)


def swap(value, bit):
    count = lax.axis_size("seq")
    return lax.ppermute(value, "seq", [(i, i ^ bit) for i in range(count)])


def spread(value):
    count = lax.axis_size("seq")
    blocks = [None] * count
    blocks[0] = value
    have = [0]
    bit = count // 2
    while bit:
        for j in list(have):
            blocks[j | bit] = swap(blocks[j], bit)
            have.append(j | bit)
        bit //= 2
    return blocks


def collect(blocks):
    blocks = list(blocks)
    kind = blocks[0].dtype
    count = len(blocks)
    alive = list(range(count))
    bit = 1
    while bit < count:
        for j in reversed(alive):
            if j & bit:
                incoming = swap(blocks[j].astype(kind), bit)
                blocks[j ^ bit] = blocks[j ^ bit].astype(F32) + incoming.astype(F32)
        alive = [j for j in alive if not j & bit]
        bit *= 2
    return blocks[0]


def reorder(blocks, me):
    blocks = list(blocks)
    bit = 1
    while bit < len(blocks):
        odd = (me & bit) > 0
        blocks = [jnp.where(odd, blocks[j ^ bit], blocks[j]) for j in range(len(blocks))]
        bit *= 2
    return blocks


def ring_order():
    count = lax.axis_size("fsdp")
    if count == 8:
        return [0, 2, 4, 6, 7, 5, 3, 1]
    return list(range(count))


def ring_place():
    device = lax.axis_index("fsdp")
    if lax.axis_size("fsdp") == 8:
        return jnp.where(device % 2 == 0, device // 2, (15 - device) // 2)
    return device


def ring_shift(value, step):
    order = ring_order()
    count = len(order)
    return lax.ppermute(
        value, "fsdp", [(order[i], order[(i + step) % count]) for i in range(count)]
    )


def ring_owner(offset):
    count = lax.axis_size("fsdp")
    at = lax.rem(ring_place() + (offset + count), count)
    if count == 8:
        return jnp.where(at < 4, 2 * at, 15 - 2 * at)
    return at


def ring_gather(value, flip):
    count = lax.axis_size("fsdp")
    found = [(0, value)]
    far = (count // 2, count - 1 - count // 2)
    moving = [value, value]
    for k in range(1, count // 2 + 1):
        for way, step in ((0, 1), (1, -1)):
            if k <= far[way ^ flip]:
                moving[way] = ring_shift(moving[way], step)
                found.append((-step * k, moving[way]))
    index = jnp.stack([ring_owner(offset) for offset, _ in found])
    return [block for _, block in found], index


def place(blocks, index, cuts, wide=None):
    count = len(blocks)
    pieces = len(cuts) - 1
    extra = [] if wide is None else [wide]

    def kernel(index_ref, *refs):
        outs = refs[count + len(extra) :]
        for i in range(count):
            for p in range(pieces):
                value = refs[i][cuts[p] : cuts[p + 1]]
                if extra:
                    value = mm(value, refs[count][...]).astype(BF)
                outs[p][index_ref[i]] = value

    block = blocks[0]
    cols = block.shape[1] if wide is None else wide.shape[1]
    shapes = [(count, cuts[p + 1] - cuts[p], cols) for p in range(pieces)]
    return pl.pallas_call(
        kernel,
        grid_spec=pltpu.PrefetchScalarGridSpec(
            num_scalar_prefetch=1,
            grid=(1,),
            in_specs=[pl.BlockSpec(a.shape, lambda i, index: (0, 0)) for a in blocks + extra],
            out_specs=[pl.BlockSpec(shape, lambda i, index: (0, 0, 0)) for shape in shapes],
        ),
        out_shape=[jax.ShapeDtypeStruct(shape, BF) for shape in shapes],
        cost_estimate=cost(0 if wide is None else count * block.size * cols, 4 * count * block.size),
        compiler_params=pltpu.CompilerParams(vmem_limit_bytes=VMEM_BYTES),
        name="place_blocks",
    )(index, *blocks, *extra)


def ring_reduce(take, flip):
    count = lax.axis_size("fsdp")
    far = (count // 2, count - 1 - count // 2)
    total = take(ring_owner(0)).astype(F32)
    for step, reach in ((1, far[flip]), (-1, far[1 - flip])):
        incoming = None
        for k in range(reach, 0, -1):
            part = take(ring_owner(step * k))
            if incoming is not None:
                part = (part.astype(F32) + incoming.astype(F32)).astype(BF)
            incoming = ring_shift(part, step)
        total = total + incoming.astype(F32)
    return total


def ring_sum(value):
    count = lax.axis_size("fsdp")
    bit = 1
    while bit < count:
        value = value + lax.ppermute(value, "fsdp", [(i, i ^ bit) for i in range(count)])
        bit *= 2
    return value


def norm_parts(value):
    mean = jnp.mean(value, axis=-1, keepdims=True)
    centered = value - mean
    inverse = lax.rsqrt(jnp.mean(centered * centered, axis=-1, keepdims=True) + EPS)
    return centered * inverse, inverse


def norm_back(grad_out, normed, inverse, gain):
    scaled = grad_out * gain
    first = jnp.mean(scaled, axis=-1, keepdims=True)
    second = jnp.mean(scaled * normed, axis=-1, keepdims=True)
    return inverse * (scaled - first - normed * second)


def three_parts(value):
    high = value.astype(BF).astype(F32)
    rest = value - high
    middle = rest.astype(BF).astype(F32)
    return high, middle, rest - middle


def put_parts(value, column, at):
    lane = lax.broadcasted_iota(jnp.int32, value.shape, 1)
    for i, part in enumerate(three_parts(column)):
        value = jnp.where(lane == at + i, -part, value)
    return value


def widen(rows, cols, dtype=BF):
    source = lax.broadcasted_iota(jnp.int32, (rows, cols), 0)
    target = lax.broadcasted_iota(jnp.int32, (rows, cols), 1)
    return ((source // HEAD) * WIDE + source % HEAD == target).astype(dtype)


def attend(qkv, wide_heads, chunk, kept):
    images, count, length, _ = qkv.shape
    heads = wide_heads // WIDE
    rows = length // CHUNKS
    keys = count * length
    flat = qkv.reshape(images, keys, 3 * wide_heads)

    def kernel(q_ref, kv_ref, *refs):
        mixed_ref, query_ref, exact_ref, turned = refs[-4:]

        @pl.when(pl.program_id(1) == 0)
        def _():
            for e in range(heads):
                at = wide_heads + e * WIDE
                turned[e] = kv_ref[0, :, at : at + WIDE].T

        total = jnp.zeros((rows, heads * HEAD), F32)
        for e in range(heads):
            here = slice(e * WIDE, (e + 1) * WIDE)
            query = q_ref[0, 0, :, here]
            v = kv_ref[0, :, 2 * wide_heads + e * WIDE : 2 * wide_heads + (e + 1) * WIDE]
            scores = mm(query, turned[e])
            top = jnp.max(scores, axis=-1, keepdims=True)
            weights = jnp.exp2(scores - top).astype(BF)
            mixed = mm(weights, v)
            summed = mixed[:, SUM_AT : SUM_AT + 1]
            mixed = mixed / summed
            log_total = top + jnp.log2(summed)
            exact_ref[0, 0, :, here] = mixed
            query_ref[0, 0, :, here] = put_parts(query.astype(F32), log_total, LSE_AT).astype(BF)
            source = lax.broadcasted_iota(jnp.int32, (WIDE, heads * HEAD), 0)
            target = lax.broadcasted_iota(jnp.int32, (WIDE, heads * HEAD), 1)
            pick = ((source < HEAD) & (source + e * HEAD == target)).astype(F32).astype(BF)
            total = total + mm(mixed.astype(BF), pick)
        mixed_ref[0, 0] = total.astype(BF)

    part = pl.BlockSpec((1, 1, rows, wide_heads), lambda i, b: (i, b, chunk, 0))
    shapes = [
        jax.ShapeDtypeStruct((images, count, rows, heads * HEAD), BF),
        jax.ShapeDtypeStruct((images, count, length, wide_heads), BF),
        jax.ShapeDtypeStruct((images, count, length, wide_heads), F32),
    ]
    outs = [pl.BlockSpec((1, 1, rows, heads * HEAD), lambda i, b: (i, b, 0, 0)), part, part]
    extra = list(kept)
    scores = images * count * rows * keys * heads
    return pl.pallas_call(
        kernel,
        grid=(images, count),
        in_specs=[part, pl.BlockSpec((1, keys, 3 * wide_heads), lambda i, b: (i, 0, 0))]
        + [pl.BlockSpec(memory_space=pl.ANY)] * len(extra),
        out_specs=outs,
        out_shape=shapes,
        input_output_aliases={2 + i: 1 + i for i in range(len(extra))},
        scratch_shapes=[pltpu.VMEM((heads, WIDE, keys), BF)],
        cost_estimate=cost(2 * scores * WIDE * 2, flat.size * 2 + 3 * images * keys * wide_heads, scores),
        compiler_params=pltpu.CompilerParams(vmem_limit_bytes=VMEM_BYTES),
        name="attend",
    )(qkv, flat, *extra)


def middle(mixed, tokens, cotangent, weights, chunk, kept):
    images, count, length, width = tokens.shape
    me, w_output, w_up, up_turned, w_down, down_turned, b_output, gain, shift, b_up = weights
    rows = length // CHUNKS
    own = mixed[0].shape[-1]
    both = 2 * rows
    hidden_count = w_up.shape[1]

    def kernel(me_ref, *refs):
        mixed_refs = refs[:count]
        (
            tok_ref,
            cot_ref,
            wo_ref,
            up_ref,
            up_turned_ref,
            down_ref,
            down_turned_ref,
            bo_ref,
            g_ref,
            s_ref,
            bu_ref,
        ) = refs[count : count + 11]
        (
            h_ref,
            z_ref,
            du_ref,
            cat_ref,
            dh_ref,
            y_ref,
            x_ref,
            gb_ref,
        ) = refs[-8:]
        block = pl.program_id(1)
        x_one = tok_ref[0].reshape(both, width).astype(F32) + bo_ref[...]
        pieces = []
        for i in range(count):
            order = (1, 0) if i & 1 else (0, 1)
            piece = jnp.concatenate([mixed_refs[i][0, at] for at in order], axis=0)
            pieces.append(piece)
            x_one = x_one + mm(piece, wo_ref[me_ref[0] ^ i])
        cat_ref[0] = jnp.concatenate(pieces, axis=-1).reshape(2, rows, width)

        @pl.when(block == 0)
        def _():
            x_ref[0] = x_one[:rows]

        normed, _ = norm_parts(x_one)
        h_two = (normed * g_ref[...] + s_ref[...]).astype(BF)
        h_ref[0] = h_two.reshape(2, rows, width)
        hidden = mm(h_two, up_ref[...]) + bu_ref[...]
        grad_act = mm(cot_ref[0].reshape(both, width), down_turned_ref[...])
        square = hidden * hidden
        inner = jnp.tanh(ROOT * (hidden + CUBIC * square * hidden))
        half = 0.5 * (1.0 + inner)
        z = (hidden * half).astype(BF)
        slope = half + 0.5 * hidden * (1.0 - inner * inner) * ROOT * (1.0 + 3.0 * CUBIC * square)
        wide_grad = grad_act * slope
        grad_hidden = wide_grad.astype(BF)
        z_ref[0] = z.reshape(2, rows, hidden_count)
        du_ref[0] = grad_hidden.reshape(2, rows, hidden_count)
        dh_ref[0] = mm(grad_hidden, up_turned_ref[...]).astype(BF).reshape(2, rows, width)
        y_ref[0] = mm(z, down_ref[...]).astype(BF).reshape(2, rows, width)
        summed = jnp.sum(grad_hidden.astype(F32), axis=0, keepdims=True)
        first = (pl.program_id(0) == 0) & (block == 0)

        @pl.when(first)
        def _():
            gb_ref[...] = summed

        @pl.when(jnp.logical_not(first))
        def _():
            gb_ref[...] += summed

    def piece_spec(i):
        return pl.BlockSpec((1, 2, rows, own), lambda im, b, me_ref: (im, b ^ (i >> 1), 0, 0))

    def whole_spec(array):
        return pl.BlockSpec(array.shape, lambda im, b, me_ref: (0,) * array.ndim)

    full = pl.BlockSpec((1, 2, rows, width), lambda im, b, me_ref: (im, b, chunk, 0))
    full_hidden = pl.BlockSpec((1, 2, rows, hidden_count), lambda im, b, me_ref: (im, b, chunk, 0))
    part = pl.BlockSpec((1, 2, rows, width), lambda im, b, me_ref: (im, b, 0, 0))
    constants = [w_output, w_up, up_turned, w_down, down_turned, b_output, gain, shift, b_up]
    extra = list(kept)
    inputs = [*mixed, tokens, cotangent, *constants, *extra]
    all_rows = images * count * rows
    return pl.pallas_call(
        kernel,
        grid_spec=pltpu.PrefetchScalarGridSpec(
            num_scalar_prefetch=1,
            grid=(images, count // 2),
            in_specs=[piece_spec(i) for i in range(count)]
            + [full, full]
            + [whole_spec(array) for array in constants]
            + [pl.BlockSpec(memory_space=pl.ANY)] * len(extra),
            out_specs=[
                full,
                full_hidden,
                full_hidden,
                full,
                part,
                part,
                pl.BlockSpec((1, rows, width), lambda im, b, me_ref: (im, 0, 0)),
                pl.BlockSpec((1, hidden_count), lambda im, b, me_ref: (0, 0)),
            ],
        ),
        out_shape=[
            jax.ShapeDtypeStruct(tokens.shape, BF),
            jax.ShapeDtypeStruct((images, count, length, hidden_count), BF),
            jax.ShapeDtypeStruct((images, count, length, hidden_count), BF),
            jax.ShapeDtypeStruct(tokens.shape, BF),
            jax.ShapeDtypeStruct((images, count, rows, width), BF),
            jax.ShapeDtypeStruct((images, count, rows, width), BF),
            jax.ShapeDtypeStruct((images, rows, width), F32),
            jax.ShapeDtypeStruct((1, hidden_count), F32),
        ],
        input_output_aliases={1 + count + 11 + i: i for i in range(len(extra))},
        cost_estimate=cost(
            all_rows * width * (width + 4 * hidden_count) * 2,
            all_rows * (width * 16 + hidden_count * 4) + (w_output.size + 2 * w_up.size) * 2,
        ),
        compiler_params=pltpu.CompilerParams(vmem_limit_bytes=VMEM_BYTES),
        name="middle",
    )(me.reshape(1), *inputs)


def mixed_back(grad, w_wide, exact, chunk, kept):
    images, count, rows, width = grad.shape
    _, _, length, wide_heads = exact.shape
    heads = wide_heads // WIDE

    def kernel(grad_ref, w_ref, exact_ref, *refs):
        out_ref = refs[-1]
        result = mm(grad_ref[0, 0], w_ref[...]).astype(BF).astype(F32)
        for e in range(heads):
            here = slice(e * WIDE, (e + 1) * WIDE)
            mine = result[:, here]
            delta = jnp.sum(mine * exact_ref[0, 0, :, here], axis=-1, keepdims=True)
            out_ref[0, 0, :, here] = put_parts(mine, delta, SUM_AT).astype(BF)

    full = pl.BlockSpec((1, 1, rows, wide_heads), lambda im, b: (im, b, chunk, 0))
    extra = list(kept)
    return pl.pallas_call(
        kernel,
        grid=(images, count),
        in_specs=[
            pl.BlockSpec((1, 1, rows, width), lambda im, b: (im, b, 0, 0)),
            pl.BlockSpec(w_wide.shape, lambda im, b: (0, 0)),
            full,
        ]
        + [pl.BlockSpec(memory_space=pl.ANY)] * len(extra),
        out_specs=full,
        out_shape=jax.ShapeDtypeStruct(exact.shape, BF),
        input_output_aliases={3 + i: i for i in range(len(extra))},
        cost_estimate=cost(
            images * count * rows * width * wide_heads,
            images * count * rows * (width * 2 + wide_heads * 6) + w_wide.size * 2,
        ),
        compiler_params=pltpu.CompilerParams(vmem_limit_bytes=VMEM_BYTES),
        name="mixed_back",
    )(grad, w_wide, exact, *extra)


def attend_back(query, grad, qkv):
    images, keys, wide_heads = query.shape
    heads = wide_heads // WIDE
    rows = min(512, keys)
    span = min(512, keys)
    steps = keys // rows

    def kernel(q_ref, do_ref, k_ref, v_ref, dq_ref, dk_ref, dv_ref, kt, dk, dv):
        step = pl.program_id(2)

        @pl.when(step == 0)
        def _():
            kt[...] = k_ref[0].T
            dk[...] = jnp.zeros_like(dk)
            dv[...] = jnp.zeros_like(dv)

        q = q_ref[0]
        do = do_ref[0]
        turned = jnp.zeros((WIDE, rows), F32)
        for at in range(0, keys, span):
            here = slice(at, at + span)
            probs = jnp.exp2(mm(k_ref[0, here], q, NT))
            grad_scores = (probs * mm(v_ref[0, here], do, NT)).astype(BF)
            dv[here] += mm(probs.astype(BF), do)
            dk[here] += mm(grad_scores, q)
            turned = turned + mm(kt[:, here], grad_scores)
        dq_ref[0] = (turned.T * SCALE).astype(BF)

        @pl.when(step == steps - 1)
        def _():
            dk_ref[0] = (dk[...] * (1.0 / LOG2E)).astype(BF)
            dv_ref[0] = dv[...].astype(BF)

    row_spec = pl.BlockSpec((1, rows, WIDE), lambda i, e, b: (i, b, e))

    def all_spec(shift):
        return pl.BlockSpec((1, keys, WIDE), lambda i, e, b: (i, 0, e + shift))

    shape = jax.ShapeDtypeStruct((images, keys, wide_heads), BF)
    scores = images * heads * keys * keys
    return pl.pallas_call(
        kernel,
        grid=(images, heads, steps),
        in_specs=[row_spec, row_spec, all_spec(heads), all_spec(2 * heads)],
        out_specs=[row_spec, all_spec(0), all_spec(0)],
        out_shape=[shape] * 3,
        scratch_shapes=[
            pltpu.VMEM((WIDE, keys), BF),
            pltpu.VMEM((keys, WIDE), F32),
            pltpu.VMEM((keys, WIDE), F32),
        ],
        cost_estimate=cost(5 * scores * WIDE * 2, 7 * images * keys * wide_heads * 2, scores),
        compiler_params=pltpu.CompilerParams(vmem_limit_bytes=VMEM_BYTES),
        name="attend_back",
    )(query, grad, qkv, qkv)


def project_back(grads, w_wide):
    images, count, length, wide_heads = grads[0].shape
    width = w_wide.shape[1]

    def kernel(q_ref, k_ref, v_ref, w_ref, out_ref):
        total = jnp.zeros((length, width), F32)
        for i, ref in enumerate((q_ref, k_ref, v_ref)):
            total = total + mm(ref[0, 0], w_ref[i * wide_heads : (i + 1) * wide_heads])
        out_ref[0, 0] = total.astype(BF)

    block = pl.BlockSpec((1, 1, length, wide_heads), lambda im, b: (im, b, 0, 0))
    return pl.pallas_call(
        kernel,
        grid=(images, count),
        in_specs=[block] * 3 + [pl.BlockSpec(w_wide.shape, lambda im, b: (0, 0))],
        out_specs=pl.BlockSpec((1, 1, length, width), lambda im, b: (im, b, 0, 0)),
        out_shape=jax.ShapeDtypeStruct((images, count, length, width), BF),
        cost_estimate=cost(
            images * count * length * width * wide_heads * 3,
            images * count * length * (wide_heads * 6 + width * 2) + w_wide.size * 2,
        ),
        compiler_params=pltpu.CompilerParams(vmem_limit_bytes=VMEM_BYTES),
        name="project_back",
    )(*grads, w_wide)


def local(
    tokens,
    patch_mask,
    gain_one,
    shift_one,
    w_query,
    b_query,
    w_key,
    w_value,
    b_value,
    w_output,
    b_output,
    gain_two,
    shift_two,
    w_up,
    b_up,
    w_down,
    b_down,
    cotangent,
):
    me = lax.axis_index("seq")
    count = lax.axis_size("seq")
    fcount = lax.axis_size("fsdp")
    images, length, width = tokens.shape
    own = w_query.shape[1]
    heads = own // HEAD
    wide_heads = heads * WIDE
    group = fcount // count
    rows = length // CHUNKS

    qkv_shard = jnp.concatenate([w_query, w_key, w_value], axis=1)
    small = jnp.concatenate(
        [patch_mask.astype(BF).reshape(-1)]
        + [gain_one, shift_one, b_output, gain_two, shift_two, b_down]
    )
    small = spread(small)
    qkv_blocks, qkv_index = ring_gather(qkv_shard, 0)
    w_wide = place(
        qkv_blocks, qkv_index, (0, qkv_shard.shape[0]), widen(3 * own, 3 * wide_heads)
    )[0].reshape(width, 3 * wide_heads)
    lower_shard = jnp.concatenate([w_output, w_down], axis=0)
    lower_shard, up_shard, _ = lax.optimization_barrier((lower_shard, w_up, qkv_blocks[-1]))
    cut = w_output.shape[0]
    output_cols, down_rows = place(
        *ring_gather(lower_shard, 1), (0, cut, cut + w_down.shape[0])
    )
    output_cols = output_cols.reshape(width, own)
    up_mat = place(*ring_gather(up_shard, 0), (0, cut))[0].reshape(width, -1)

    patches = images * length
    valid = jnp.stack([block[:patches].reshape(images, length) for block in small], axis=1)
    bias_mask = jnp.where(valid > 0, 0.0, NEG).astype(F32)
    vectors = reorder([block[patches:].reshape(6, own) for block in small], me)
    vectors = jnp.concatenate(vectors, axis=1).astype(F32)
    g_one, s_one, b_out, g_two, s_two, b_dn = [vectors[i : i + 1] for i in range(6)]

    output_mat = jnp.concatenate(reorder(spread(output_cols), me), axis=1)
    output_mat = output_mat.reshape(count, own, width)

    def down_part(j):
        start = (me ^ j) * group
        return lax.dynamic_slice_in_dim(down_rows, start, group, 0)

    down_parts = [down_part(0)] + [swap(down_part(j), j) for j in range(1, count)]
    down_mat = jnp.concatenate(reorder(down_parts, me), axis=2).reshape(-1, width)

    expand = widen(own, wide_heads)
    own_rows = lax.dynamic_index_in_dim(output_mat, me, 0, keepdims=False)
    output_wide = mm(own_rows.T, expand).astype(BF)
    lane = np.arange(3 * wide_heads) % WIDE
    kind = np.arange(3 * wide_heads) // wide_heads
    factor = np.where(kind == 0, SCALE * LOG2E, 1.0).astype(np.float32)
    ones = (kind == 0) & (lane == MASK_AT)
    ones |= (kind == 1) & (lane >= LSE_AT) & (lane < LSE_AT + 3)
    ones |= (kind == 2) & (lane >= SUM_AT) & (lane < SUM_AT + 3)
    at_mask = ((kind == 1) & (lane == MASK_AT)).astype(np.float32)

    def widen_vector(vector):
        shaped = vector.astype(F32).reshape(heads, HEAD)
        return jnp.pad(shaped, ((0, 0), (0, WIDE - HEAD))).reshape(-1)

    def narrow(vector):
        return vector.reshape(heads, WIDE)[:, :HEAD].reshape(-1)

    bias_wide = jnp.concatenate(
        [widen_vector(b_query), jnp.zeros((wide_heads,), F32), widen_vector(b_value)]
    )
    bias_wide = bias_wide * factor + ones.astype(np.float32)
    weights = (me, output_mat, up_mat, up_mat.T, down_mat, down_mat.T, b_out, g_two, s_two, b_up.astype(F32)[None])

    def run(tokens, bias_mask, cotangent):
        images = tokens.shape[0]
        tok_all = jnp.stack(spread(tokens), axis=1)
        tok_all, cot_first = lax.optimization_barrier((tok_all, cotangent))
        cot_all = jnp.stack(spread(cot_first), axis=1)
        normed, _ = norm_parts(tok_all.astype(F32))
        h_one = (normed * g_one + s_one).astype(BF)
        product = jnp.einsum("ijld,de->ijle", h_one, w_wide, preferred_element_type=F32)
        qkv = (product * factor + bias_wide + bias_mask[..., None] * at_mask).astype(BF)

        kept_attend, kept_middle = (), ()
        mixed_chunks = []
        for c in range(CHUNKS):
            mixed, *kept_attend = attend(qkv, wide_heads, c, kept_attend)
            mixed_chunks.append(spread(mixed))
        query_wide, mixed_exact = kept_attend
        hidden_parts, out_parts, x_parts = [], [], []
        up_bias_grad = 0.0
        for c in range(CHUNKS):
            *kept_middle, dh, y, x_own, gb = middle(
                mixed_chunks[c], tok_all, cot_all, weights, c, kept_middle
            )
            hidden_parts.append(collect([dh[:, j] for j in range(count)]))
            out_parts.append(y)
            x_parts.append(x_own)
            up_bias_grad = up_bias_grad + gb[0]
        h_two, activated, grad_hidden, mixed_all = kept_middle

        kept_back = ()
        grad_attn_all, grad_residual = [], []
        early = 0.0
        for c in range(CHUNKS):
            grad_norm = hidden_parts[c].astype(F32)
            normed_two, inverse_two = norm_parts(x_parts[c])
            cot_own = cotangent[:, c * rows : (c + 1) * rows].astype(F32)
            residual = cot_own + norm_back(grad_norm, normed_two, inverse_two, g_two)
            grad_attn = residual.astype(BF)
            grad_residual.append(residual)
            early = early + jnp.stack(
                [
                    jnp.sum(grad_norm * normed_two, axis=(0, 1)),
                    jnp.sum(grad_norm, axis=(0, 1)),
                    jnp.sum(grad_attn.astype(F32), axis=(0, 1)),
                    jnp.sum(cot_own, axis=(0, 1)),
                ]
            )
            stacked = jnp.stack(spread(grad_attn), axis=1)
            grad_attn_all.append(stacked)
            kept_back = (mixed_back(stacked, output_wide, mixed_exact, c, kept_back),)
        grad_mixed = kept_back[0]

        down_grad = jnp.einsum(
            "ijlf,ijld->fd", activated, cot_all, preferred_element_type=F32
        )
        up_grad = jnp.einsum("ijld,ijlf->df", h_two, grad_hidden, preferred_element_type=F32)
        grad_attn_all = jnp.concatenate(grad_attn_all, axis=2)
        grad_attn_cols = lax.dynamic_slice_in_dim(grad_attn_all, me * own, own, 3)
        output_grad = jnp.einsum(
            "ijle,ijld->ed", mixed_all, grad_attn_cols, preferred_element_type=F32
        )

        wide_shape = (images, count * length, wide_heads)
        grads = attend_back(
            query_wide.reshape(wide_shape),
            grad_mixed.reshape(wide_shape),
            qkv.reshape(images, count * length, 3 * wide_heads),
        )
        grads = [g.reshape(images, count, length, wide_heads) for g in grads]
        grad_h = project_back(grads, w_wide.T)
        grad_norm_one = collect([grad_h[:, j] for j in range(count)]).astype(F32)
        qkv_grad = [
            jnp.einsum("ijld,ijle->de", h_one, g, preferred_element_type=F32) for g in grads
        ]

        out_parts, grad_mixed = lax.optimization_barrier((out_parts, grad_mixed))
        out_sum = collect(
            [jnp.concatenate([y[:, j] for y in out_parts], axis=1) for j in range(count)]
        )
        layer_out = (jnp.concatenate(x_parts, axis=1) + out_sum.astype(F32) + b_dn).astype(BF)
        normed_one, inverse_one = norm_parts(tokens.astype(F32))
        grad_tokens = (
            jnp.concatenate(grad_residual, axis=1)
            + norm_back(grad_norm_one, normed_one, inverse_one, g_one)
        ).astype(BF)
        late = jnp.stack(
            [
                jnp.sum(grad_norm_one * normed_one, axis=(0, 1)),
                jnp.sum(grad_norm_one, axis=(0, 1)),
            ]
        )
        bias_grads = [jnp.sum(grads[i].astype(F32), axis=(0, 1, 2)) for i in (0, 2)]
        sums = (down_grad, up_grad, output_grad, qkv_grad, early, up_bias_grad, late, bias_grads)
        return sums, (layer_out, grad_tokens)

    if images == 1:
        sums, (layer_out, grad_tokens) = run(tokens, bias_mask, cotangent)
    else:
        items = (tokens[:, None], bias_mask[:, None], cotangent[:, None])
        shapes = jax.eval_shape(lambda item: run(*item)[0], jax.tree.map(lambda a: a[0], items))
        empty = jax.tree.map(lambda a: jnp.zeros(a.shape, a.dtype), shapes)

        def step(totals, item):
            sums, results = run(*item)
            return jax.tree.map(jnp.add, totals, sums), results

        sums, (layer_out, grad_tokens) = lax.scan(step, empty, items)
        layer_out, grad_tokens = layer_out[:, 0], grad_tokens[:, 0]
    down_grad, up_grad, output_grad, qkv_grad, early, up_bias_grad, late, bias_grads = sums

    down_grad = down_grad.astype(BF).reshape(group, -1, width)

    def down_cols(j):
        return lax.dynamic_slice_in_dim(down_grad, (me ^ j) * own, own, 2)

    down_pieces = [down_cols(0)] + [swap(down_cols(j), j) for j in range(1, count)]
    down_pieces = jnp.concatenate(reorder(down_pieces, me), axis=0)
    final_up = lax.psum_scatter(
        up_grad.astype(BF).reshape(fcount, width // fcount, -1), "fsdp", scatter_dimension=0
    ).astype(F32)
    final_down = lax.psum_scatter(down_pieces, "fsdp", scatter_dimension=0).astype(F32)
    output_grad = reorder(jnp.split(output_grad.astype(BF), count, axis=0), me)
    output_grad = jnp.concatenate(output_grad, axis=0)
    qkv_grad = [mm(full.astype(BF), expand, NT).astype(BF) for full in qkv_grad]
    four = jnp.concatenate(qkv_grad + [output_grad], axis=1).reshape(fcount, width // fcount, -1)
    four = ring_reduce(lambda f: lax.dynamic_index_in_dim(four, f, 0, keepdims=False), 0)

    def to_owner(stack):
        kinds = stack.shape[0]
        parts = jnp.split(stack.reshape(kinds, count, own), count, axis=1)
        return collect(reorder([part[:, 0] for part in parts], me))

    early = to_owner(early)
    early = ring_sum(jnp.concatenate([early.reshape(-1), up_bias_grad]))
    late = to_owner(late)
    late = ring_sum(jnp.concatenate([late.reshape(-1)] + [narrow(g) for g in bias_grads]))
    gain_two_grad, shift_two_grad, b_output_grad, b_down_grad = [
        early[i * own : (i + 1) * own] for i in range(4)
    ]
    b_up_grad = early[4 * own :]
    gain_one_grad, shift_one_grad, b_query_grad, b_value_grad = [
        late[i * own : (i + 1) * own] for i in range(4)
    ]
    final_query, final_key, final_value, final_output = [
        four[:, i * own : (i + 1) * own] for i in range(4)
    ]
    return (
        layer_out,
        grad_tokens,
        gain_one_grad,
        shift_one_grad,
        final_query,
        b_query_grad,
        final_key,
        final_value,
        b_value_grad,
        final_output,
        b_output_grad,
        gain_two_grad,
        shift_two_grad,
        final_up,
        b_up_grad,
        final_down,
        b_down_grad,
    )


def solution(mesh):
    rows = P("fsdp", "seq", None)
    matrix = P("fsdp", "seq")
    vector = P("seq")
    return jax.shard_map(
        local,
        mesh=mesh,
        in_specs=(
            rows,
            matrix,
            vector,
            vector,
            matrix,
            vector,
            matrix,
            matrix,
            vector,
            matrix,
            vector,
            vector,
            vector,
            matrix,
            vector,
            matrix,
            vector,
            rows,
        ),
        out_specs=(
            rows,
            rows,
            vector,
            vector,
            matrix,
            vector,
            matrix,
            matrix,
            vector,
            matrix,
            vector,
            vector,
            vector,
            matrix,
            vector,
            matrix,
            vector,
        ),
        check_vma=False,
    )
```

```python
import functools
import math

import jax
import jax.numpy as jnp
import numpy as np
from jax import lax
from jax.experimental import pallas as pl
from jax.experimental.pallas import tpu as pltpu
from jax.sharding import PartitionSpec as P

HEAD = 72
WIDE = 128
MASK_AT = HEAD
LSE_AT = HEAD + 1
SUM_AT = HEAD
CHUNKS = 2

EPS = 1e-06
ROOT = 0.7978845608028654
CUBIC = 0.044715
NEG = -1e30
LOG2E = math.log2(math.e)
SCALE = HEAD ** (-0.5)

BF = jnp.bfloat16
F32 = jnp.float32
NT = (((1,), (1,)), ((), ()))
NN = (((1,), (0,)), ((), ()))
VMEM_BYTES = 56 << 20


def mm(left, right, dims=NN):
    return lax.dot_general(left, right, dims, preferred_element_type=F32)


def cost(macs, moved, special=0):
    return pl.CostEstimate(flops=2 * macs, bytes_accessed=moved, transcendentals=special)


def swap(value, bit):
    count = lax.axis_size("seq")
    return lax.ppermute(value, "seq", [(i, i ^ bit) for i in range(count)])


def spread(value):
    count = lax.axis_size("seq")
    blocks = [None] * count
    blocks[0] = value
    have = [0]
    bit = count // 2
    while bit:
        for j in list(have):
            blocks[j | bit] = swap(blocks[j], bit)
            have.append(j | bit)
        bit //= 2
    return blocks


def collect(blocks):
    blocks = list(blocks)
    kind = blocks[0].dtype
    count = len(blocks)
    alive = list(range(count))
    bit = 1
    while bit < count:
        for j in reversed(alive):
            if j & bit:
                incoming = swap(blocks[j].astype(kind), bit)
                blocks[j ^ bit] = blocks[j ^ bit].astype(F32) + incoming.astype(F32)
        alive = [j for j in alive if not j & bit]
        bit *= 2
    return blocks[0]


def collect_direct(blocks):
    total = blocks[0].astype(F32)
    for j in range(len(blocks) - 1, 0, -1):
        total = total + swap(blocks[j], j).astype(F32)
    return total


def reorder(blocks, me):
    blocks = list(blocks)
    bit = 1
    while bit < len(blocks):
        odd = (me & bit) > 0
        blocks = [jnp.where(odd, blocks[j ^ bit], blocks[j]) for j in range(len(blocks))]
        bit *= 2
    return blocks


def ring_order():
    count = lax.axis_size("fsdp")
    if count == 8:
        return [0, 2, 4, 6, 7, 5, 3, 1]
    return list(range(count))


def ring_place():
    device = lax.axis_index("fsdp")
    if lax.axis_size("fsdp") == 8:
        return jnp.where(device % 2 == 0, device // 2, (15 - device) // 2)
    return device


def ring_shift(value, step):
    order = ring_order()
    count = len(order)
    return lax.ppermute(
        value, "fsdp", [(order[i], order[(i + step) % count]) for i in range(count)]
    )


def ring_owner(offset):
    count = lax.axis_size("fsdp")
    at = lax.rem(ring_place() + (offset + count), count)
    if count == 8:
        return jnp.where(at < 4, 2 * at, 15 - 2 * at)
    return at


def ring_gather(value, flip):
    count = lax.axis_size("fsdp")
    found = [(0, value)]
    far = (count // 2, count - 1 - count // 2)
    moving = [value, value]
    for k in range(1, count // 2 + 1):
        for way, step in ((0, 1), (1, -1)):
            if k <= far[way ^ flip]:
                moving[way] = ring_shift(moving[way], step)
                found.append((-step * k, moving[way]))
        moving = list(lax.optimization_barrier(tuple(moving)))
    index = jnp.stack([ring_owner(offset) for offset, _ in found])
    return [block for _, block in found], index


def place_wide(blocks, index, wide):
    count = len(blocks)
    rows, cols = blocks[0].shape
    merged = rows % 16 == 0

    def kernel(index_ref, *refs):
        wide_ref, out_ref, held = refs[count:]
        for i in range(count):
            held[index_ref[i]] = refs[i][...]
        if merged:
            out_ref[...] = mm(held[...].reshape(count * rows, cols), wide_ref[...]).astype(BF)
        else:
            for i in range(count):
                out_ref[i] = mm(held[i], wide_ref[...]).astype(BF)

    shape = (count * rows, wide.shape[1]) if merged else (count, rows, wide.shape[1])
    out = pl.pallas_call(
        kernel,
        grid_spec=pltpu.PrefetchScalarGridSpec(
            num_scalar_prefetch=1,
            grid=(1,),
            in_specs=[pl.BlockSpec(a.shape, lambda i, index: (0, 0)) for a in [*blocks, wide]],
            out_specs=pl.BlockSpec(shape, lambda i, index: (0,) * len(shape)),
            scratch_shapes=[pltpu.VMEM((count, rows, cols), BF)],
        ),
        out_shape=jax.ShapeDtypeStruct(shape, BF),
        cost_estimate=cost(count * rows * cols * wide.shape[1], 4 * count * rows * cols),
        compiler_params=pltpu.CompilerParams(vmem_limit_bytes=VMEM_BYTES),
        name="place_wide",
    )(index, *blocks, wide)
    return out.reshape(count * rows, wide.shape[1])


def ring_reduce(take, flip):
    count = lax.axis_size("fsdp")
    far = (count // 2, count - 1 - count // 2)
    total = take(ring_owner(0)).astype(F32)
    incoming = [None, None]
    for k in range(count // 2, 0, -1):
        for way, step in ((0, 1), (1, -1)):
            if k <= far[way ^ flip]:
                part = take(ring_owner(step * k))
                if incoming[way] is not None:
                    part = (part.astype(F32) + incoming[way].astype(F32)).astype(BF)
                incoming[way] = ring_shift(part, step)
        if incoming[1] is not None and incoming[0] is not None:
            incoming = list(lax.optimization_barrier(tuple(incoming)))
    return total + incoming[0].astype(F32) + incoming[1].astype(F32)


def ring_sum(value):
    count = lax.axis_size("fsdp")
    bit = 1
    while bit < count:
        value = value + lax.ppermute(value, "fsdp", [(i, i ^ bit) for i in range(count)])
        bit *= 2
    return value


def norm_parts(value):
    mean = jnp.mean(value, axis=-1, keepdims=True)
    centered = value - mean
    inverse = lax.rsqrt(jnp.mean(centered * centered, axis=-1, keepdims=True) + EPS)
    return centered * inverse, inverse


def norm_back(grad_out, normed, inverse, gain):
    scaled = grad_out * gain
    first = jnp.mean(scaled, axis=-1, keepdims=True)
    second = jnp.mean(scaled * normed, axis=-1, keepdims=True)
    return inverse * (scaled - first - normed * second)


def three_parts(value):
    high = value.astype(BF).astype(F32)
    rest = value - high
    middle = rest.astype(BF).astype(F32)
    return high, middle, rest - middle


def put_parts(value, column, at):
    lane = lax.broadcasted_iota(jnp.int32, value.shape, 1)
    for i, part in enumerate(three_parts(column)):
        value = jnp.where(lane == at + i, -part, value)
    return value


def widen(rows, cols, dtype=BF):
    source = lax.broadcasted_iota(jnp.int32, (rows, cols), 0)
    target = lax.broadcasted_iota(jnp.int32, (rows, cols), 1)
    return ((source // HEAD) * WIDE + source % HEAD == target).astype(dtype)


def attend(qkv, wide_heads, chunk, kept):
    images, count, length, _ = qkv.shape
    heads = wide_heads // WIDE
    rows = length // CHUNKS
    keys = count * length
    flat = qkv.reshape(images, keys, 3 * wide_heads)

    def kernel(q_ref, kv_ref, *refs):
        mixed_ref, query_ref, exact_ref, turned = refs[-4:]

        @pl.when(pl.program_id(1) == 0)
        def _():
            for e in range(heads):
                at = wide_heads + e * WIDE
                turned[e] = kv_ref[0, :, at : at + WIDE].T

        total = jnp.zeros((rows, heads * HEAD), F32)
        for e in range(heads):
            here = slice(e * WIDE, (e + 1) * WIDE)
            query = q_ref[0, 0, :, here]
            v = kv_ref[0, :, 2 * wide_heads + e * WIDE : 2 * wide_heads + (e + 1) * WIDE]
            scores = mm(query, turned[e])
            top = jnp.max(scores, axis=-1, keepdims=True)
            weights = jnp.exp2(scores - top).astype(BF)
            mixed = mm(weights, v)
            summed = mixed[:, SUM_AT : SUM_AT + 1]
            mixed = mixed / summed
            log_total = top + jnp.log2(summed)
            exact_ref[0, 0, :, here] = mixed
            query_ref[0, 0, :, here] = put_parts(query.astype(F32), log_total, LSE_AT).astype(BF)
            source = lax.broadcasted_iota(jnp.int32, (WIDE, heads * HEAD), 0)
            target = lax.broadcasted_iota(jnp.int32, (WIDE, heads * HEAD), 1)
            pick = ((source < HEAD) & (source + e * HEAD == target)).astype(F32).astype(BF)
            total = total + mm(mixed.astype(BF), pick)
        mixed_ref[0, 0] = total.astype(BF)

    part = pl.BlockSpec((1, 1, rows, wide_heads), lambda i, b: (i, b, chunk, 0))
    shapes = [
        jax.ShapeDtypeStruct((images, count, rows, heads * HEAD), BF),
        jax.ShapeDtypeStruct((images, count, length, wide_heads), BF),
        jax.ShapeDtypeStruct((images, count, length, wide_heads), F32),
    ]
    outs = [pl.BlockSpec((1, 1, rows, heads * HEAD), lambda i, b: (i, b, 0, 0)), part, part]
    extra = list(kept)
    scores = images * count * rows * keys * heads
    return pl.pallas_call(
        kernel,
        grid=(images, count),
        in_specs=[part, pl.BlockSpec((1, keys, 3 * wide_heads), lambda i, b: (i, 0, 0))]
        + [pl.BlockSpec(memory_space=pl.ANY)] * len(extra),
        out_specs=outs,
        out_shape=shapes,
        input_output_aliases={2 + i: 1 + i for i in range(len(extra))},
        scratch_shapes=[pltpu.VMEM((heads, WIDE, keys), BF)],
        cost_estimate=cost(2 * scores * WIDE * 2, flat.size * 2 + 3 * images * keys * wide_heads, scores),
        compiler_params=pltpu.CompilerParams(vmem_limit_bytes=VMEM_BYTES),
        name="attend",
    )(qkv, flat, *extra)


def middle(mixed, tokens, cotangent, weights, chunk, kept):
    images, count, length, width = tokens.shape
    me, w_output, w_up, up_turned, w_down, down_turned, b_output, gain, shift, b_up = weights
    rows = length // CHUNKS
    own = mixed[0].shape[-1]
    both = 2 * rows
    hidden_count = w_up.shape[1]

    def kernel(me_ref, *refs):
        mixed_refs = refs[:count]
        (
            tok_ref,
            cot_ref,
            wo_ref,
            up_ref,
            up_turned_ref,
            down_ref,
            down_turned_ref,
            bo_ref,
            g_ref,
            s_ref,
            bu_ref,
        ) = refs[count : count + 11]
        outs = refs[-(6 + 2 * count) :]
        h_ref, z_ref, du_ref, cat_ref, x_ref, gb_ref = outs[:6]
        dh_refs, y_refs = outs[6 : 6 + count], outs[6 + count :]
        block = pl.program_id(1)
        x_one = tok_ref[0].reshape(both, width).astype(F32) + bo_ref[...]
        pieces = []
        for i in range(count):
            order = (1, 0) if i & 1 else (0, 1)
            piece = jnp.concatenate([mixed_refs[i][0, at] for at in order], axis=0)
            pieces.append(piece)
            x_one = x_one + mm(piece, wo_ref[me_ref[0] ^ i])
        cat_ref[0] = jnp.concatenate(pieces, axis=-1).reshape(2, rows, width)

        @pl.when(block == 0)
        def _():
            x_ref[0] = x_one[:rows]

        normed, _ = norm_parts(x_one)
        h_two = (normed * g_ref[...] + s_ref[...]).astype(BF)
        h_ref[0] = h_two.reshape(2, rows, width)
        hidden = mm(h_two, up_ref[...]) + bu_ref[...]
        grad_act = mm(cot_ref[0].reshape(both, width), down_turned_ref[...])
        square = hidden * hidden
        inner = jnp.tanh(ROOT * (hidden + CUBIC * square * hidden))
        half = 0.5 * (1.0 + inner)
        z = (hidden * half).astype(BF)
        slope = half + 0.5 * hidden * (1.0 - inner * inner) * ROOT * (1.0 + 3.0 * CUBIC * square)
        wide_grad = grad_act * slope
        grad_hidden = wide_grad.astype(BF)
        z_ref[0] = z.reshape(2, rows, hidden_count)
        du_ref[0] = grad_hidden.reshape(2, rows, hidden_count)
        dh = mm(grad_hidden, up_turned_ref[...]).astype(BF)
        y = mm(z, down_ref[...]).astype(BF)
        for pair in range(count // 2):

            @pl.when(block == pair)
            def _():
                for side in (0, 1):
                    here = slice(side * rows, (side + 1) * rows)
                    dh_refs[2 * pair + side][0] = dh[here]
                    y_refs[2 * pair + side][0] = y[here]

        summed = jnp.sum(grad_hidden.astype(F32), axis=0, keepdims=True)
        first = (pl.program_id(0) == 0) & (block == 0)

        @pl.when(first)
        def _():
            gb_ref[...] = summed

        @pl.when(jnp.logical_not(first))
        def _():
            gb_ref[...] += summed

    def piece_spec(i):
        return pl.BlockSpec((1, 2, rows, own), lambda im, b, me_ref: (im, b ^ (i >> 1), 0, 0))

    def whole_spec(array):
        return pl.BlockSpec(array.shape, lambda im, b, me_ref: (0,) * array.ndim)

    full = pl.BlockSpec((1, 2, rows, width), lambda im, b, me_ref: (im, b, chunk, 0))
    full_hidden = pl.BlockSpec((1, 2, rows, hidden_count), lambda im, b, me_ref: (im, b, chunk, 0))
    part = pl.BlockSpec((1, rows, width), lambda im, b, me_ref: (im, 0, 0))
    constants = [w_output, w_up, up_turned, w_down, down_turned, b_output, gain, shift, b_up]
    extra = list(kept)
    inputs = [*mixed, tokens, cotangent, *constants, *extra]
    all_rows = images * count * rows
    return pl.pallas_call(
        kernel,
        grid_spec=pltpu.PrefetchScalarGridSpec(
            num_scalar_prefetch=1,
            grid=(images, count // 2),
            in_specs=[piece_spec(i) for i in range(count)]
            + [full, full]
            + [whole_spec(array) for array in constants]
            + [pl.BlockSpec(memory_space=pl.ANY)] * len(extra),
            out_specs=[
                full,
                full_hidden,
                full_hidden,
                full,
                part,
                pl.BlockSpec((1, hidden_count), lambda im, b, me_ref: (0, 0)),
            ]
            + [part] * (2 * count),
        ),
        out_shape=[
            jax.ShapeDtypeStruct(tokens.shape, BF),
            jax.ShapeDtypeStruct((images, count, length, hidden_count), BF),
            jax.ShapeDtypeStruct((images, count, length, hidden_count), BF),
            jax.ShapeDtypeStruct(tokens.shape, BF),
            jax.ShapeDtypeStruct((images, rows, width), F32),
            jax.ShapeDtypeStruct((1, hidden_count), F32),
        ]
        + [jax.ShapeDtypeStruct((images, rows, width), BF)] * (2 * count),
        input_output_aliases={1 + count + 11 + i: i for i in range(len(extra))},
        cost_estimate=cost(
            all_rows * width * (width + 4 * hidden_count) * 2,
            all_rows * (width * 16 + hidden_count * 4) + (w_output.size + 2 * w_up.size) * 2,
        ),
        compiler_params=pltpu.CompilerParams(vmem_limit_bytes=VMEM_BYTES),
        name="middle",
    )(me.reshape(1), *inputs)


def mixed_back(grad, w_wide, exact, chunk, kept):
    images, count, rows, width = grad.shape
    _, _, length, wide_heads = exact.shape
    heads = wide_heads // WIDE

    def kernel(grad_ref, w_ref, exact_ref, *refs):
        out_ref = refs[-1]
        result = mm(grad_ref[0].reshape(2 * rows, width), w_ref[...]).astype(BF).astype(F32)
        for e in range(heads):
            here = slice(e * WIDE, (e + 1) * WIDE)
            mine = result[:, here]
            exact = exact_ref[0, :, :, here].reshape(2 * rows, WIDE)
            delta = jnp.sum(mine * exact, axis=-1, keepdims=True)
            value = put_parts(mine, delta, SUM_AT).astype(BF)
            out_ref[0, :, :, here] = value.reshape(2, rows, WIDE)

    full = pl.BlockSpec((1, 2, rows, wide_heads), lambda im, b: (im, b, chunk, 0))
    extra = list(kept)
    return pl.pallas_call(
        kernel,
        grid=(images, count // 2),
        in_specs=[
            pl.BlockSpec((1, 2, rows, width), lambda im, b: (im, b, 0, 0)),
            pl.BlockSpec(w_wide.shape, lambda im, b: (0, 0)),
            full,
        ]
        + [pl.BlockSpec(memory_space=pl.ANY)] * len(extra),
        out_specs=full,
        out_shape=jax.ShapeDtypeStruct(exact.shape, BF),
        input_output_aliases={3 + i: i for i in range(len(extra))},
        cost_estimate=cost(
            images * count * rows * width * wide_heads,
            images * count * rows * (width * 2 + wide_heads * 6) + w_wide.size * 2,
        ),
        compiler_params=pltpu.CompilerParams(vmem_limit_bytes=VMEM_BYTES),
        name="mixed_back",
    )(grad, w_wide, exact, *extra)


def attend_back(query, grad, qkv, first, heads):
    images, keys, wide_heads = query.shape
    every = wide_heads // WIDE
    rows = min(512, keys)
    span = min(512, keys)
    steps = keys // rows

    def kernel(q_ref, do_ref, k_ref, v_ref, dq_ref, dk_ref, dv_ref, kt, dk, dv):
        step = pl.program_id(2)

        @pl.when(step == 0)
        def _():
            kt[...] = k_ref[0].T
            dk[...] = jnp.zeros_like(dk)
            dv[...] = jnp.zeros_like(dv)

        q = q_ref[0]
        do = do_ref[0]
        turned = jnp.zeros((WIDE, rows), F32)
        for at in range(0, keys, span):
            here = slice(at, at + span)
            probs = jnp.exp2(mm(k_ref[0, here], q, NT))
            grad_scores = (probs * mm(v_ref[0, here], do, NT)).astype(BF)
            dv[here] += mm(probs.astype(BF), do)
            dk[here] += mm(grad_scores, q)
            turned = turned + mm(kt[:, here], grad_scores)
        dq_ref[0] = (turned.T * SCALE).astype(BF)

        @pl.when(step == steps - 1)
        def _():
            dk_ref[0] = (dk[...] * (1.0 / LOG2E)).astype(BF)
            dv_ref[0] = dv[...].astype(BF)

    row_in = pl.BlockSpec((1, rows, WIDE), lambda i, e, b: (i, b, e + first))
    row_out = pl.BlockSpec((1, rows, WIDE), lambda i, e, b: (i, b, e))

    def all_spec(shift):
        return pl.BlockSpec((1, keys, WIDE), lambda i, e, b: (i, 0, e + shift))

    shape = jax.ShapeDtypeStruct((images, keys, heads * WIDE), BF)
    scores = images * heads * keys * keys
    return pl.pallas_call(
        kernel,
        grid=(images, heads, steps),
        in_specs=[row_in, row_in, all_spec(every + first), all_spec(2 * every + first)],
        out_specs=[row_out, all_spec(0), all_spec(0)],
        out_shape=[shape] * 3,
        scratch_shapes=[
            pltpu.VMEM((WIDE, keys), BF),
            pltpu.VMEM((keys, WIDE), F32),
            pltpu.VMEM((keys, WIDE), F32),
        ],
        cost_estimate=cost(5 * scores * WIDE * 2, 7 * images * keys * wide_heads * 2, scores),
        compiler_params=pltpu.CompilerParams(vmem_limit_bytes=VMEM_BYTES),
        name="attend_back",
    )(query, grad, qkv, qkv)


def project_back(grads, tokens, w_turned, gain, shift, narrow):
    images, count, length, width = tokens.shape
    parts = len(grads[0])
    part = grads[0][0].shape[-1]
    wide = parts * part
    own = narrow.shape[1]
    flat = [piece for kind in grads for piece in kind]
    last_image, last_block = images - 1, count - 1

    def kernel(*refs):
        ins = refs[: len(flat)]
        tok_ref, w_ref, g_ref, s_ref, n_ref = refs[len(flat) : len(flat) + 5]
        outs = refs[len(flat) + 5 : -1]
        held = refs[-1]
        dh_refs = outs[:count]
        weight_ref, norm_ref, bias_ref = outs[count:]
        block = pl.program_id(1)
        first = (pl.program_id(0) == 0) & (block == 0)

        @pl.when(first)
        def _():
            held[...] = jnp.zeros_like(held)
            norm_ref[...] = jnp.zeros_like(norm_ref)
            bias_ref[...] = jnp.zeros_like(bias_ref)

        normed, _ = norm_parts(tok_ref[0, 0].astype(F32))
        turned = (normed * g_ref[...] + s_ref[...]).astype(BF).T
        total = jnp.zeros((length, width), F32)
        for i, ref in enumerate(ins):
            piece = ref[0, 0]
            here = slice(i * part, (i + 1) * part)
            total = total + mm(piece, w_ref[here])
            held[:, here] += mm(turned, piece)
            bias_ref[:, here] += jnp.sum(piece.astype(F32), axis=0, keepdims=True)
        for j in range(count):

            @pl.when(block == j)
            def _():
                dh_refs[j][0] = total.astype(BF)

        norm_ref[0:1] += jnp.sum(total * normed, axis=0, keepdims=True)
        norm_ref[1:2] += jnp.sum(total, axis=0, keepdims=True)

        @pl.when((pl.program_id(0) == last_image) & (block == last_block))
        def _():
            for kind in range(3):
                whole = held[:, kind * wide : (kind + 1) * wide].astype(BF)
                weight_ref[kind] = mm(whole, n_ref[...]).astype(BF)

    piece_spec = pl.BlockSpec((1, 1, length, part), lambda im, b: (im, b, 0, 0))
    row_spec = pl.BlockSpec((1, 1, length, width), lambda im, b: (im, b, 0, 0))

    def whole_spec(shape):
        return pl.BlockSpec(shape, lambda im, b: (0,) * len(shape))

    shapes = [(3, width, own), (2, width), (1, 3 * wide)]
    kinds = [BF, F32, F32]
    all_rows = images * count * length
    return pl.pallas_call(
        kernel,
        grid=(images, count),
        in_specs=[piece_spec] * len(flat)
        + [row_spec]
        + [whole_spec(a.shape) for a in (w_turned, gain, shift, narrow)],
        out_specs=[pl.BlockSpec((1, length, width), lambda im, b: (im, 0, 0))] * count
        + [whole_spec(shape) for shape in shapes],
        out_shape=[jax.ShapeDtypeStruct((images, length, width), BF)] * count
        + [jax.ShapeDtypeStruct(shape, kind) for shape, kind in zip(shapes, kinds)],
        scratch_shapes=[pltpu.VMEM((width, 3 * wide), F32)],
        cost_estimate=cost(
            2 * all_rows * width * wide * 3,
            all_rows * (wide * 6 + width * 4) + w_turned.size * 2,
        ),
        compiler_params=pltpu.CompilerParams(vmem_limit_bytes=VMEM_BYTES),
        name="project_back",
    )(*flat, tokens, w_turned, gain, shift, narrow)


def local(
    tokens,
    patch_mask,
    gain_one,
    shift_one,
    w_query,
    b_query,
    w_key,
    w_value,
    b_value,
    w_output,
    b_output,
    gain_two,
    shift_two,
    w_up,
    b_up,
    w_down,
    b_down,
    cotangent,
):
    me = lax.axis_index("seq")
    count = lax.axis_size("seq")
    fcount = lax.axis_size("fsdp")
    images, length, width = tokens.shape
    own = w_query.shape[1]
    heads = own // HEAD
    wide_heads = heads * WIDE
    group = fcount // count
    rows = length // CHUNKS

    qkv_shard = jnp.concatenate([w_query, w_key, w_value], axis=1)
    small = jnp.concatenate(
        [patch_mask.astype(BF).reshape(-1)]
        + [gain_one, shift_one, b_output, gain_two, shift_two, b_down]
    )
    small = spread(small)
    qkv_blocks, qkv_index = ring_gather(qkv_shard, 0)
    w_wide = place_wide(qkv_blocks, qkv_index, widen(3 * own, 3 * wide_heads))
    cut = w_output.shape[0]
    lower = jnp.concatenate([w_output, w_down], axis=0)
    lower = lax.all_gather(lower, "fsdp", axis=0)
    output_cols = lower[:, :cut].reshape(width, own)
    down_rows = lower[:, cut:]
    up_mat = lax.all_gather(w_up, "fsdp", axis=0, tiled=True)

    patches = images * length
    valid = jnp.stack([block[:patches].reshape(images, length) for block in small], axis=1)
    bias_mask = jnp.where(valid > 0, 0.0, NEG).astype(F32)
    vectors = reorder([block[patches:].reshape(6, own) for block in small], me)
    vectors = jnp.concatenate(vectors, axis=1).astype(F32)
    g_one, s_one, b_out, g_two, s_two, b_dn = [vectors[i : i + 1] for i in range(6)]

    output_mat = jnp.concatenate(reorder(spread(output_cols), me), axis=1)
    output_mat = output_mat.reshape(count, own, width)

    def down_part(j):
        start = (me ^ j) * group
        return lax.dynamic_slice_in_dim(down_rows, start, group, 0)

    down_parts = [down_part(0)] + [swap(down_part(j), j) for j in range(1, count)]
    down_mat = jnp.concatenate(reorder(down_parts, me), axis=2).reshape(-1, width)

    expand = widen(own, wide_heads)
    own_rows = lax.dynamic_index_in_dim(output_mat, me, 0, keepdims=False)
    output_wide = mm(own_rows.T, expand).astype(BF)
    lane = np.arange(3 * wide_heads) % WIDE
    kind = np.arange(3 * wide_heads) // wide_heads
    factor = np.where(kind == 0, SCALE * LOG2E, 1.0).astype(np.float32)
    ones = (kind == 0) & (lane == MASK_AT)
    ones |= (kind == 1) & (lane >= LSE_AT) & (lane < LSE_AT + 3)
    ones |= (kind == 2) & (lane >= SUM_AT) & (lane < SUM_AT + 3)
    at_mask = ((kind == 1) & (lane == MASK_AT)).astype(np.float32)

    def widen_vector(vector):
        shaped = vector.astype(F32).reshape(heads, HEAD)
        return jnp.pad(shaped, ((0, 0), (0, WIDE - HEAD))).reshape(-1)

    def narrow(vector):
        return vector.reshape(heads, WIDE)[:, :HEAD].reshape(-1)

    bias_wide = jnp.concatenate(
        [widen_vector(b_query), jnp.zeros((wide_heads,), F32), widen_vector(b_value)]
    )
    bias_wide = bias_wide * factor + ones.astype(np.float32)
    weights = (me, output_mat, up_mat, up_mat.T, down_mat, down_mat.T, b_out, g_two, s_two, b_up.astype(F32)[None])

    images_all = images
    w_turned = w_wide.T

    def run(tokens, bias_mask, cotangent):
        images = tokens.shape[0]
        tok_all = jnp.stack(spread(tokens), axis=1)
        tok_all, cot_first = lax.optimization_barrier((tok_all, cotangent))
        cot_all = jnp.stack(spread(cot_first), axis=1)
        normed, _ = norm_parts(tok_all.astype(F32))
        h_one = (normed * g_one + s_one).astype(BF)
        product = jnp.einsum("ijld,de->ijle", h_one, w_wide, preferred_element_type=F32)
        qkv = (product * factor + bias_wide + bias_mask[..., None] * at_mask).astype(BF)

        kept_attend, kept_middle = (), ()
        mixed_chunks = []
        for c in range(CHUNKS):
            mixed, *kept_attend = attend(qkv, wide_heads, c, kept_attend)
            mixed_chunks.append(spread(mixed))
        query_wide, mixed_exact = kept_attend
        def grad_rows(c, hidden_grad, x_own):
            grad_norm = hidden_grad.astype(F32)
            normed_two, inverse_two = norm_parts(x_own)
            cot_own = cotangent[:, c * rows : (c + 1) * rows].astype(F32)
            residual = cot_own + norm_back(grad_norm, normed_two, inverse_two, g_two)
            grad_attn = residual.astype(BF)
            sums = jnp.stack(
                [
                    jnp.sum(grad_norm * normed_two, axis=(0, 1)),
                    jnp.sum(grad_norm, axis=(0, 1)),
                    jnp.sum(grad_attn.astype(F32), axis=(0, 1)),
                    jnp.sum(cot_own, axis=(0, 1)),
                ]
            )
            return residual, grad_attn, sums

        out_parts, x_parts = [], []
        grad_attn_all, grad_residual = [], []
        hidden_parts = []
        early, up_bias_grad = 0.0, 0.0
        for c in range(CHUNKS):
            result = middle(mixed_chunks[c], tok_all, cot_all, weights, c, kept_middle)
            kept_middle, x_own, gb = result[:4], result[4], result[5]
            hidden_parts.append(list(result[6 : 6 + count]))
            out_parts.append(result[6 + count :])
            x_parts.append(x_own)
            up_bias_grad = up_bias_grad + gb[0]
        h_two, activated, grad_hidden, mixed_all = kept_middle
        cot_down, up_in = cot_all, h_two
        kept_back = ()
        for c in range(CHUNKS):
            last = c == CHUNKS - 1
            hidden_grad = (collect if last else collect_direct)(hidden_parts[c])
            residual, grad_attn, sums = grad_rows(c, hidden_grad, x_parts[c])
            grad_residual.append(residual)
            early = early + sums
            if not last:
                grad_attn, cot_down, up_in = lax.optimization_barrier(
                    (grad_attn, cot_down, up_in)
                )
            stacked = jnp.stack(spread(grad_attn), axis=1)
            grad_attn_all.append(stacked)
            kept_back = (mixed_back(stacked, output_wide, mixed_exact, c, kept_back),)
        grad_mixed = kept_back[0]

        up_grad = jnp.einsum("ijld,ijlf->df", up_in, grad_hidden, preferred_element_type=F32)
        down_grad = jnp.einsum(
            "ijlf,ijld->fd", activated, cot_down, preferred_element_type=F32
        )

        wide_shape = (images, count * length, wide_heads)
        query_in = query_wide.reshape(wide_shape)
        grad_in = grad_mixed.reshape(wide_shape)
        flat_qkv = qkv.reshape(images, count * length, 3 * wide_heads)
        halves = 2 if heads % 2 == 0 else 1
        step = heads // halves
        out_parts, grad_in = lax.optimization_barrier((out_parts, grad_in))
        out_blocks = [jnp.concatenate([y[j] for y in out_parts], axis=1) for j in range(count)]
        pieces = []
        for half in range(halves):
            pieces.append(attend_back(query_in, grad_in, flat_qkv, half * step, step))
        grads = [
            [piece[k].reshape(images, count, length, -1) for piece in pieces] for k in range(3)
        ]
        out_sum = collect(out_blocks)
        grad_attn_all = jnp.concatenate(grad_attn_all, axis=2)
        mixed_late, grad_attn_all, _ = lax.optimization_barrier(
            (mixed_all, grad_attn_all, pieces[0][0])
        )
        grad_attn_cols = lax.dynamic_slice_in_dim(grad_attn_all, me * own, own, 3)
        output_grad = jnp.einsum(
            "ijle,ijld->ed", mixed_late, grad_attn_cols, preferred_element_type=F32
        )
        result = project_back(grads, tok_all, w_turned, g_one, s_one, expand.T)
        qkv_grad, late, bias_grads = result[count:]
        grad_norm_one = collect(list(result[:count])).astype(F32)

        layer_out = (jnp.concatenate(x_parts, axis=1) + out_sum.astype(F32) + b_dn).astype(BF)
        normed_one, inverse_one = norm_parts(tokens.astype(F32))
        grad_tokens = (
            jnp.concatenate(grad_residual, axis=1)
            + norm_back(grad_norm_one, normed_one, inverse_one, g_one)
        ).astype(BF)
        qkv_grad = qkv_grad if images_all == 1 else qkv_grad.astype(F32)
        sums = (down_grad, up_grad, output_grad, qkv_grad, early, up_bias_grad, late, bias_grads)
        return sums, (layer_out, grad_tokens)

    if images == 1:
        sums, (layer_out, grad_tokens) = run(tokens, bias_mask, cotangent)
    else:
        items = (tokens[:, None], bias_mask[:, None], cotangent[:, None])
        shapes = jax.eval_shape(lambda item: run(*item)[0], jax.tree.map(lambda a: a[0], items))
        empty = jax.tree.map(lambda a: jnp.zeros(a.shape, a.dtype), shapes)

        def step(totals, item):
            sums, results = run(*item)
            return jax.tree.map(jnp.add, totals, sums), results

        sums, (layer_out, grad_tokens) = lax.scan(step, empty, items)
        layer_out, grad_tokens = layer_out[:, 0], grad_tokens[:, 0]
    down_grad, up_grad, output_grad, qkv_grad, early, up_bias_grad, late, bias_grads = sums

    down_grad = down_grad.astype(BF).reshape(group, -1, width)

    def down_cols(j):
        return lax.dynamic_slice_in_dim(down_grad, (me ^ j) * own, own, 2)

    down_pieces = [down_cols(0)] + [swap(down_cols(j), j) for j in range(1, count)]
    down_pieces = jnp.concatenate(reorder(down_pieces, me), axis=0)
    final_up = lax.psum_scatter(
        up_grad.astype(BF).reshape(fcount, width // fcount, -1), "fsdp", scatter_dimension=0
    ).astype(F32)
    final_down = lax.psum_scatter(down_pieces, "fsdp", scatter_dimension=0).astype(F32)
    output_grad = reorder(jnp.split(output_grad.astype(BF), count, axis=0), me)
    output_grad = jnp.concatenate(output_grad, axis=0)
    qkv_grad = qkv_grad.astype(BF).reshape(3, fcount, width // fcount, own)
    output_grad = output_grad.reshape(fcount, width // fcount, own)

    def four_parts(f):
        parts = lax.dynamic_index_in_dim(qkv_grad, f, 1, keepdims=False)
        last = lax.dynamic_index_in_dim(output_grad, f, 0, keepdims=True)
        return jnp.concatenate([parts, last], axis=0)

    four = ring_reduce(four_parts, 0)

    def to_owner(stack):
        kinds = stack.shape[0]
        parts = jnp.split(stack.reshape(kinds, count, own), count, axis=1)
        return collect(reorder([part[:, 0] for part in parts], me))

    early = to_owner(early)
    early = ring_sum(jnp.concatenate([early.reshape(-1), up_bias_grad]))
    late = to_owner(late)
    bias_grads = [bias_grads[0, i * wide_heads : (i + 1) * wide_heads] for i in (0, 2)]
    late = ring_sum(jnp.concatenate([late.reshape(-1)] + [narrow(g) for g in bias_grads]))
    gain_two_grad, shift_two_grad, b_output_grad, b_down_grad = [
        early[i * own : (i + 1) * own] for i in range(4)
    ]
    b_up_grad = early[4 * own :]
    gain_one_grad, shift_one_grad, b_query_grad, b_value_grad = [
        late[i * own : (i + 1) * own] for i in range(4)
    ]
    final_query, final_key, final_value, final_output = [four[i] for i in range(4)]
    return (
        layer_out,
        grad_tokens,
        gain_one_grad,
        shift_one_grad,
        final_query,
        b_query_grad,
        final_key,
        final_value,
        b_value_grad,
        final_output,
        b_output_grad,
        gain_two_grad,
        shift_two_grad,
        final_up,
        b_up_grad,
        final_down,
        b_down_grad,
    )


def solution(mesh):
    rows = P("fsdp", "seq", None)
    matrix = P("fsdp", "seq")
    vector = P("seq")
    return jax.shard_map(
        local,
        mesh=mesh,
        in_specs=(
            rows,
            matrix,
            vector,
            vector,
            matrix,
            vector,
            matrix,
            matrix,
            vector,
            matrix,
            vector,
            vector,
            vector,
            matrix,
            vector,
            matrix,
            vector,
            rows,
        ),
        out_specs=(
            rows,
            rows,
            vector,
            vector,
            matrix,
            vector,
            matrix,
            matrix,
            vector,
            matrix,
            vector,
            vector,
            vector,
            matrix,
            vector,
            matrix,
            vector,
        ),
        check_vma=False,
    )
```

```python
import functools
import math

import jax
import jax.numpy as jnp
import numpy as np
from jax import lax
from jax.experimental import pallas as pl
from jax.experimental.pallas import tpu as pltpu
from jax.sharding import PartitionSpec as P

HEAD = 72
WIDE = 128
MASK_AT = HEAD
LSE_AT = HEAD + 1
SUM_AT = HEAD
CHUNKS = 1
BESIDE_AT = 3

EPS = 1e-06
ROOT = 0.7978845608028654
CUBIC = 0.044715
NEG = -1e30
LOG2E = math.log2(math.e)
SCALE = HEAD ** (-0.5)

BF = jnp.bfloat16
F32 = jnp.float32
NT = (((1,), (1,)), ((), ()))
NN = (((1,), (0,)), ((), ()))
VMEM_BYTES = 56 << 20


def mm(left, right, dims=NN):
    return lax.dot_general(left, right, dims, preferred_element_type=F32)


def cost(macs, moved, special=0):
    return pl.CostEstimate(flops=macs // 64, bytes_accessed=moved // 64, transcendentals=special // 64)


def swap(value, bit):
    count = lax.axis_size("seq")
    return lax.ppermute(value, "seq", [(i, i ^ bit) for i in range(count)])


def spread(value):
    count = lax.axis_size("seq")
    blocks = [None] * count
    blocks[0] = value
    have = [0]
    bit = count // 2
    while bit:
        for j in list(have):
            blocks[j | bit] = swap(blocks[j], bit)
            have.append(j | bit)
        bit //= 2
    return blocks


def collect(blocks):
    blocks = list(blocks)
    kind = blocks[0].dtype
    count = len(blocks)
    alive = list(range(count))
    bit = 1
    while bit < count:
        for j in reversed(alive):
            if j & bit:
                incoming = swap(blocks[j].astype(kind), bit)
                blocks[j ^ bit] = blocks[j ^ bit].astype(F32) + incoming.astype(F32)
        alive = [j for j in alive if not j & bit]
        bit *= 2
    return blocks[0]


def together(*values):
    return lax.optimization_barrier(values)


def collect_pair(blocks):
    own, near, across, far = blocks
    far = swap(far, 1)
    near = swap(near, 1)
    across = (across.astype(F32) + far.astype(F32)).astype(BF)
    return own.astype(F32) + near.astype(F32), across


def reorder(blocks, me):
    blocks = list(blocks)
    bit = 1
    while bit < len(blocks):
        odd = (me & bit) > 0
        blocks = [jnp.where(odd, blocks[j ^ bit], blocks[j]) for j in range(len(blocks))]
        bit *= 2
    return blocks


def ring_order():
    count = lax.axis_size("fsdp")
    if count == 8:
        return [0, 2, 4, 6, 7, 5, 3, 1]
    return list(range(count))


def ring_place():
    device = lax.axis_index("fsdp")
    if lax.axis_size("fsdp") == 8:
        return jnp.where(device % 2 == 0, device // 2, (15 - device) // 2)
    return device


def ring_shift(value, step):
    order = ring_order()
    count = len(order)
    return lax.ppermute(
        value, "fsdp", [(order[i], order[(i + step) % count]) for i in range(count)]
    )


def ring_owner(offset):
    count = lax.axis_size("fsdp")
    at = lax.rem(ring_place() + (offset + count), count)
    if count == 8:
        return jnp.where(at < 4, 2 * at, 15 - 2 * at)
    return at


def ring_gather(value, flip):
    count = lax.axis_size("fsdp")
    found = [(0, value)]
    far = (count // 2, count - 1 - count // 2)
    moving = [value, value]
    for k in range(1, count // 2 + 1):
        for way, step in ((0, 1), (1, -1)):
            if k <= far[way ^ flip]:
                moving[way] = ring_shift(moving[way], step)
                found.append((-step * k, moving[way]))
        moving = list(lax.optimization_barrier(tuple(moving)))
    index = jnp.stack([ring_owner(offset) for offset, _ in found])
    return [block for _, block in found], index


def place_wide(blocks, index, wide):
    count = len(blocks)
    rows, cols = blocks[0].shape
    merged = rows % 16 == 0

    def kernel(index_ref, *refs):
        wide_ref, out_ref, held = refs[count:]
        for i in range(count):
            held[index_ref[i]] = refs[i][...]
        if merged:
            out_ref[...] = mm(held[...].reshape(count * rows, cols), wide_ref[...]).astype(BF)
        else:
            for i in range(count):
                out_ref[i] = mm(held[i], wide_ref[...]).astype(BF)

    shape = (count * rows, wide.shape[1]) if merged else (count, rows, wide.shape[1])
    out = pl.pallas_call(
        kernel,
        grid_spec=pltpu.PrefetchScalarGridSpec(
            num_scalar_prefetch=1,
            grid=(1,),
            in_specs=[pl.BlockSpec(a.shape, lambda i, index: (0, 0)) for a in [*blocks, wide]],
            out_specs=pl.BlockSpec(shape, lambda i, index: (0,) * len(shape)),
            scratch_shapes=[pltpu.VMEM((count, rows, cols), BF)],
        ),
        out_shape=jax.ShapeDtypeStruct(shape, BF),
        cost_estimate=cost(count * rows * cols * wide.shape[1], 4 * count * rows * cols),
        compiler_params=pltpu.CompilerParams(vmem_limit_bytes=VMEM_BYTES),
        name="place_wide",
    )(index, *blocks, wide)
    return out.reshape(count * rows, wide.shape[1])


def ring_reduce(take, flip, beside, side, side_steps):
    side_steps = list(side_steps)
    count = lax.axis_size("fsdp")
    far = (count // 2, count - 1 - count // 2)
    total = take(ring_owner(0)).astype(F32)
    incoming = [None, None]
    for k in range(count // 2, 0, -1):
        for way, step in ((0, 1), (1, -1)):
            if k <= far[way ^ flip]:
                part = take(ring_owner(step * k))
                if incoming[way] is not None:
                    part = (part.astype(F32) + incoming[way].astype(F32)).astype(BF)
                incoming[way] = ring_shift(part, step)
        if side_steps:
            side = side_steps.pop(0)(side)
        if incoming[1] is not None and incoming[0] is not None:
            incoming, side = together(incoming, side)
        if k == BESIDE_AT:
            incoming, beside = together(incoming, beside)
    return total + incoming[0].astype(F32) + incoming[1].astype(F32), beside, side


def sum_steps():
    count = lax.axis_size("fsdp")

    def step(bit, value):
        return value + lax.ppermute(value, "fsdp", [(i, i ^ bit) for i in range(count)])

    bits = [1 << i for i in range(count.bit_length() - 1)]
    return [functools.partial(step, bit) for bit in bits]


def norm_parts(value):
    mean = jnp.mean(value, axis=-1, keepdims=True)
    centered = value - mean
    inverse = lax.rsqrt(jnp.mean(centered * centered, axis=-1, keepdims=True) + EPS)
    return centered * inverse, inverse


def norm_back(grad_out, normed, inverse, gain):
    scaled = grad_out * gain
    first = jnp.mean(scaled, axis=-1, keepdims=True)
    second = jnp.mean(scaled * normed, axis=-1, keepdims=True)
    return inverse * (scaled - first - normed * second)


def three_parts(value):
    high = value.astype(BF).astype(F32)
    rest = value - high
    middle = rest.astype(BF).astype(F32)
    return high, middle, rest - middle


def put_parts(value, column, at):
    lane = lax.broadcasted_iota(jnp.int32, value.shape, 1)
    for i, part in enumerate(three_parts(column)):
        value = jnp.where(lane == at + i, -part, value)
    return value


def widen(rows, cols, dtype=BF):
    source = lax.broadcasted_iota(jnp.int32, (rows, cols), 0)
    target = lax.broadcasted_iota(jnp.int32, (rows, cols), 1)
    return ((source // HEAD) * WIDE + source % HEAD == target).astype(dtype)


def attend(qkv, wide_heads, chunk, kept):
    images, count, length, _ = qkv.shape
    heads = wide_heads // WIDE
    rows = length // CHUNKS
    keys = count * length
    flat = qkv.reshape(images, keys, 3 * wide_heads)

    def kernel(q_ref, kv_ref, *refs):
        mixed_ref, query_ref, exact_ref, turned = refs[-4:]

        @pl.when(pl.program_id(1) == 0)
        def _():
            for e in range(heads):
                at = wide_heads + e * WIDE
                turned[e] = kv_ref[0, :, at : at + WIDE].T

        total = jnp.zeros((rows, heads * HEAD), F32)
        for e in range(heads):
            here = slice(e * WIDE, (e + 1) * WIDE)
            query = q_ref[0, 0, :, here]
            v = kv_ref[0, :, 2 * wide_heads + e * WIDE : 2 * wide_heads + (e + 1) * WIDE]
            scores = mm(query, turned[e])
            top = jnp.max(scores, axis=-1, keepdims=True)
            weights = jnp.exp2(scores - top).astype(BF)
            mixed = mm(weights, v)
            summed = mixed[:, SUM_AT : SUM_AT + 1]
            mixed = mixed / summed
            log_total = top + jnp.log2(summed)
            exact_ref[0, 0, :, here] = mixed
            query_ref[0, 0, :, here] = put_parts(query.astype(F32), log_total, LSE_AT).astype(BF)
            source = lax.broadcasted_iota(jnp.int32, (WIDE, heads * HEAD), 0)
            target = lax.broadcasted_iota(jnp.int32, (WIDE, heads * HEAD), 1)
            pick = ((source < HEAD) & (source + e * HEAD == target)).astype(F32).astype(BF)
            total = total + mm(mixed.astype(BF), pick)
        mixed_ref[0, 0] = total.astype(BF)

    part = pl.BlockSpec((1, 1, rows, wide_heads), lambda i, b: (i, b, chunk, 0))
    shapes = [
        jax.ShapeDtypeStruct((images, count, rows, heads * HEAD), BF),
        jax.ShapeDtypeStruct((images, count, length, wide_heads), BF),
        jax.ShapeDtypeStruct((images, count, length, wide_heads), F32),
    ]
    outs = [pl.BlockSpec((1, 1, rows, heads * HEAD), lambda i, b: (i, b, 0, 0)), part, part]
    extra = list(kept)
    scores = images * count * rows * keys * heads
    return pl.pallas_call(
        kernel,
        grid=(images, count),
        in_specs=[part, pl.BlockSpec((1, keys, 3 * wide_heads), lambda i, b: (i, 0, 0))]
        + [pl.BlockSpec(memory_space=pl.ANY)] * len(extra),
        out_specs=outs,
        out_shape=shapes,
        input_output_aliases={2 + i: 1 + i for i in range(len(extra))},
        scratch_shapes=[pltpu.VMEM((heads, WIDE, keys), BF)],
        cost_estimate=cost(2 * scores * WIDE * 2, flat.size * 2 + 3 * images * keys * wide_heads, scores),
        compiler_params=pltpu.CompilerParams(vmem_limit_bytes=VMEM_BYTES),
        name="attend",
    )(qkv, flat, *extra)


def middle(mixed, tokens, cotangent, weights, chunk, kept):
    images, count, length, width = tokens.shape
    me, w_output, w_up, up_turned, w_down, down_turned, b_output, gain, shift, b_up = weights
    rows = length // CHUNKS
    own = mixed[0].shape[-1]
    hidden_count = w_up.shape[1]

    def kernel(me_ref, *refs):
        mixed_refs = refs[:count]
        (
            tok_ref,
            cot_ref,
            wo_ref,
            up_ref,
            up_turned_ref,
            down_ref,
            down_turned_ref,
            bo_ref,
            g_ref,
            s_ref,
            bu_ref,
        ) = refs[count : count + 11]
        outs = refs[-(6 + 2 * count) :]
        h_ref, z_ref, du_ref, cat_ref, x_ref, gb_ref = outs[:6]
        dh_refs, y_refs = outs[6 : 6 + count], outs[6 + count :]
        block = pl.program_id(1)
        x_one = tok_ref[0, 0].astype(F32) + bo_ref[...]
        pieces = []
        for i in range(count):
            piece = mixed_refs[i][0, 0]
            pieces.append(piece)
            x_one = x_one + mm(piece, wo_ref[me_ref[0] ^ i])
        cat_ref[0, 0] = jnp.concatenate(pieces, axis=-1)

        @pl.when(block == 0)
        def _():
            x_ref[0] = x_one

        normed, _ = norm_parts(x_one)
        h_two = (normed * g_ref[...] + s_ref[...]).astype(BF)
        h_ref[0, 0] = h_two
        hidden = mm(h_two, up_ref[...]) + bu_ref[...]
        grad_act = mm(cot_ref[0, 0], down_turned_ref[...])
        square = hidden * hidden
        inner = jnp.tanh(ROOT * (hidden + CUBIC * square * hidden))
        half = 0.5 * (1.0 + inner)
        z = (hidden * half).astype(BF)
        slope = half + 0.5 * hidden * (1.0 - inner * inner) * ROOT * (1.0 + 3.0 * CUBIC * square)
        wide_grad = grad_act * slope
        grad_hidden = wide_grad.astype(BF)
        z_ref[0, 0] = z
        du_ref[0, 0] = grad_hidden
        dh = mm(grad_hidden, up_turned_ref[...]).astype(BF)
        y = mm(z, down_ref[...]).astype(BF)
        for j in range(count):

            @pl.when(block == j)
            def _():
                dh_refs[j][0] = dh
                y_refs[j][0] = y

        summed = jnp.sum(grad_hidden.astype(F32), axis=0, keepdims=True)
        first = (pl.program_id(0) == 0) & (block == 0)

        @pl.when(first)
        def _():
            gb_ref[...] = summed

        @pl.when(jnp.logical_not(first))
        def _():
            gb_ref[...] += summed

    def piece_spec(i):
        return pl.BlockSpec((1, 1, rows, own), lambda im, b, me_ref: (im, b ^ i, 0, 0))

    def whole_spec(array):
        return pl.BlockSpec(array.shape, lambda im, b, me_ref: (0,) * array.ndim)

    full = pl.BlockSpec((1, 1, rows, width), lambda im, b, me_ref: (im, b, chunk, 0))
    full_hidden = pl.BlockSpec((1, 1, rows, hidden_count), lambda im, b, me_ref: (im, b, chunk, 0))
    part = pl.BlockSpec((1, rows, width), lambda im, b, me_ref: (im, 0, 0))
    constants = [w_output, w_up, up_turned, w_down, down_turned, b_output, gain, shift, b_up]
    extra = list(kept)
    inputs = [*mixed, tokens, cotangent, *constants, *extra]
    all_rows = images * count * rows
    return pl.pallas_call(
        kernel,
        grid_spec=pltpu.PrefetchScalarGridSpec(
            num_scalar_prefetch=1,
            grid=(images, count),
            in_specs=[piece_spec(i) for i in range(count)]
            + [full, full]
            + [whole_spec(array) for array in constants]
            + [pl.BlockSpec(memory_space=pl.ANY)] * len(extra),
            out_specs=[
                full,
                full_hidden,
                full_hidden,
                full,
                part,
                pl.BlockSpec((1, hidden_count), lambda im, b, me_ref: (0, 0)),
            ]
            + [part] * (2 * count),
        ),
        out_shape=[
            jax.ShapeDtypeStruct(tokens.shape, BF),
            jax.ShapeDtypeStruct((images, count, length, hidden_count), BF),
            jax.ShapeDtypeStruct((images, count, length, hidden_count), BF),
            jax.ShapeDtypeStruct(tokens.shape, BF),
            jax.ShapeDtypeStruct((images, rows, width), F32),
            jax.ShapeDtypeStruct((1, hidden_count), F32),
        ]
        + [jax.ShapeDtypeStruct((images, rows, width), BF)] * (2 * count),
        input_output_aliases={1 + count + 11 + i: i for i in range(len(extra))},
        cost_estimate=cost(
            all_rows * width * (width + 4 * hidden_count) * 2,
            all_rows * (width * 16 + hidden_count * 4) + (w_output.size + 2 * w_up.size) * 2,
        ),
        compiler_params=pltpu.CompilerParams(vmem_limit_bytes=VMEM_BYTES),
        name="middle",
    )(me.reshape(1), *inputs)


def mixed_back(grad, w_wide, exact, chunk, kept):
    images, count, rows, width = grad.shape
    _, _, length, wide_heads = exact.shape
    heads = wide_heads // WIDE

    def kernel(grad_ref, w_ref, exact_ref, *refs):
        out_ref = refs[-1]
        result = mm(grad_ref[0, 0], w_ref[...]).astype(BF).astype(F32)
        for e in range(heads):
            here = slice(e * WIDE, (e + 1) * WIDE)
            mine = result[:, here]
            exact = exact_ref[0, 0, :, here]
            delta = jnp.sum(mine * exact, axis=-1, keepdims=True)
            value = put_parts(mine, delta, SUM_AT).astype(BF)
            out_ref[0, 0, :, here] = value

    full = pl.BlockSpec((1, 1, rows, wide_heads), lambda im, b: (im, b, chunk, 0))
    extra = list(kept)
    return pl.pallas_call(
        kernel,
        grid=(images, count),
        in_specs=[
            pl.BlockSpec((1, 1, rows, width), lambda im, b: (im, b, 0, 0)),
            pl.BlockSpec(w_wide.shape, lambda im, b: (0, 0)),
            full,
        ]
        + [pl.BlockSpec(memory_space=pl.ANY)] * len(extra),
        out_specs=full,
        out_shape=jax.ShapeDtypeStruct(exact.shape, BF),
        input_output_aliases={3 + i: i for i in range(len(extra))},
        cost_estimate=cost(
            images * count * rows * width * wide_heads,
            images * count * rows * (width * 2 + wide_heads * 6) + w_wide.size * 2,
        ),
        compiler_params=pltpu.CompilerParams(vmem_limit_bytes=VMEM_BYTES),
        name="mixed_back",
    )(grad, w_wide, exact, *extra)


def attend_back(query, grad, qkv, first, heads):
    images, keys, wide_heads = query.shape
    every = wide_heads // WIDE
    rows = min(512, keys)
    span = min(512, keys)
    steps = keys // rows

    def kernel(q_ref, do_ref, k_ref, v_ref, dq_ref, dk_ref, dv_ref, kt, dk, dv):
        step = pl.program_id(2)

        @pl.when(step == 0)
        def _():
            kt[...] = k_ref[0].T
            dk[...] = jnp.zeros_like(dk)
            dv[...] = jnp.zeros_like(dv)

        q = q_ref[0]
        do = do_ref[0]
        turned = jnp.zeros((WIDE, rows), F32)
        for at in range(0, keys, span):
            here = slice(at, at + span)
            probs = jnp.exp2(mm(k_ref[0, here], q, NT))
            grad_scores = (probs * mm(v_ref[0, here], do, NT)).astype(BF)
            dv[here] += mm(probs.astype(BF), do)
            dk[here] += mm(grad_scores, q)
            turned = turned + mm(kt[:, here], grad_scores)
        dq_ref[0] = (turned.T * SCALE).astype(BF)

        @pl.when(step == steps - 1)
        def _():
            dk_ref[0] = (dk[...] * (1.0 / LOG2E)).astype(BF)
            dv_ref[0] = dv[...].astype(BF)

    row_in = pl.BlockSpec((1, rows, WIDE), lambda i, e, b: (i, b, e + first))
    row_out = pl.BlockSpec((1, rows, WIDE), lambda i, e, b: (i, b, e))

    def all_spec(shift):
        return pl.BlockSpec((1, keys, WIDE), lambda i, e, b: (i, 0, e + shift))

    shape = jax.ShapeDtypeStruct((images, keys, heads * WIDE), BF)
    scores = images * heads * keys * keys
    return pl.pallas_call(
        kernel,
        grid=(images, heads, steps),
        in_specs=[row_in, row_in, all_spec(every + first), all_spec(2 * every + first)],
        out_specs=[row_out, all_spec(0), all_spec(0)],
        out_shape=[shape] * 3,
        scratch_shapes=[
            pltpu.VMEM((WIDE, keys), BF),
            pltpu.VMEM((keys, WIDE), F32),
            pltpu.VMEM((keys, WIDE), F32),
        ],
        cost_estimate=cost(5 * scores * WIDE * 2, 7 * images * keys * wide_heads * 2, scores),
        compiler_params=pltpu.CompilerParams(vmem_limit_bytes=VMEM_BYTES),
        name="attend_back",
    )(query, grad, qkv, qkv)


def project_back(grads, tokens, w_turned, gain, shift, narrow):
    images, count, length, width = tokens.shape
    parts = len(grads[0])
    part = grads[0][0].shape[-1]
    wide = parts * part
    own = narrow.shape[1]
    flat = [piece for kind in grads for piece in kind]
    last_image, last_block = images - 1, count - 1

    def kernel(*refs):
        ins = refs[: len(flat)]
        tok_ref, w_ref, g_ref, s_ref, n_ref = refs[len(flat) : len(flat) + 5]
        outs = refs[len(flat) + 5 : -1]
        held = refs[-1]
        dh_refs = outs[:count]
        weight_ref, norm_ref, bias_ref = outs[count:]
        block = pl.program_id(1)
        first = (pl.program_id(0) == 0) & (block == 0)

        @pl.when(first)
        def _():
            held[...] = jnp.zeros_like(held)
            norm_ref[...] = jnp.zeros_like(norm_ref)
            bias_ref[...] = jnp.zeros_like(bias_ref)

        normed, _ = norm_parts(tok_ref[0, 0].astype(F32))
        turned = (normed * g_ref[...] + s_ref[...]).astype(BF).T
        total = jnp.zeros((length, width), F32)
        for i, ref in enumerate(ins):
            piece = ref[0, 0]
            here = slice(i * part, (i + 1) * part)
            total = total + mm(piece, w_ref[here])
            held[:, here] += mm(turned, piece)
            bias_ref[:, here] += jnp.sum(piece.astype(F32), axis=0, keepdims=True)
        for j in range(count):

            @pl.when(block == j)
            def _():
                dh_refs[j][0] = total.astype(BF)

        norm_ref[0:1] += jnp.sum(total * normed, axis=0, keepdims=True)
        norm_ref[1:2] += jnp.sum(total, axis=0, keepdims=True)

        @pl.when((pl.program_id(0) == last_image) & (block == last_block))
        def _():
            for kind in range(3):
                whole = held[:, kind * wide : (kind + 1) * wide].astype(BF)
                weight_ref[kind] = mm(whole, n_ref[...]).astype(BF)

    piece_spec = pl.BlockSpec((1, 1, length, part), lambda im, b: (im, b, 0, 0))
    row_spec = pl.BlockSpec((1, 1, length, width), lambda im, b: (im, b, 0, 0))

    def whole_spec(shape):
        return pl.BlockSpec(shape, lambda im, b: (0,) * len(shape))

    shapes = [(3, width, own), (2, width), (1, 3 * wide)]
    kinds = [BF, F32, F32]
    all_rows = images * count * length
    return pl.pallas_call(
        kernel,
        grid=(images, count),
        in_specs=[piece_spec] * len(flat)
        + [row_spec]
        + [whole_spec(a.shape) for a in (w_turned, gain, shift, narrow)],
        out_specs=[pl.BlockSpec((1, length, width), lambda im, b: (im, 0, 0))] * count
        + [whole_spec(shape) for shape in shapes],
        out_shape=[jax.ShapeDtypeStruct((images, length, width), BF)] * count
        + [jax.ShapeDtypeStruct(shape, kind) for shape, kind in zip(shapes, kinds)],
        scratch_shapes=[pltpu.VMEM((width, 3 * wide), F32)],
        cost_estimate=cost(
            2 * all_rows * width * wide * 3,
            all_rows * (wide * 6 + width * 4) + w_turned.size * 2,
        ),
        compiler_params=pltpu.CompilerParams(vmem_limit_bytes=VMEM_BYTES),
        name="project_back",
    )(*flat, tokens, w_turned, gain, shift, narrow)


def local(
    tokens,
    patch_mask,
    gain_one,
    shift_one,
    w_query,
    b_query,
    w_key,
    w_value,
    b_value,
    w_output,
    b_output,
    gain_two,
    shift_two,
    w_up,
    b_up,
    w_down,
    b_down,
    cotangent,
):
    me = lax.axis_index("seq")
    count = lax.axis_size("seq")
    fcount = lax.axis_size("fsdp")
    images, length, width = tokens.shape
    own = w_query.shape[1]
    heads = own // HEAD
    wide_heads = heads * WIDE
    group = fcount // count
    rows = length // CHUNKS

    qkv_shard = jnp.concatenate([w_query, w_key, w_value], axis=1)
    small = jnp.concatenate(
        [patch_mask.astype(BF).reshape(-1)]
        + [gain_one, shift_one, b_output, gain_two, shift_two, b_down]
    )
    small = spread(small)
    qkv_blocks, qkv_index = ring_gather(qkv_shard, 0)
    tok_blocks = None
    if images == 1 and count == 4:
        near, across = swap(tokens, 1), swap(tokens, 2)
        across, qkv_blocks = together(across, qkv_blocks)
        tok_blocks = [tokens, near, across, swap(across, 1)]
    w_wide = place_wide(qkv_blocks, qkv_index, widen(3 * own, 3 * wide_heads))
    cut = w_output.shape[0]
    lower = jnp.concatenate([w_output, w_down], axis=0)
    lower = lax.all_gather(lower, "fsdp", axis=0)
    output_cols = lower[:, :cut].reshape(width, own)
    down_rows = lower[:, cut:]
    up_mat = lax.all_gather(w_up, "fsdp", axis=0, tiled=True)

    patches = images * length
    valid = jnp.stack([block[:patches].reshape(images, length) for block in small], axis=1)
    bias_mask = jnp.where(valid > 0, 0.0, NEG).astype(F32)
    vectors = reorder([block[patches:].reshape(6, own) for block in small], me)
    vectors = jnp.concatenate(vectors, axis=1).astype(F32)
    g_one, s_one, b_out, g_two, s_two, b_dn = [vectors[i : i + 1] for i in range(6)]

    output_parts = spread(output_cols)

    def down_part(j):
        start = (me ^ j) * group
        return lax.dynamic_slice_in_dim(down_rows, start, group, 0)

    down_sent = [down_part(j) for j in range(count)]
    down_parts = [down_sent[0]] + [swap(down_sent[j], j) for j in range(1, count)]

    expand = widen(own, wide_heads)
    lane = np.arange(3 * wide_heads) % WIDE
    kind = np.arange(3 * wide_heads) // wide_heads
    factor = np.where(kind == 0, SCALE * LOG2E, 1.0).astype(np.float32)
    ones = (kind == 0) & (lane == MASK_AT)
    ones |= (kind == 1) & (lane >= LSE_AT) & (lane < LSE_AT + 3)
    ones |= (kind == 2) & (lane >= SUM_AT) & (lane < SUM_AT + 3)
    at_mask = ((kind == 1) & (lane == MASK_AT)).astype(np.float32)

    def widen_vector(vector):
        shaped = vector.astype(F32).reshape(heads, HEAD)
        return jnp.pad(shaped, ((0, 0), (0, WIDE - HEAD))).reshape(-1)

    def narrow(vector):
        return vector.reshape(heads, WIDE)[:, :HEAD].reshape(-1)

    bias_wide = jnp.concatenate(
        [widen_vector(b_query), jnp.zeros((wide_heads,), F32), widen_vector(b_value)]
    )
    bias_wide = bias_wide * factor + ones.astype(np.float32)

    single = images == 1
    w_turned = w_wide.T

    def scatter_up(up_grad):
        blocks = up_grad.astype(BF).reshape(fcount, width // fcount, -1)
        return lax.psum_scatter(blocks, "fsdp", scatter_dimension=0)

    def send_down(down_grad):
        shaped = down_grad.astype(BF).reshape(width, group, -1).transpose(1, 0, 2)

        def cols(j):
            return lax.dynamic_slice_in_dim(shaped, (me ^ j) * own, own, 1)

        return [cols(0)] + [swap(cols(j), j) for j in range(1, count)]

    def merge_down(got):
        return jnp.concatenate(reorder(got, me), axis=0)

    def run(tokens, bias_mask, cotangent, tok_blocks=None):
        images = tokens.shape[0]
        if tok_blocks is None:
            tok_blocks = spread(tokens)
        tok_all = jnp.stack(tok_blocks, axis=1)
        tok_all, cot_first = together(tok_all, cotangent)
        cot_blocks = spread(cot_first)
        normed, _ = norm_parts(tok_all.astype(F32))
        h_one = (normed * g_one + s_one).astype(BF)
        product = jnp.einsum("ijld,de->ijle", h_one, w_wide, preferred_element_type=F32)
        qkv = (product * factor + bias_wide + bias_mask[..., None] * at_mask).astype(BF)
        qkv, cot_blocks = together(qkv, cot_blocks)
        cot_all = jnp.stack(cot_blocks, axis=1)

        kept_attend, kept_middle = (), ()
        mixed_chunks = []
        for c in range(CHUNKS):
            mixed, *kept_attend = attend(qkv, wide_heads, c, kept_attend)
            mixed_chunks.append(spread(mixed))
        query_wide, mixed_exact = kept_attend
        mixed_exact, down_in, output_in = together(mixed_exact, down_parts, output_parts)
        down_mat = jnp.concatenate(reorder(down_in, me), axis=2).reshape(-1, width)
        output_mat = jnp.concatenate(reorder(output_in, me), axis=1)
        output_mat = output_mat.reshape(count, own, width)
        own_rows = lax.dynamic_index_in_dim(output_mat, me, 0, keepdims=False)
        output_wide = mm(own_rows.T, expand).astype(BF)
        weights = (
            me,
            output_mat,
            up_mat,
            up_mat.T,
            down_mat,
            down_mat.T,
            b_out,
            g_two,
            s_two,
            b_up.astype(F32)[None],
        )
        def grad_rows(c, hidden_grad, x_own):
            grad_norm = hidden_grad.astype(F32)
            normed_two, inverse_two = norm_parts(x_own)
            cot_own = cotangent[:, c * rows : (c + 1) * rows].astype(F32)
            residual = cot_own + norm_back(grad_norm, normed_two, inverse_two, g_two)
            grad_attn = residual.astype(BF)
            sums = jnp.stack(
                [
                    jnp.sum(grad_norm * normed_two, axis=(0, 1)),
                    jnp.sum(grad_norm, axis=(0, 1)),
                    jnp.sum(grad_attn.astype(F32), axis=(0, 1)),
                    jnp.sum(cot_own, axis=(0, 1)),
                ]
            )
            return residual, grad_attn, sums

        out_parts, x_parts = [], []
        grad_attn_all, grad_residual = [], []
        hidden_parts = []
        early, up_bias_grad = 0.0, 0.0
        for c in range(CHUNKS):
            result = middle(mixed_chunks[c], tok_all, cot_all, weights, c, kept_middle)
            kept_middle, x_own, gb = result[:4], result[4], result[5]
            hidden_parts.append(list(result[6 : 6 + count]))
            out_parts.append(result[6 + count :])
            x_parts.append(x_own)
            up_bias_grad = up_bias_grad + gb[0]
        h_two, activated, grad_hidden, mixed_all = kept_middle
        blocks = hidden_parts[0]
        if count == 4:
            near_sum, crossing = collect_pair(blocks)
            h_two, crossing = together(h_two, crossing)
            incoming = swap(crossing, 2)
        else:
            near_sum, incoming = collect(blocks), jnp.zeros((), F32)
        up_grad = jnp.einsum(
            "ijld,ijlf->df",
            h_two,
            grad_hidden,
            preferred_element_type=F32,
        ).astype(BF if single else F32)
        incoming, up_grad = together(incoming, up_grad)
        if single:
            up_grad = scatter_up(up_grad)
        hidden_grad = near_sum + incoming.astype(F32)
        residual, grad_attn, early = grad_rows(0, hidden_grad, x_parts[0])
        grad_attn, activated = together(grad_attn, activated)
        down_grad = jnp.einsum(
            "ijld,ijlf->df",
            cot_all,
            activated,
            preferred_element_type=F32,
        ).astype(BF if single else F32)
        grad_residual.append(residual)
        attn_blocks, down_grad = together(spread(grad_attn), down_grad)
        grad_attn_all = jnp.stack(attn_blocks, axis=1)
        grad_mixed = mixed_back(grad_attn_all, output_wide, mixed_exact, 0, ())

        wide_shape = (images, count * length, wide_heads)
        query_in = query_wide.reshape(wide_shape)
        grad_in = grad_mixed.reshape(wide_shape)
        flat_qkv = qkv.reshape(images, count * length, 3 * wide_heads)
        halves = 2 if heads % 2 == 0 else 1
        step = heads // halves
        grad_in, out_blocks, down_grad = together(grad_in, list(out_parts[0]), down_grad)
        if single:
            down_grad = send_down(down_grad)
            grad_in, up_grad = together(grad_in, up_grad)
        if count == 4:
            out_sum, out_across = collect_pair(out_blocks)
            grad_in, out_across = together(grad_in, out_across)
            out_incoming = swap(out_across, 2)
        else:
            out_sum, out_incoming = collect(out_blocks), jnp.zeros((), F32)
        first = attend_back(query_in, grad_in, flat_qkv, 0, step)
        pieces = [first]
        if halves == 2:
            first, down_grad = together(first, down_grad)
            if single:
                down_grad = merge_down(down_grad)
            query_in, down_grad = together(query_in, down_grad)
            pieces = [first, attend_back(query_in, grad_in, flat_qkv, step, step)]
            pieces, out_incoming = together(pieces, out_incoming)
        elif single:
            down_grad = merge_down(down_grad)
        out_sum = out_sum + out_incoming.astype(F32)
        grads = [
            [piece[k].reshape(images, count, length, -1) for piece in pieces] for k in range(3)
        ]
        grad_attn_cols = lax.dynamic_slice_in_dim(grad_attn_all, me * own, own, 3)
        output_grad = jnp.einsum(
            "ijle,ijld->ed", mixed_all, grad_attn_cols, preferred_element_type=F32
        )
        result = project_back(grads, tok_all, w_turned, g_one, s_one, expand.T)
        qkv_grad, late, bias_grads = result[count:]
        grad_norm_one = collect(list(result[:count])).astype(F32)

        layer_out = (jnp.concatenate(x_parts, axis=1) + out_sum.astype(F32) + b_dn).astype(BF)
        normed_one, inverse_one = norm_parts(tokens.astype(F32))
        grad_tokens = (
            jnp.concatenate(grad_residual, axis=1)
            + norm_back(grad_norm_one, normed_one, inverse_one, g_one)
        ).astype(BF)
        qkv_grad = qkv_grad if single else qkv_grad.astype(F32)
        sums = (down_grad, up_grad, output_grad, qkv_grad, early, up_bias_grad, late, bias_grads)
        return sums, (layer_out, grad_tokens)

    if images == 1:
        sums, (layer_out, grad_tokens) = run(tokens, bias_mask, cotangent, tok_blocks)
    else:
        items = (tokens[:, None], bias_mask[:, None], cotangent[:, None])
        shapes = jax.eval_shape(lambda item: run(*item)[0], jax.tree.map(lambda a: a[0], items))
        empty = jax.tree.map(lambda a: jnp.zeros(a.shape, a.dtype), shapes)

        def step(totals, item):
            sums, results = run(*item)
            return jax.tree.map(jnp.add, totals, sums), results

        sums, (layer_out, grad_tokens) = lax.scan(step, empty, items)
        layer_out, grad_tokens = layer_out[:, 0], grad_tokens[:, 0]
    down_grad, up_grad, output_grad, qkv_grad, early, up_bias_grad, late, bias_grads = sums

    down_pieces = down_grad if single else merge_down(send_down(down_grad))
    final_up = (up_grad if single else scatter_up(up_grad)).astype(F32)
    final_down = lax.psum_scatter(down_pieces, "fsdp", scatter_dimension=0)
    output_grad = reorder(jnp.split(output_grad.astype(BF), count, axis=0), me)
    output_grad = jnp.concatenate(output_grad, axis=0)
    qkv_grad = qkv_grad.astype(BF).reshape(3, fcount, width // fcount, own)
    output_grad = output_grad.reshape(fcount, width // fcount, own)

    def four_parts(f):
        parts = lax.dynamic_index_in_dim(qkv_grad, f, 1, keepdims=False)
        last = lax.dynamic_index_in_dim(output_grad, f, 0, keepdims=True)
        return jnp.concatenate([parts, last], axis=0)


    def to_owner(stack):
        kinds = stack.shape[0]
        parts = jnp.split(stack.reshape(kinds, count, own), count, axis=1)
        parts = reorder([part[:, 0] for part in parts], me)
        total = parts[0]
        for j in range(1, count):
            total = total + swap(parts[j], j)
        return jnp.concatenate(
            [total.reshape(-1)] + [narrow(g) for g in bias_grads] + [up_bias_grad]
        )

    bias_grads = [bias_grads[0, i * wide_heads : (i + 1) * wide_heads] for i in (0, 2)]
    four, final_down, vectors = ring_reduce(
        four_parts,
        0,
        final_down,
        jnp.concatenate([early, late], axis=0),
        [to_owner] + sum_steps(),
    )
    final_down = final_down.astype(F32).T
    (
        gain_two_grad,
        shift_two_grad,
        b_output_grad,
        b_down_grad,
        gain_one_grad,
        shift_one_grad,
        b_query_grad,
        b_value_grad,
    ) = [vectors[i * own : (i + 1) * own] for i in range(8)]
    b_up_grad = vectors[8 * own :]
    final_query, final_key, final_value, final_output = [four[i] for i in range(4)]
    return (
        layer_out,
        grad_tokens,
        gain_one_grad,
        shift_one_grad,
        final_query,
        b_query_grad,
        final_key,
        final_value,
        b_value_grad,
        final_output,
        b_output_grad,
        gain_two_grad,
        shift_two_grad,
        final_up,
        b_up_grad,
        final_down,
        b_down_grad,
    )


def solution(mesh):
    rows = P("fsdp", "seq", None)
    matrix = P("fsdp", "seq")
    vector = P("seq")
    return jax.shard_map(
        local,
        mesh=mesh,
        in_specs=(
            rows,
            matrix,
            vector,
            vector,
            matrix,
            vector,
            matrix,
            matrix,
            vector,
            matrix,
            vector,
            vector,
            vector,
            matrix,
            vector,
            matrix,
            vector,
            rows,
        ),
        out_specs=(
            rows,
            rows,
            vector,
            vector,
            matrix,
            vector,
            matrix,
            matrix,
            vector,
            matrix,
            vector,
            vector,
            vector,
            matrix,
            vector,
            matrix,
            vector,
        ),
        check_vma=False,
    )
```

```python
import functools
import math

import jax
import jax.numpy as jnp
import numpy as np
from jax import lax
from jax.experimental import pallas as pl
from jax.experimental.pallas import tpu as pltpu
from jax.sharding import PartitionSpec as P

HEAD = 72
WIDE = 128
MASK_AT = HEAD
LSE_AT = HEAD + 1
SUM_AT = HEAD
CHUNKS = 1
BESIDE_AT = 3

EPS = 1e-06
ROOT = 0.7978845608028654
CUBIC = 0.044715
NEG = -1e30
LOG2E = math.log2(math.e)
SCALE = HEAD ** (-0.5)

BF = jnp.bfloat16
F32 = jnp.float32
NT = (((1,), (1,)), ((), ()))
NN = (((1,), (0,)), ((), ()))
VMEM_BYTES = 56 << 20


def mm(left, right, dims=NN):
    return lax.dot_general(left, right, dims, preferred_element_type=F32)


def cost(macs, moved, special=0):
    return pl.CostEstimate(flops=macs // 64, bytes_accessed=moved // 64, transcendentals=special // 64)


def swap(value, bit):
    count = lax.axis_size("seq")
    return lax.ppermute(value, "seq", [(i, i ^ bit) for i in range(count)])


def spread(value):
    count = lax.axis_size("seq")
    blocks = [None] * count
    blocks[0] = value
    have = [0]
    bit = count // 2
    while bit:
        for j in list(have):
            blocks[j | bit] = swap(blocks[j], bit)
            have.append(j | bit)
        bit //= 2
    return blocks


def collect(blocks):
    blocks = list(blocks)
    kind = blocks[0].dtype
    count = len(blocks)
    alive = list(range(count))
    bit = 1
    while bit < count:
        for j in reversed(alive):
            if j & bit:
                incoming = swap(blocks[j].astype(kind), bit)
                blocks[j ^ bit] = blocks[j ^ bit].astype(F32) + incoming.astype(F32)
        alive = [j for j in alive if not j & bit]
        bit *= 2
    return blocks[0]


def together(*values):
    return lax.optimization_barrier(values)


def collect_pair(blocks):
    own, near, across, far = blocks
    far = swap(far, 1)
    near = swap(near, 1)
    across = (across.astype(F32) + far.astype(F32)).astype(BF)
    return own.astype(F32) + near.astype(F32), across


def reorder(blocks, me):
    blocks = list(blocks)
    bit = 1
    while bit < len(blocks):
        odd = (me & bit) > 0
        blocks = [jnp.where(odd, blocks[j ^ bit], blocks[j]) for j in range(len(blocks))]
        bit *= 2
    return blocks


def ring_order():
    count = lax.axis_size("fsdp")
    if count == 8:
        return [0, 2, 4, 6, 7, 5, 3, 1]
    return list(range(count))


def ring_place():
    device = lax.axis_index("fsdp")
    if lax.axis_size("fsdp") == 8:
        return jnp.where(device % 2 == 0, device // 2, (15 - device) // 2)
    return device


def ring_shift(value, step):
    order = ring_order()
    count = len(order)
    return lax.ppermute(
        value, "fsdp", [(order[i], order[(i + step) % count]) for i in range(count)]
    )


def ring_owner(offset):
    count = lax.axis_size("fsdp")
    at = lax.rem(ring_place() + (offset + count), count)
    if count == 8:
        return jnp.where(at < 4, 2 * at, 15 - 2 * at)
    return at


def ring_gather(value, flip):
    count = lax.axis_size("fsdp")
    found = [(0, value)]
    far = (count // 2, count - 1 - count // 2)
    moving = [value, value]
    for k in range(1, count // 2 + 1):
        for way, step in ((0, 1), (1, -1)):
            if k <= far[way ^ flip]:
                moving[way] = ring_shift(moving[way], step)
                found.append((-step * k, moving[way]))
        moving = list(lax.optimization_barrier(tuple(moving)))
    index = jnp.stack([ring_owner(offset) for offset, _ in found])
    return [block for _, block in found], index


def place_wide(blocks, index, wide):
    count = len(blocks)
    rows, cols = blocks[0].shape
    merged = rows % 16 == 0

    def kernel(index_ref, *refs):
        wide_ref, out_ref, held = refs[count:]
        for i in range(count):
            held[index_ref[i]] = refs[i][...]
        if merged:
            out_ref[...] = mm(held[...].reshape(count * rows, cols), wide_ref[...]).astype(BF)
        else:
            for i in range(count):
                out_ref[i] = mm(held[i], wide_ref[...]).astype(BF)

    shape = (count * rows, wide.shape[1]) if merged else (count, rows, wide.shape[1])
    out = pl.pallas_call(
        kernel,
        grid_spec=pltpu.PrefetchScalarGridSpec(
            num_scalar_prefetch=1,
            grid=(1,),
            in_specs=[pl.BlockSpec(a.shape, lambda i, index: (0, 0)) for a in [*blocks, wide]],
            out_specs=pl.BlockSpec(shape, lambda i, index: (0,) * len(shape)),
            scratch_shapes=[pltpu.VMEM((count, rows, cols), BF)],
        ),
        out_shape=jax.ShapeDtypeStruct(shape, BF),
        cost_estimate=cost(count * rows * cols * wide.shape[1], 4 * count * rows * cols),
        compiler_params=pltpu.CompilerParams(vmem_limit_bytes=VMEM_BYTES),
        name="place_wide",
    )(index, *blocks, wide)
    return out.reshape(count * rows, wide.shape[1])


def ring_reduce(take, flip, beside, side, side_steps):
    side_steps = list(side_steps)
    count = lax.axis_size("fsdp")
    far = (count // 2, count - 1 - count // 2)
    total = take(ring_owner(0)).astype(F32)
    incoming = [None, None]
    for k in range(count // 2, 0, -1):
        for way, step in ((0, 1), (1, -1)):
            if k <= far[way ^ flip]:
                part = take(ring_owner(step * k))
                if incoming[way] is not None:
                    part = (part.astype(F32) + incoming[way].astype(F32)).astype(BF)
                incoming[way] = ring_shift(part, step)
        if side_steps:
            side = side_steps.pop(0)(side)
        if incoming[1] is not None and incoming[0] is not None:
            incoming, side = together(incoming, side)
        if k == BESIDE_AT:
            incoming, beside = together(incoming, beside)
    return total + incoming[0].astype(F32) + incoming[1].astype(F32), beside, side


def sum_steps():
    count = lax.axis_size("fsdp")

    def step(bit, value):
        return value + lax.ppermute(value, "fsdp", [(i, i ^ bit) for i in range(count)])

    bits = [1 << i for i in range(count.bit_length() - 1)]
    return [functools.partial(step, bit) for bit in bits]


def norm_parts(value):
    mean = jnp.mean(value, axis=-1, keepdims=True)
    centered = value - mean
    inverse = lax.rsqrt(jnp.mean(centered * centered, axis=-1, keepdims=True) + EPS)
    return centered * inverse, inverse


def norm_back(grad_out, normed, inverse, gain):
    scaled = grad_out * gain
    first = jnp.mean(scaled, axis=-1, keepdims=True)
    second = jnp.mean(scaled * normed, axis=-1, keepdims=True)
    return inverse * (scaled - first - normed * second)


def three_parts(value):
    high = value.astype(BF).astype(F32)
    rest = value - high
    middle = rest.astype(BF).astype(F32)
    return high, middle, rest - middle


def put_parts(value, column, at):
    lane = lax.broadcasted_iota(jnp.int32, value.shape, 1)
    for i, part in enumerate(three_parts(column)):
        value = jnp.where(lane == at + i, -part, value)
    return value


def widen(rows, cols, dtype=BF):
    source = lax.broadcasted_iota(jnp.int32, (rows, cols), 0)
    target = lax.broadcasted_iota(jnp.int32, (rows, cols), 1)
    return ((source // HEAD) * WIDE + source % HEAD == target).astype(dtype)


def glue(kernel, me, inputs, shapes, name, scratch=()):
    def spec(shape):
        return pl.BlockSpec(shape, lambda i, me_ref: (0,) * len(shape))

    return pl.pallas_call(
        kernel,
        grid_spec=pltpu.PrefetchScalarGridSpec(
            num_scalar_prefetch=1,
            grid=(1,),
            in_specs=[spec(a.shape) for a in inputs],
            out_specs=[spec(shape) for shape in shapes],
            scratch_shapes=scratch,
        ),
        out_shape=[jax.ShapeDtypeStruct(shape, BF) for shape in shapes],
        cost_estimate=cost(0, 4 * sum(a.size for a in inputs)),
        compiler_params=pltpu.CompilerParams(vmem_limit_bytes=VMEM_BYTES),
        name=name,
    )(me.reshape(1), *inputs)


def cut_lower(lower, me, count, split):
    blocks, own, total = lower.shape
    group = blocks // count

    def kernel(me_ref, in_ref, *outs):
        for j in range(count):
            start = (me_ref[0] ^ j) * group
            for h in range(group):
                outs[j][h] = in_ref[start + h][:, :split]
        outs[count][...] = jnp.concatenate([in_ref[f][:, split:] for f in range(blocks)], axis=-1)

    shapes = [(group, own, split)] * count + [(own, blocks * (total - split))]
    *down, output = glue(kernel, me, [lower], shapes, "cut_lower")
    return down, output


def build_weights(down, output, me):
    count = len(down)
    group, own, split = down[0].shape
    width = count * own
    hidden_count = group * split

    def kernel(me_ref, *refs):
        down_refs, output_refs = refs[:count], refs[count : 2 * count]
        down_ref, turned_ref, output_ref, held_down, held_output = refs[2 * count :]
        for j in range(count):
            at = me_ref[0] ^ j
            parts = [down_refs[j][h] for h in range(group)]
            held_down[at] = jnp.concatenate(parts, axis=-1)
            held_output[at] = output_refs[j][...]
        turned = held_down[...].reshape(width, hidden_count)
        turned_ref[...] = turned
        down_ref[...] = turned.T
        output_ref[...] = held_output[...].reshape(width, width).T.reshape(count, own, width)

    shapes = [(hidden_count, width), (width, hidden_count), (count, own, width)]
    scratch = [pltpu.VMEM((count, own, hidden_count), BF), pltpu.VMEM((count, own, width), BF)]
    return glue(kernel, me, [*down, *output], shapes, "build_weights", scratch)


def cut_down(grad, me, count, group):
    width, hidden_count = grad.shape
    own, split = width // count, hidden_count // group

    def kernel(me_ref, in_ref, *outs):
        for j in range(count):
            start = pl.multiple_of((me_ref[0] ^ j) * own, own)
            rows = in_ref[pl.ds(start, own), :]
            for h in range(group):
                outs[j][h] = rows[:, h * split : (h + 1) * split]

    return glue(kernel, me, [grad], [(group, own, split)] * count, "cut_down")


def merge_blocks(parts, me):
    count = len(parts)
    group, own, split = parts[0].shape

    def kernel(me_ref, *refs):
        out = refs[count]
        for j in range(count):
            for h in range(group):
                out[(me_ref[0] ^ j) * group + h] = refs[j][h]

    return glue(kernel, me, parts, [(count * group, own, split)], "merge_blocks")[0]


def attend(qkv, wide_heads, chunk, kept):
    images, count, length, _ = qkv.shape
    heads = wide_heads // WIDE
    rows = length // CHUNKS
    keys = count * length
    flat = qkv.reshape(images, keys, 3 * wide_heads)

    def kernel(q_ref, kv_ref, *refs):
        mixed_ref, query_ref, exact_ref, turned = refs[-4:]

        @pl.when(pl.program_id(1) == 0)
        def _():
            for e in range(heads):
                at = wide_heads + e * WIDE
                turned[e] = kv_ref[0, :, at : at + WIDE].T

        total = jnp.zeros((rows, heads * HEAD), F32)
        for e in range(heads):
            here = slice(e * WIDE, (e + 1) * WIDE)
            query = q_ref[0, 0, :, here]
            v = kv_ref[0, :, 2 * wide_heads + e * WIDE : 2 * wide_heads + (e + 1) * WIDE]
            scores = mm(query, turned[e])
            top = jnp.max(scores, axis=-1, keepdims=True)
            weights = jnp.exp2(scores - top).astype(BF)
            mixed = mm(weights, v)
            summed = mixed[:, SUM_AT : SUM_AT + 1]
            mixed = mixed / summed
            log_total = top + jnp.log2(summed)
            exact_ref[0, 0, :, here] = mixed
            query_ref[0, 0, :, here] = put_parts(query.astype(F32), log_total, LSE_AT).astype(BF)
            source = lax.broadcasted_iota(jnp.int32, (WIDE, heads * HEAD), 0)
            target = lax.broadcasted_iota(jnp.int32, (WIDE, heads * HEAD), 1)
            pick = ((source < HEAD) & (source + e * HEAD == target)).astype(F32).astype(BF)
            total = total + mm(mixed.astype(BF), pick)
        mixed_ref[0, 0] = total.T.astype(BF)

    part = pl.BlockSpec((1, 1, rows, wide_heads), lambda i, b: (i, b, chunk, 0))
    shapes = [
        jax.ShapeDtypeStruct((images, count, heads * HEAD, rows), BF),
        jax.ShapeDtypeStruct((images, count, length, wide_heads), BF),
        jax.ShapeDtypeStruct((images, count, length, wide_heads), F32),
    ]
    outs = [pl.BlockSpec((1, 1, heads * HEAD, rows), lambda i, b: (i, b, 0, 0)), part, part]
    extra = list(kept)
    scores = images * count * rows * keys * heads
    return pl.pallas_call(
        kernel,
        grid=(images, count),
        in_specs=[part, pl.BlockSpec((1, keys, 3 * wide_heads), lambda i, b: (i, 0, 0))]
        + [pl.BlockSpec(memory_space=pl.ANY)] * len(extra),
        out_specs=outs,
        out_shape=shapes,
        input_output_aliases={2 + i: 1 + i for i in range(len(extra))},
        scratch_shapes=[pltpu.VMEM((heads, WIDE, keys), BF)],
        cost_estimate=cost(2 * scores * WIDE * 2, flat.size * 2 + 3 * images * keys * wide_heads, scores),
        compiler_params=pltpu.CompilerParams(vmem_limit_bytes=VMEM_BYTES),
        name="attend",
    )(qkv, flat, *extra)


def middle(mixed, tokens, cotangent, weights, chunk, kept):
    images, count, length, width = tokens.shape
    me, w_output, w_up, up_turned, w_down, down_turned, b_output, gain, shift, b_up = weights
    rows = length // CHUNKS
    own = mixed[0].shape[-2]
    hidden_count = w_up.shape[1]

    def kernel(me_ref, *refs):
        mixed_refs = refs[:count]
        (
            tok_ref,
            cot_ref,
            wo_ref,
            up_ref,
            up_turned_ref,
            down_ref,
            down_turned_ref,
            bo_ref,
            g_ref,
            s_ref,
            bu_ref,
        ) = refs[count : count + 11]
        outs = refs[-(6 + 2 * count) :]
        h_ref, z_ref, du_ref, cat_ref, x_ref, gb_ref = outs[:6]
        dh_refs, y_refs = outs[6 : 6 + count], outs[6 + count :]
        block = pl.program_id(1)
        x_one = tok_ref[0, 0].astype(F32) + bo_ref[...]
        pieces = []
        for i in range(count):
            piece = mixed_refs[i][0, 0].T
            pieces.append(piece)
            x_one = x_one + mm(piece, wo_ref[me_ref[0] ^ i])
        cat_ref[0, 0] = jnp.concatenate(pieces, axis=-1)

        @pl.when(block == 0)
        def _():
            x_ref[0] = x_one

        normed, _ = norm_parts(x_one)
        h_two = (normed * g_ref[...] + s_ref[...]).astype(BF)
        h_ref[0, 0] = h_two
        hidden = mm(h_two, up_ref[...]) + bu_ref[...]
        grad_act = mm(cot_ref[0, 0], down_turned_ref[...])
        square = hidden * hidden
        inner = jnp.tanh(ROOT * (hidden + CUBIC * square * hidden))
        half = 0.5 * (1.0 + inner)
        z = (hidden * half).astype(BF)
        slope = half + 0.5 * hidden * (1.0 - inner * inner) * ROOT * (1.0 + 3.0 * CUBIC * square)
        wide_grad = grad_act * slope
        grad_hidden = wide_grad.astype(BF)
        z_ref[0, 0] = z
        du_ref[0, 0] = grad_hidden
        dh = mm(grad_hidden, up_turned_ref[...]).astype(BF)
        y = mm(z, down_ref[...]).astype(BF)
        for j in range(count):

            @pl.when(block == j)
            def _():
                dh_refs[j][0] = dh
                y_refs[j][0] = y

        summed = jnp.sum(grad_hidden.astype(F32), axis=0, keepdims=True)
        first = (pl.program_id(0) == 0) & (block == 0)

        @pl.when(first)
        def _():
            gb_ref[...] = summed

        @pl.when(jnp.logical_not(first))
        def _():
            gb_ref[...] += summed

    def piece_spec(i):
        return pl.BlockSpec((1, 1, own, rows), lambda im, b, me_ref: (im, b ^ i, 0, 0))

    def whole_spec(array):
        return pl.BlockSpec(array.shape, lambda im, b, me_ref: (0,) * array.ndim)

    full = pl.BlockSpec((1, 1, rows, width), lambda im, b, me_ref: (im, b, chunk, 0))
    full_hidden = pl.BlockSpec((1, 1, rows, hidden_count), lambda im, b, me_ref: (im, b, chunk, 0))
    part = pl.BlockSpec((1, rows, width), lambda im, b, me_ref: (im, 0, 0))
    constants = [w_output, w_up, up_turned, w_down, down_turned, b_output, gain, shift, b_up]
    extra = list(kept)
    inputs = [*mixed, tokens, cotangent, *constants, *extra]
    all_rows = images * count * rows
    return pl.pallas_call(
        kernel,
        grid_spec=pltpu.PrefetchScalarGridSpec(
            num_scalar_prefetch=1,
            grid=(images, count),
            in_specs=[piece_spec(i) for i in range(count)]
            + [full, full]
            + [whole_spec(array) for array in constants]
            + [pl.BlockSpec(memory_space=pl.ANY)] * len(extra),
            out_specs=[
                full,
                full_hidden,
                full_hidden,
                full,
                part,
                pl.BlockSpec((1, hidden_count), lambda im, b, me_ref: (0, 0)),
            ]
            + [part] * (2 * count),
        ),
        out_shape=[
            jax.ShapeDtypeStruct(tokens.shape, BF),
            jax.ShapeDtypeStruct((images, count, length, hidden_count), BF),
            jax.ShapeDtypeStruct((images, count, length, hidden_count), BF),
            jax.ShapeDtypeStruct(tokens.shape, BF),
            jax.ShapeDtypeStruct((images, rows, width), F32),
            jax.ShapeDtypeStruct((1, hidden_count), F32),
        ]
        + [jax.ShapeDtypeStruct((images, rows, width), BF)] * (2 * count),
        input_output_aliases={1 + count + 11 + i: i for i in range(len(extra))},
        cost_estimate=cost(
            all_rows * width * (width + 4 * hidden_count) * 2,
            all_rows * (width * 16 + hidden_count * 4) + (w_output.size + 2 * w_up.size) * 2,
        ),
        compiler_params=pltpu.CompilerParams(vmem_limit_bytes=VMEM_BYTES),
        name="middle",
    )(me.reshape(1), *inputs)


def mixed_back(grad, w_wide, exact, chunk, kept):
    images, count, rows, width = grad.shape
    _, _, length, wide_heads = exact.shape
    heads = wide_heads // WIDE

    def kernel(grad_ref, w_ref, exact_ref, *refs):
        out_ref = refs[-1]
        result = mm(grad_ref[0, 0], w_ref[...]).astype(BF).astype(F32)
        for e in range(heads):
            here = slice(e * WIDE, (e + 1) * WIDE)
            mine = result[:, here]
            exact = exact_ref[0, 0, :, here]
            delta = jnp.sum(mine * exact, axis=-1, keepdims=True)
            value = put_parts(mine, delta, SUM_AT).astype(BF)
            out_ref[0, 0, :, here] = value

    full = pl.BlockSpec((1, 1, rows, wide_heads), lambda im, b: (im, b, chunk, 0))
    extra = list(kept)
    return pl.pallas_call(
        kernel,
        grid=(images, count),
        in_specs=[
            pl.BlockSpec((1, 1, rows, width), lambda im, b: (im, b, 0, 0)),
            pl.BlockSpec(w_wide.shape, lambda im, b: (0, 0)),
            full,
        ]
        + [pl.BlockSpec(memory_space=pl.ANY)] * len(extra),
        out_specs=full,
        out_shape=jax.ShapeDtypeStruct(exact.shape, BF),
        input_output_aliases={3 + i: i for i in range(len(extra))},
        cost_estimate=cost(
            images * count * rows * width * wide_heads,
            images * count * rows * (width * 2 + wide_heads * 6) + w_wide.size * 2,
        ),
        compiler_params=pltpu.CompilerParams(vmem_limit_bytes=VMEM_BYTES),
        name="mixed_back",
    )(grad, w_wide, exact, *extra)


def attend_back(query, grad, qkv, first, heads):
    images, keys, wide_heads = query.shape
    every = wide_heads // WIDE
    rows = min(512, keys)
    span = min(512, keys)
    steps = keys // rows

    def kernel(q_ref, do_ref, k_ref, v_ref, dq_ref, dk_ref, dv_ref, kt, dk, dv):
        step = pl.program_id(2)

        @pl.when(step == 0)
        def _():
            kt[...] = k_ref[0].T
            dk[...] = jnp.zeros_like(dk)
            dv[...] = jnp.zeros_like(dv)

        q = q_ref[0]
        do = do_ref[0]
        turned = jnp.zeros((WIDE, rows), F32)
        for at in range(0, keys, span):
            here = slice(at, at + span)
            probs = jnp.exp2(mm(k_ref[0, here], q, NT))
            grad_scores = (probs * mm(v_ref[0, here], do, NT)).astype(BF)
            dv[here] += mm(probs.astype(BF), do)
            dk[here] += mm(grad_scores, q)
            turned = turned + mm(kt[:, here], grad_scores)
        dq_ref[0] = (turned.T * SCALE).astype(BF)

        @pl.when(step == steps - 1)
        def _():
            dk_ref[0] = (dk[...] * (1.0 / LOG2E)).astype(BF)
            dv_ref[0] = dv[...].astype(BF)

    row_in = pl.BlockSpec((1, rows, WIDE), lambda i, e, b: (i, b, e + first))
    row_out = pl.BlockSpec((1, rows, WIDE), lambda i, e, b: (i, b, e))

    def all_spec(shift):
        return pl.BlockSpec((1, keys, WIDE), lambda i, e, b: (i, 0, e + shift))

    shape = jax.ShapeDtypeStruct((images, keys, heads * WIDE), BF)
    scores = images * heads * keys * keys
    return pl.pallas_call(
        kernel,
        grid=(images, heads, steps),
        in_specs=[row_in, row_in, all_spec(every + first), all_spec(2 * every + first)],
        out_specs=[row_out, all_spec(0), all_spec(0)],
        out_shape=[shape] * 3,
        scratch_shapes=[
            pltpu.VMEM((WIDE, keys), BF),
            pltpu.VMEM((keys, WIDE), F32),
            pltpu.VMEM((keys, WIDE), F32),
        ],
        cost_estimate=cost(5 * scores * WIDE * 2, 7 * images * keys * wide_heads * 2, scores),
        compiler_params=pltpu.CompilerParams(vmem_limit_bytes=VMEM_BYTES),
        name="attend_back",
    )(query, grad, qkv, qkv)


def project_back(grads, tokens, w_turned, gain, shift, narrow):
    images, count, length, width = tokens.shape
    parts = len(grads[0])
    part = grads[0][0].shape[-1]
    wide = parts * part
    own = narrow.shape[1]
    flat = [piece for kind in grads for piece in kind]
    last_image, last_block = images - 1, count - 1

    def kernel(*refs):
        ins = refs[: len(flat)]
        tok_ref, w_ref, g_ref, s_ref, n_ref = refs[len(flat) : len(flat) + 5]
        outs = refs[len(flat) + 5 : -1]
        held = refs[-1]
        dh_refs = outs[:count]
        weight_ref, norm_ref, bias_ref = outs[count:]
        block = pl.program_id(1)
        first = (pl.program_id(0) == 0) & (block == 0)

        @pl.when(first)
        def _():
            held[...] = jnp.zeros_like(held)
            norm_ref[...] = jnp.zeros_like(norm_ref)
            bias_ref[...] = jnp.zeros_like(bias_ref)

        normed, _ = norm_parts(tok_ref[0, 0].astype(F32))
        turned = (normed * g_ref[...] + s_ref[...]).astype(BF).T
        total = jnp.zeros((length, width), F32)
        for i, ref in enumerate(ins):
            piece = ref[0, 0]
            here = slice(i * part, (i + 1) * part)
            total = total + mm(piece, w_ref[here])
            held[:, here] += mm(turned, piece)
            bias_ref[:, here] += jnp.sum(piece.astype(F32), axis=0, keepdims=True)
        for j in range(count):

            @pl.when(block == j)
            def _():
                dh_refs[j][0] = total.astype(BF)

        norm_ref[0:1] += jnp.sum(total * normed, axis=0, keepdims=True)
        norm_ref[1:2] += jnp.sum(total, axis=0, keepdims=True)

        @pl.when((pl.program_id(0) == last_image) & (block == last_block))
        def _():
            for kind in range(3):
                whole = held[:, kind * wide : (kind + 1) * wide].astype(BF)
                weight_ref[kind] = mm(whole, n_ref[...]).astype(BF)

    piece_spec = pl.BlockSpec((1, 1, length, part), lambda im, b: (im, b, 0, 0))
    row_spec = pl.BlockSpec((1, 1, length, width), lambda im, b: (im, b, 0, 0))

    def whole_spec(shape):
        return pl.BlockSpec(shape, lambda im, b: (0,) * len(shape))

    shapes = [(3, width, own), (2, width), (1, 3 * wide)]
    kinds = [BF, F32, F32]
    all_rows = images * count * length
    return pl.pallas_call(
        kernel,
        grid=(images, count),
        in_specs=[piece_spec] * len(flat)
        + [row_spec]
        + [whole_spec(a.shape) for a in (w_turned, gain, shift, narrow)],
        out_specs=[pl.BlockSpec((1, length, width), lambda im, b: (im, 0, 0))] * count
        + [whole_spec(shape) for shape in shapes],
        out_shape=[jax.ShapeDtypeStruct((images, length, width), BF)] * count
        + [jax.ShapeDtypeStruct(shape, kind) for shape, kind in zip(shapes, kinds)],
        scratch_shapes=[pltpu.VMEM((width, 3 * wide), F32)],
        cost_estimate=cost(
            2 * all_rows * width * wide * 3,
            all_rows * (wide * 6 + width * 4) + w_turned.size * 2,
        ),
        compiler_params=pltpu.CompilerParams(vmem_limit_bytes=VMEM_BYTES),
        name="project_back",
    )(*flat, tokens, w_turned, gain, shift, narrow)


def local(
    tokens,
    patch_mask,
    gain_one,
    shift_one,
    w_query,
    b_query,
    w_key,
    w_value,
    b_value,
    w_output,
    b_output,
    gain_two,
    shift_two,
    w_up,
    b_up,
    w_down,
    b_down,
    cotangent,
):
    me = lax.axis_index("seq")
    count = lax.axis_size("seq")
    fcount = lax.axis_size("fsdp")
    images, length, width = tokens.shape
    own = w_query.shape[1]
    heads = own // HEAD
    wide_heads = heads * WIDE
    group = fcount // count
    rows = length // CHUNKS

    qkv_shard = jnp.concatenate([w_query, w_key, w_value], axis=1)
    small = jnp.concatenate(
        [patch_mask.astype(BF).reshape(-1)]
        + [gain_one, shift_one, b_output, gain_two, shift_two, b_down]
    )
    small = spread(small)
    qkv_blocks, qkv_index = ring_gather(qkv_shard, 0)
    tok_blocks, cot_blocks = None, None
    fast = images == 1 and count == 4
    if fast:
        near, across = swap(tokens, 1), swap(tokens, 2)
        across, cot_sent = together(across, cotangent)
        cot_across = swap(cot_sent, 2)
        across, cot_sent, qkv_blocks = together(across, cot_sent, qkv_blocks)
        tok_blocks = [tokens, near, across, swap(across, 1)]
    w_wide = place_wide(qkv_blocks, qkv_index, widen(3 * own, 3 * wide_heads))
    split = w_down.shape[0]
    lower = jnp.concatenate([w_down.T, w_output.T], axis=1)
    lower = lax.all_gather(lower, "fsdp", axis=0)
    if fast:
        down_sent, output_cols = cut_lower(lower, me, count, split)
    else:
        output_cols = lower[:, :, split:].transpose(1, 0, 2).reshape(own, width)
        down_sent = [
            lax.dynamic_slice_in_dim(lower[:, :, :split], (me ^ j) * group, group, 0)
            for j in range(count)
        ]
    up_mat = lax.all_gather(w_up, "fsdp", axis=0, tiled=True)

    patches = images * length
    valid = jnp.stack([block[:patches].reshape(images, length) for block in small], axis=1)
    bias_mask = jnp.where(valid > 0, 0.0, NEG).astype(F32)
    vectors = reorder([block[patches:].reshape(6, own) for block in small], me)
    vectors = jnp.concatenate(vectors, axis=1).astype(F32)
    g_one, s_one, b_out, g_two, s_two, b_dn = [vectors[i : i + 1] for i in range(6)]

    expand = widen(own, wide_heads)
    lane = np.arange(3 * wide_heads) % WIDE
    kind = np.arange(3 * wide_heads) // wide_heads
    factor = np.where(kind == 0, SCALE * LOG2E, 1.0).astype(np.float32)
    ones = (kind == 0) & (lane == MASK_AT)
    ones |= (kind == 1) & (lane >= LSE_AT) & (lane < LSE_AT + 3)
    ones |= (kind == 2) & (lane >= SUM_AT) & (lane < SUM_AT + 3)
    at_mask = ((kind == 1) & (lane == MASK_AT)).astype(np.float32)

    def widen_vector(vector):
        shaped = vector.astype(F32).reshape(heads, HEAD)
        return jnp.pad(shaped, ((0, 0), (0, WIDE - HEAD))).reshape(-1)

    def narrow(vector):
        return vector.reshape(heads, WIDE)[:, :HEAD].reshape(-1)

    bias_wide = jnp.concatenate(
        [widen_vector(b_query), jnp.zeros((wide_heads,), F32), widen_vector(b_value)]
    )
    bias_wide = bias_wide * factor + ones.astype(np.float32)

    single = images == 1
    down_exchanged = [down_sent[0]] + [swap(down_sent[j], j) for j in range(1, count)]
    cot_begun = (cot_sent, None, cot_across) if fast else None
    w_turned = w_wide.T

    def scatter_up(up_grad):
        blocks = up_grad.astype(BF).reshape(fcount, width // fcount, -1)
        return lax.psum_scatter(blocks, "fsdp", scatter_dimension=0)

    def send_down(down_grad):
        if fast:
            sent = cut_down(down_grad, me, count, group)
            return [sent[0]] + [swap(sent[j], j) for j in range(1, count)]
        shaped = down_grad.astype(BF).reshape(width, group, -1).transpose(1, 0, 2)

        def cols(j):
            return lax.dynamic_slice_in_dim(shaped, (me ^ j) * own, own, 1)

        return [cols(0)] + [swap(cols(j), j) for j in range(1, count)]

    def merge_down(got):
        if fast:
            return merge_blocks(got, me)
        return jnp.concatenate(reorder(got, me), axis=0)

    def run(tokens, bias_mask, cotangent, tok_blocks=None):
        images = tokens.shape[0]
        if tok_blocks is None:
            tok_blocks = spread(tokens)
        tok_all = jnp.stack(tok_blocks, axis=1)
        normed, _ = norm_parts(tok_all.astype(F32))
        h_one = (normed * g_one + s_one).astype(BF)
        product = jnp.einsum("ijld,de->ijle", h_one, w_wide, preferred_element_type=F32)
        qkv = (product * factor + bias_wide + bias_mask[..., None] * at_mask).astype(BF)
        if fast:
            qkv, cot_across, down_parts, turned = together(
                qkv, cot_begun[2], down_exchanged, w_turned
            )
            cot_blocks = [cotangent, swap(cot_begun[0], 1), cot_across, swap(cot_across, 1)]
        else:
            cot_blocks = spread(cotangent)
            down_parts, turned = down_exchanged, w_turned
        output_parts = spread(output_cols)
        up_turned = up_mat.T
        cot_all = jnp.stack(cot_blocks, axis=1)

        kept_attend, kept_middle = (), ()
        mixed_chunks = []
        for c in range(CHUNKS):
            mixed, *kept_attend = attend(qkv, wide_heads, c, kept_attend)
            mixed_chunks.append(spread(mixed))
        query_wide, mixed_exact = kept_attend
        mixed_exact, down_in, output_in = together(mixed_exact, down_parts, output_parts)
        if fast:
            down_mat, down_turned, output_mat = build_weights(down_in, output_in, me)
        else:
            down_turned = jnp.stack(reorder(down_in, me)).transpose(0, 2, 1, 3)
            down_turned = down_turned.reshape(width, -1)
            down_mat = down_turned.T
            output_mat = jnp.concatenate(reorder(output_in, me), axis=0).T
            output_mat = output_mat.reshape(count, own, width)
        own_rows = lax.dynamic_index_in_dim(output_mat, me, 0, keepdims=False)
        output_wide = mm(own_rows.T, expand).astype(BF)
        weights = (
            me,
            output_mat,
            up_mat,
            up_turned,
            down_mat,
            down_turned,
            b_out,
            g_two,
            s_two,
            b_up.astype(F32)[None],
        )
        def grad_rows(c, hidden_grad, x_own):
            grad_norm = hidden_grad.astype(F32)
            normed_two, inverse_two = norm_parts(x_own)
            cot_own = cotangent[:, c * rows : (c + 1) * rows].astype(F32)
            residual = cot_own + norm_back(grad_norm, normed_two, inverse_two, g_two)
            grad_attn = residual.astype(BF)
            sums = jnp.stack(
                [
                    jnp.sum(grad_norm * normed_two, axis=(0, 1)),
                    jnp.sum(grad_norm, axis=(0, 1)),
                    jnp.sum(grad_attn.astype(F32), axis=(0, 1)),
                    jnp.sum(cot_own, axis=(0, 1)),
                ]
            )
            return residual, grad_attn, sums

        out_parts, x_parts = [], []
        grad_attn_all, grad_residual = [], []
        hidden_parts = []
        early, up_bias_grad = 0.0, 0.0
        for c in range(CHUNKS):
            result = middle(mixed_chunks[c], tok_all, cot_all, weights, c, kept_middle)
            kept_middle, x_own, gb = result[:4], result[4], result[5]
            hidden_parts.append(list(result[6 : 6 + count]))
            out_parts.append(result[6 + count :])
            x_parts.append(x_own)
            up_bias_grad = up_bias_grad + gb[0]
        h_two, activated, grad_hidden, mixed_all = kept_middle
        blocks = hidden_parts[0]
        if count == 4:
            near_sum, crossing = collect_pair(blocks)
            h_two, crossing = together(h_two, crossing)
            incoming = swap(crossing, 2)
        else:
            near_sum, incoming = collect(blocks), jnp.zeros((), F32)
        up_grad = jnp.einsum(
            "ijld,ijlf->df",
            h_two,
            grad_hidden,
            preferred_element_type=F32,
        ).astype(BF if single else F32)
        incoming, up_grad = together(incoming, up_grad)
        if single:
            up_grad = scatter_up(up_grad)
        hidden_grad = near_sum + incoming.astype(F32)
        residual, grad_attn, early = grad_rows(0, hidden_grad, x_parts[0])
        grad_attn, activated = together(grad_attn, activated)
        down_grad = jnp.einsum(
            "ijld,ijlf->df",
            cot_all,
            activated,
            preferred_element_type=F32,
        ).astype(BF if single else F32)
        grad_residual.append(residual)
        if fast:
            across = swap(grad_attn, 2)
            near = swap(grad_attn, 1)
            across, down_grad = together(across, down_grad)
            attn_blocks = [grad_attn, near, across, swap(across, 1)]
        else:
            attn_blocks = spread(grad_attn)
        grad_attn_all = jnp.stack(attn_blocks, axis=1)
        grad_mixed = mixed_back(grad_attn_all, output_wide, mixed_exact, 0, ())

        wide_shape = (images, count * length, wide_heads)
        query_in = query_wide.reshape(wide_shape)
        grad_in = grad_mixed.reshape(wide_shape)
        flat_qkv = qkv.reshape(images, count * length, 3 * wide_heads)
        halves = 2 if heads % 2 == 0 else 1
        step = heads // halves
        grad_in, out_blocks, down_grad = together(grad_in, list(out_parts[0]), down_grad)
        if single:
            down_grad = send_down(down_grad)
            grad_in, up_grad = together(grad_in, up_grad)
        if count == 4:
            out_sum, out_across = collect_pair(out_blocks)
            grad_in, out_across = together(grad_in, out_across)
            out_incoming = swap(out_across, 2)
        else:
            out_sum, out_incoming = collect(out_blocks), jnp.zeros((), F32)
        first = attend_back(query_in, grad_in, flat_qkv, 0, step)
        pieces = [first]
        if halves == 2:
            first, down_grad = together(first, down_grad)
            if single:
                down_grad = merge_down(down_grad)
            query_in, down_grad = together(query_in, down_grad)
            pieces = [first, attend_back(query_in, grad_in, flat_qkv, step, step)]
            pieces, out_incoming = together(pieces, out_incoming)
        elif single:
            down_grad = merge_down(down_grad)
        out_sum = out_sum + out_incoming.astype(F32)
        grads = [
            [piece[k].reshape(images, count, length, -1) for piece in pieces] for k in range(3)
        ]
        grad_attn_cols = lax.dynamic_slice_in_dim(grad_attn_all, me * own, own, 3)
        output_grad = jnp.einsum(
            "ijle,ijld->ed", mixed_all, grad_attn_cols, preferred_element_type=F32
        )
        result = project_back(grads, tok_all, turned, g_one, s_one, expand.T)
        qkv_grad, late, bias_grads = result[count:]
        grad_norm_one = collect(list(result[:count])).astype(F32)

        layer_out = (jnp.concatenate(x_parts, axis=1) + out_sum.astype(F32) + b_dn).astype(BF)
        normed_one, inverse_one = norm_parts(tokens.astype(F32))
        grad_tokens = (
            jnp.concatenate(grad_residual, axis=1)
            + norm_back(grad_norm_one, normed_one, inverse_one, g_one)
        ).astype(BF)
        qkv_grad = qkv_grad if single else qkv_grad.astype(F32)
        sums = (down_grad, up_grad, output_grad, qkv_grad, early, up_bias_grad, late, bias_grads)
        return sums, (layer_out, grad_tokens)

    if images == 1:
        sums, (layer_out, grad_tokens) = run(tokens, bias_mask, cotangent, tok_blocks)
    else:
        items = (tokens[:, None], bias_mask[:, None], cotangent[:, None])
        shapes = jax.eval_shape(lambda item: run(*item)[0], jax.tree.map(lambda a: a[0], items))
        empty = jax.tree.map(lambda a: jnp.zeros(a.shape, a.dtype), shapes)

        def step(totals, item):
            sums, results = run(*item)
            return jax.tree.map(jnp.add, totals, sums), results

        sums, (layer_out, grad_tokens) = lax.scan(step, empty, items)
        layer_out, grad_tokens = layer_out[:, 0], grad_tokens[:, 0]
    down_grad, up_grad, output_grad, qkv_grad, early, up_bias_grad, late, bias_grads = sums

    down_pieces = down_grad if single else merge_down(send_down(down_grad))
    final_up = (up_grad if single else scatter_up(up_grad)).astype(F32)
    final_down = lax.psum_scatter(down_pieces, "fsdp", scatter_dimension=0)
    output_grad = reorder(jnp.split(output_grad.astype(BF), count, axis=0), me)
    output_grad = jnp.concatenate(output_grad, axis=0)
    qkv_grad = qkv_grad.astype(BF).reshape(3, fcount, width // fcount, own)
    output_grad = output_grad.reshape(fcount, width // fcount, own)

    def four_parts(f):
        parts = lax.dynamic_index_in_dim(qkv_grad, f, 1, keepdims=False)
        last = lax.dynamic_index_in_dim(output_grad, f, 0, keepdims=True)
        return jnp.concatenate([parts, last], axis=0)


    def to_owner(stack):
        kinds = stack.shape[0]
        parts = jnp.split(stack.reshape(kinds, count, own), count, axis=1)
        parts = reorder([part[:, 0] for part in parts], me)
        total = parts[0]
        for j in range(1, count):
            total = total + swap(parts[j], j)
        return jnp.concatenate(
            [total.reshape(-1)] + [narrow(g) for g in bias_grads] + [up_bias_grad]
        )

    bias_grads = [bias_grads[0, i * wide_heads : (i + 1) * wide_heads] for i in (0, 2)]
    four, final_down, vectors = ring_reduce(
        four_parts,
        0,
        final_down,
        jnp.concatenate([early, late], axis=0),
        [to_owner] + sum_steps(),
    )
    final_down = final_down.astype(F32).T
    (
        gain_two_grad,
        shift_two_grad,
        b_output_grad,
        b_down_grad,
        gain_one_grad,
        shift_one_grad,
        b_query_grad,
        b_value_grad,
    ) = [vectors[i * own : (i + 1) * own] for i in range(8)]
    b_up_grad = vectors[8 * own :]
    final_query, final_key, final_value, final_output = [four[i] for i in range(4)]
    return (
        layer_out,
        grad_tokens,
        gain_one_grad,
        shift_one_grad,
        final_query,
        b_query_grad,
        final_key,
        final_value,
        b_value_grad,
        final_output,
        b_output_grad,
        gain_two_grad,
        shift_two_grad,
        final_up,
        b_up_grad,
        final_down,
        b_down_grad,
    )


def solution(mesh):
    rows = P("fsdp", "seq", None)
    matrix = P("fsdp", "seq")
    vector = P("seq")
    return jax.shard_map(
        local,
        mesh=mesh,
        in_specs=(
            rows,
            matrix,
            vector,
            vector,
            matrix,
            vector,
            matrix,
            matrix,
            vector,
            matrix,
            vector,
            vector,
            vector,
            matrix,
            vector,
            matrix,
            vector,
            rows,
        ),
        out_specs=(
            rows,
            rows,
            vector,
            vector,
            matrix,
            vector,
            matrix,
            matrix,
            vector,
            matrix,
            vector,
            vector,
            vector,
            matrix,
            vector,
            matrix,
            vector,
        ),
        check_vma=False,
    )
```

```python
import functools
import math

import jax
import jax.numpy as jnp
import numpy as np
from jax import lax
from jax.experimental import pallas as pl
from jax.experimental.pallas import tpu as pltpu
from jax.sharding import PartitionSpec as P

HEAD = 72
WIDE = 128
MASK_AT = HEAD
LSE_AT = HEAD + 1
SUM_AT = HEAD
CHUNKS = 1
BESIDE_AT = 3

EPS = 1e-06
ROOT = 0.7978845608028654
CUBIC = 0.044715
NEG = -1e30
LOG2E = math.log2(math.e)
SCALE = HEAD ** (-0.5)

BF = jnp.bfloat16
F32 = jnp.float32
NT = (((1,), (1,)), ((), ()))
NN = (((1,), (0,)), ((), ()))
VMEM_BYTES = 56 << 20


def mm(left, right, dims=NN):
    return lax.dot_general(left, right, dims, preferred_element_type=F32)


def cost(macs, moved, special=0):
    return pl.CostEstimate(flops=macs // 64, bytes_accessed=moved // 64, transcendentals=special // 64)


def swap(value, bit):
    count = lax.axis_size("seq")
    return lax.ppermute(value, "seq", [(i, i ^ bit) for i in range(count)])


def spread(value):
    count = lax.axis_size("seq")
    blocks = [None] * count
    blocks[0] = value
    have = [0]
    bit = count // 2
    while bit:
        for j in list(have):
            blocks[j | bit] = swap(blocks[j], bit)
            have.append(j | bit)
        bit //= 2
    return blocks


def collect(blocks):
    blocks = list(blocks)
    kind = blocks[0].dtype
    count = len(blocks)
    alive = list(range(count))
    bit = 1
    while bit < count:
        for j in reversed(alive):
            if j & bit:
                incoming = swap(blocks[j].astype(kind), bit)
                blocks[j ^ bit] = blocks[j ^ bit].astype(F32) + incoming.astype(F32)
        alive = [j for j in alive if not j & bit]
        bit *= 2
    return blocks[0]


def together(*values):
    return lax.optimization_barrier(values)


def collect_pair(blocks):
    own, near, across, far = blocks
    far = swap(far, 1)
    near = swap(near, 1)
    across = (across.astype(F32) + far.astype(F32)).astype(BF)
    return own.astype(F32) + near.astype(F32), across


def reorder(blocks, me):
    blocks = list(blocks)
    bit = 1
    while bit < len(blocks):
        odd = (me & bit) > 0
        blocks = [jnp.where(odd, blocks[j ^ bit], blocks[j]) for j in range(len(blocks))]
        bit *= 2
    return blocks


def ring_order():
    count = lax.axis_size("fsdp")
    if count == 8:
        return [0, 2, 4, 6, 7, 5, 3, 1]
    return list(range(count))


def ring_place():
    device = lax.axis_index("fsdp")
    if lax.axis_size("fsdp") == 8:
        return jnp.where(device % 2 == 0, device // 2, (15 - device) // 2)
    return device


def ring_shift(value, step):
    order = ring_order()
    count = len(order)
    return lax.ppermute(
        value, "fsdp", [(order[i], order[(i + step) % count]) for i in range(count)]
    )


def ring_owner(offset):
    count = lax.axis_size("fsdp")
    at = lax.rem(ring_place() + (offset + count), count)
    if count == 8:
        return jnp.where(at < 4, 2 * at, 15 - 2 * at)
    return at


def ring_gather(value, flip):
    count = lax.axis_size("fsdp")
    found = [(0, value)]
    far = (count // 2, count - 1 - count // 2)
    moving = [value, value]
    for k in range(1, count // 2 + 1):
        for way, step in ((0, 1), (1, -1)):
            if k <= far[way ^ flip]:
                moving[way] = ring_shift(moving[way], step)
                found.append((-step * k, moving[way]))
        moving = list(lax.optimization_barrier(tuple(moving)))
    index = jnp.stack([ring_owner(offset) for offset, _ in found])
    return [block for _, block in found], index


def place_wide(blocks, index, wide):
    count = len(blocks)
    rows, cols = blocks[0].shape
    merged = rows % 16 == 0

    def kernel(index_ref, *refs):
        wide_ref, out_ref, held = refs[count:]
        for i in range(count):
            held[index_ref[i]] = refs[i][...]
        if merged:
            out_ref[...] = mm(held[...].reshape(count * rows, cols), wide_ref[...]).astype(BF)
        else:
            for i in range(count):
                out_ref[i] = mm(held[i], wide_ref[...]).astype(BF)

    shape = (count * rows, wide.shape[1]) if merged else (count, rows, wide.shape[1])
    out = pl.pallas_call(
        kernel,
        grid_spec=pltpu.PrefetchScalarGridSpec(
            num_scalar_prefetch=1,
            grid=(1,),
            in_specs=[pl.BlockSpec(a.shape, lambda i, index: (0, 0)) for a in [*blocks, wide]],
            out_specs=pl.BlockSpec(shape, lambda i, index: (0,) * len(shape)),
            scratch_shapes=[pltpu.VMEM((count, rows, cols), BF)],
        ),
        out_shape=jax.ShapeDtypeStruct(shape, BF),
        cost_estimate=cost(count * rows * cols * wide.shape[1], 4 * count * rows * cols),
        compiler_params=pltpu.CompilerParams(vmem_limit_bytes=VMEM_BYTES),
        name="place_wide",
    )(index, *blocks, wide)
    return out.reshape(count * rows, wide.shape[1])


def ring_reduce(take, flip, beside, side, side_steps):
    side_steps = list(side_steps)
    count = lax.axis_size("fsdp")
    far = (count // 2, count - 1 - count // 2)
    total = take(ring_owner(0)).astype(F32)
    incoming = [None, None]
    for k in range(count // 2, 0, -1):
        for way, step in ((0, 1), (1, -1)):
            if k <= far[way ^ flip]:
                part = take(ring_owner(step * k))
                if incoming[way] is not None:
                    part = (part.astype(F32) + incoming[way].astype(F32)).astype(BF)
                incoming[way] = ring_shift(part, step)
        if side_steps:
            side = side_steps.pop(0)(side)
        if incoming[1] is not None and incoming[0] is not None:
            incoming, side = together(incoming, side)
        if k == BESIDE_AT:
            incoming, beside = together(incoming, beside)
    return total + incoming[0].astype(F32) + incoming[1].astype(F32), beside, side


def sum_steps():
    count = lax.axis_size("fsdp")

    def step(bit, value):
        return value + lax.ppermute(value, "fsdp", [(i, i ^ bit) for i in range(count)])

    bits = [1 << i for i in range(count.bit_length() - 1)]
    return [functools.partial(step, bit) for bit in bits]


def norm_parts(value):
    mean = jnp.mean(value, axis=-1, keepdims=True)
    centered = value - mean
    inverse = lax.rsqrt(jnp.mean(centered * centered, axis=-1, keepdims=True) + EPS)
    return centered * inverse, inverse


def norm_back(grad_out, normed, inverse, gain):
    scaled = grad_out * gain
    first = jnp.mean(scaled, axis=-1, keepdims=True)
    second = jnp.mean(scaled * normed, axis=-1, keepdims=True)
    return inverse * (scaled - first - normed * second)


def three_parts(value):
    high = value.astype(BF).astype(F32)
    rest = value - high
    middle = rest.astype(BF).astype(F32)
    return high, middle, rest - middle


def put_parts(value, column, at):
    lane = lax.broadcasted_iota(jnp.int32, value.shape, 1)
    for i, part in enumerate(three_parts(column)):
        value = jnp.where(lane == at + i, -part, value)
    return value


def widen(rows, cols, dtype=BF):
    source = lax.broadcasted_iota(jnp.int32, (rows, cols), 0)
    target = lax.broadcasted_iota(jnp.int32, (rows, cols), 1)
    return ((source // HEAD) * WIDE + source % HEAD == target).astype(dtype)


def glue(kernel, me, inputs, shapes, name, scratch=()):
    def spec(shape):
        return pl.BlockSpec(shape, lambda i, me_ref: (0,) * len(shape))

    return pl.pallas_call(
        kernel,
        grid_spec=pltpu.PrefetchScalarGridSpec(
            num_scalar_prefetch=1,
            grid=(1,),
            in_specs=[spec(a.shape) for a in inputs],
            out_specs=[spec(shape) for shape in shapes],
            scratch_shapes=scratch,
        ),
        out_shape=[jax.ShapeDtypeStruct(shape, BF) for shape in shapes],
        cost_estimate=cost(0, 4 * sum(a.size for a in inputs)),
        compiler_params=pltpu.CompilerParams(vmem_limit_bytes=VMEM_BYTES),
        name=name,
    )(me.reshape(1), *inputs)


def cut_lower(lower, me, count, split):
    blocks, own, total = lower.shape
    group = blocks // count

    def kernel(me_ref, in_ref, *outs):
        for j in range(count):
            start = (me_ref[0] ^ j) * group
            for h in range(group):
                outs[j][h] = in_ref[start + h][:, :split]
        outs[count][...] = jnp.concatenate([in_ref[f][:, split:] for f in range(blocks)], axis=-1)

    shapes = [(group, own, split)] * count + [(own, blocks * (total - split))]
    *down, output = glue(kernel, me, [lower], shapes, "cut_lower")
    return down, output


def build_weights(down, output, me):
    count = len(down)
    group, own, split = down[0].shape
    width = count * own
    hidden_count = group * split

    def kernel(me_ref, *refs):
        down_refs, output_refs = refs[:count], refs[count : 2 * count]
        down_ref, turned_ref, output_ref, held_down, held_output = refs[2 * count :]
        for j in range(count):
            at = me_ref[0] ^ j
            parts = [down_refs[j][h] for h in range(group)]
            held_down[at] = jnp.concatenate(parts, axis=-1)
            held_output[at] = output_refs[j][...]
        turned = held_down[...].reshape(width, hidden_count)
        turned_ref[...] = turned
        down_ref[...] = turned.T
        output_ref[...] = held_output[...].reshape(width, width).T.reshape(count, own, width)

    shapes = [(hidden_count, width), (width, hidden_count), (count, own, width)]
    scratch = [pltpu.VMEM((count, own, hidden_count), BF), pltpu.VMEM((count, own, width), BF)]
    return glue(kernel, me, [*down, *output], shapes, "build_weights", scratch)


def cut_down(grad, me, count, group):
    width, hidden_count = grad.shape
    own, split = width // count, hidden_count // group

    def kernel(me_ref, in_ref, *outs):
        for j in range(count):
            start = pl.multiple_of((me_ref[0] ^ j) * own, own)
            rows = in_ref[pl.ds(start, own), :]
            for h in range(group):
                outs[j][h] = rows[:, h * split : (h + 1) * split]

    return glue(kernel, me, [grad], [(group, own, split)] * count, "cut_down")


def hold_rows(grad, me, blocks):
    rows = grad.shape[0] // blocks

    def kernel(me_ref, in_ref, out_ref):
        for f in range(blocks):
            out_ref[f] = in_ref[f * rows : (f + 1) * rows]

    return glue(kernel, me, [grad], [(blocks, rows, grad.shape[1])], "hold_rows")[0]


def merge_blocks(parts, me):
    count = len(parts)
    group, own, split = parts[0].shape

    def kernel(me_ref, *refs):
        out = refs[count]
        for j in range(count):
            for h in range(group):
                out[(me_ref[0] ^ j) * group + h] = refs[j][h]

    return glue(kernel, me, parts, [(count * group, own, split)], "merge_blocks")[0]


def attend(qkv, wide_heads, first, heads, kept):
    images, count, length, _ = qkv.shape
    rows = length
    half = first // heads
    keys = count * length
    flat = qkv.reshape(images, keys, 3 * wide_heads)

    def kernel(q_ref, kv_ref, *refs):
        mixed_ref, query_ref, exact_ref, turned = refs[-4:]

        @pl.when(pl.program_id(1) == 0)
        def _():
            for e in range(heads):
                at = wide_heads + (first + e) * WIDE
                turned[e] = kv_ref[0, :, at : at + WIDE].T

        total = jnp.zeros((rows, heads * HEAD), F32)
        for e in range(heads):
            here = slice(e * WIDE, (e + 1) * WIDE)
            query = q_ref[0, 0, :, here]
            at = 2 * wide_heads + (first + e) * WIDE
            v = kv_ref[0, :, at : at + WIDE]
            scores = mm(query, turned[e])
            top = jnp.max(scores, axis=-1, keepdims=True)
            weights = jnp.exp2(scores - top).astype(BF)
            mixed = mm(weights, v)
            summed = mixed[:, SUM_AT : SUM_AT + 1]
            mixed = mixed / summed
            log_total = top + jnp.log2(summed)
            exact_ref[0, 0, :, here] = mixed
            query_ref[0, 0, :, here] = put_parts(query.astype(F32), log_total, LSE_AT).astype(BF)
            source = lax.broadcasted_iota(jnp.int32, (WIDE, heads * HEAD), 0)
            target = lax.broadcasted_iota(jnp.int32, (WIDE, heads * HEAD), 1)
            pick = ((source < HEAD) & (source + e * HEAD == target)).astype(F32).astype(BF)
            total = total + mm(mixed.astype(BF), pick)
        mixed_ref[0, 0] = total.T.astype(BF)

    part = pl.BlockSpec((1, 1, rows, heads * WIDE), lambda i, b: (i, b, 0, half))
    shapes = [
        jax.ShapeDtypeStruct((images, count, heads * HEAD, rows), BF),
        jax.ShapeDtypeStruct((images, count, length, wide_heads), BF),
        jax.ShapeDtypeStruct((images, count, length, wide_heads), F32),
    ]
    outs = [pl.BlockSpec((1, 1, heads * HEAD, rows), lambda i, b: (i, b, 0, 0)), part, part]
    extra = list(kept)
    scores = images * count * rows * keys * heads
    return pl.pallas_call(
        kernel,
        grid=(images, count),
        in_specs=[part, pl.BlockSpec((1, keys, 3 * wide_heads), lambda i, b: (i, 0, 0))]
        + [pl.BlockSpec(memory_space=pl.ANY)] * len(extra),
        out_specs=outs,
        out_shape=shapes,
        input_output_aliases={2 + i: 1 + i for i in range(len(extra))},
        scratch_shapes=[pltpu.VMEM((heads, WIDE, keys), BF)],
        cost_estimate=cost(2 * scores * WIDE * 2, flat.size * 2 + 3 * images * keys * wide_heads, scores),
        compiler_params=pltpu.CompilerParams(vmem_limit_bytes=VMEM_BYTES),
        name="attend",
    )(qkv, flat, *extra)


def middle(mixed, tokens, cotangent, weights, chunk, kept):
    images, count, length, width = tokens.shape
    me, w_output, w_up, up_turned, w_down, down_turned, b_output, gain, shift, b_up = weights
    rows = length // CHUNKS
    halves = len(mixed[0])
    part_own = mixed[0][0].shape[-2]
    mixed = [piece for pieces in mixed for piece in pieces]
    hidden_count = w_up.shape[1]

    def kernel(me_ref, *refs):
        mixed_refs = refs[: count * halves]
        (
            tok_ref,
            cot_ref,
            wo_ref,
            up_ref,
            up_turned_ref,
            down_ref,
            down_turned_ref,
            bo_ref,
            g_ref,
            s_ref,
            bu_ref,
        ) = refs[count * halves : count * halves + 11]
        outs = refs[-(6 + 2 * count) :]
        h_ref, z_ref, du_ref, cat_ref, x_ref, gb_ref = outs[:6]
        dh_refs, y_refs = outs[6 : 6 + count], outs[6 + count :]
        block = pl.program_id(1)
        x_one = tok_ref[0, 0].astype(F32) + bo_ref[...]
        pieces = []
        for i in range(count):
            parts = [ref[0, 0] for ref in mixed_refs[i * halves : (i + 1) * halves]]
            piece = jnp.concatenate(parts, axis=0).T
            pieces.append(piece)
            x_one = x_one + mm(piece, wo_ref[me_ref[0] ^ i])
        cat_ref[0, 0] = jnp.concatenate(pieces, axis=-1)

        @pl.when(block == 0)
        def _():
            x_ref[0] = x_one

        normed, _ = norm_parts(x_one)
        h_two = (normed * g_ref[...] + s_ref[...]).astype(BF)
        h_ref[0, 0] = h_two
        hidden = mm(h_two, up_ref[...]) + bu_ref[...]
        grad_act = mm(cot_ref[0, 0], down_turned_ref[...])
        square = hidden * hidden
        inner = jnp.tanh(ROOT * (hidden + CUBIC * square * hidden))
        half = 0.5 * (1.0 + inner)
        z = (hidden * half).astype(BF)
        slope = half + 0.5 * hidden * (1.0 - inner * inner) * ROOT * (1.0 + 3.0 * CUBIC * square)
        wide_grad = grad_act * slope
        grad_hidden = wide_grad.astype(BF)
        z_ref[0, 0] = z
        du_ref[0, 0] = grad_hidden
        dh = mm(grad_hidden, up_turned_ref[...]).astype(BF)
        y = mm(z, down_ref[...]).astype(BF)
        for j in range(count):

            @pl.when(block == j)
            def _():
                dh_refs[j][0] = dh
                y_refs[j][0] = y

        summed = jnp.sum(grad_hidden.astype(F32), axis=0, keepdims=True)
        first = (pl.program_id(0) == 0) & (block == 0)

        @pl.when(first)
        def _():
            gb_ref[...] = summed

        @pl.when(jnp.logical_not(first))
        def _():
            gb_ref[...] += summed

    def piece_spec(i):
        return pl.BlockSpec((1, 1, part_own, rows), lambda im, b, me_ref: (im, b ^ i, 0, 0))

    def whole_spec(array):
        return pl.BlockSpec(array.shape, lambda im, b, me_ref: (0,) * array.ndim)

    full = pl.BlockSpec((1, 1, rows, width), lambda im, b, me_ref: (im, b, chunk, 0))
    full_hidden = pl.BlockSpec((1, 1, rows, hidden_count), lambda im, b, me_ref: (im, b, chunk, 0))
    part = pl.BlockSpec((1, rows, width), lambda im, b, me_ref: (im, 0, 0))
    constants = [w_output, w_up, up_turned, w_down, down_turned, b_output, gain, shift, b_up]
    extra = list(kept)
    inputs = [*mixed, tokens, cotangent, *constants, *extra]
    all_rows = images * count * rows
    return pl.pallas_call(
        kernel,
        grid_spec=pltpu.PrefetchScalarGridSpec(
            num_scalar_prefetch=1,
            grid=(images, count),
            in_specs=[piece_spec(i) for i in range(count) for _ in range(halves)]
            + [full, full]
            + [whole_spec(array) for array in constants]
            + [pl.BlockSpec(memory_space=pl.ANY)] * len(extra),
            out_specs=[
                full,
                full_hidden,
                full_hidden,
                full,
                part,
                pl.BlockSpec((1, hidden_count), lambda im, b, me_ref: (0, 0)),
            ]
            + [part] * (2 * count),
        ),
        out_shape=[
            jax.ShapeDtypeStruct(tokens.shape, BF),
            jax.ShapeDtypeStruct((images, count, length, hidden_count), BF),
            jax.ShapeDtypeStruct((images, count, length, hidden_count), BF),
            jax.ShapeDtypeStruct(tokens.shape, BF),
            jax.ShapeDtypeStruct((images, rows, width), F32),
            jax.ShapeDtypeStruct((1, hidden_count), F32),
        ]
        + [jax.ShapeDtypeStruct((images, rows, width), BF)] * (2 * count),
        input_output_aliases={1 + count * halves + 11 + i: i for i in range(len(extra))},
        cost_estimate=cost(
            all_rows * width * (width + 4 * hidden_count) * 2,
            all_rows * (width * 16 + hidden_count * 4) + (w_output.size + 2 * w_up.size) * 2,
        ),
        compiler_params=pltpu.CompilerParams(vmem_limit_bytes=VMEM_BYTES),
        name="middle",
    )(me.reshape(1), *inputs)


def mixed_back(grad, w_wide, exact, chunk, kept):
    images, count, rows, width = grad.shape
    _, _, length, wide_heads = exact.shape
    heads = wide_heads // WIDE

    def kernel(grad_ref, w_ref, exact_ref, *refs):
        out_ref = refs[-1]
        result = mm(grad_ref[0, 0], w_ref[...]).astype(BF).astype(F32)
        for e in range(heads):
            here = slice(e * WIDE, (e + 1) * WIDE)
            mine = result[:, here]
            exact = exact_ref[0, 0, :, here]
            delta = jnp.sum(mine * exact, axis=-1, keepdims=True)
            value = put_parts(mine, delta, SUM_AT).astype(BF)
            out_ref[0, 0, :, here] = value

    full = pl.BlockSpec((1, 1, rows, wide_heads), lambda im, b: (im, b, chunk, 0))
    extra = list(kept)
    return pl.pallas_call(
        kernel,
        grid=(images, count),
        in_specs=[
            pl.BlockSpec((1, 1, rows, width), lambda im, b: (im, b, 0, 0)),
            pl.BlockSpec(w_wide.shape, lambda im, b: (0, 0)),
            full,
        ]
        + [pl.BlockSpec(memory_space=pl.ANY)] * len(extra),
        out_specs=full,
        out_shape=jax.ShapeDtypeStruct(exact.shape, BF),
        input_output_aliases={3 + i: i for i in range(len(extra))},
        cost_estimate=cost(
            images * count * rows * width * wide_heads,
            images * count * rows * (width * 2 + wide_heads * 6) + w_wide.size * 2,
        ),
        compiler_params=pltpu.CompilerParams(vmem_limit_bytes=VMEM_BYTES),
        name="mixed_back",
    )(grad, w_wide, exact, *extra)


def attend_back(query, grad, qkv, first, heads):
    images, keys, wide_heads = query.shape
    every = wide_heads // WIDE
    rows = min(512, keys)
    span = min(512, keys)
    steps = keys // rows

    def kernel(q_ref, do_ref, k_ref, v_ref, dq_ref, dk_ref, dv_ref, kt, dk, dv):
        step = pl.program_id(2)

        @pl.when(step == 0)
        def _():
            kt[...] = k_ref[0].T
            dk[...] = jnp.zeros_like(dk)
            dv[...] = jnp.zeros_like(dv)

        q = q_ref[0]
        do = do_ref[0]
        turned = jnp.zeros((WIDE, rows), F32)
        for at in range(0, keys, span):
            here = slice(at, at + span)
            probs = jnp.exp2(mm(k_ref[0, here], q, NT))
            grad_scores = (probs * mm(v_ref[0, here], do, NT)).astype(BF)
            dv[here] += mm(probs.astype(BF), do)
            dk[here] += mm(grad_scores, q)
            turned = turned + mm(kt[:, here], grad_scores)
        dq_ref[0] = (turned.T * SCALE).astype(BF)

        @pl.when(step == steps - 1)
        def _():
            dk_ref[0] = (dk[...] * (1.0 / LOG2E)).astype(BF)
            dv_ref[0] = dv[...].astype(BF)

    row_in = pl.BlockSpec((1, rows, WIDE), lambda i, e, b: (i, b, e + first))
    row_out = pl.BlockSpec((1, rows, WIDE), lambda i, e, b: (i, b, e))

    def all_spec(shift):
        return pl.BlockSpec((1, keys, WIDE), lambda i, e, b: (i, 0, e + shift))

    shape = jax.ShapeDtypeStruct((images, keys, heads * WIDE), BF)
    scores = images * heads * keys * keys
    return pl.pallas_call(
        kernel,
        grid=(images, heads, steps),
        in_specs=[row_in, row_in, all_spec(every + first), all_spec(2 * every + first)],
        out_specs=[row_out, all_spec(0), all_spec(0)],
        out_shape=[shape] * 3,
        scratch_shapes=[
            pltpu.VMEM((WIDE, keys), BF),
            pltpu.VMEM((keys, WIDE), F32),
            pltpu.VMEM((keys, WIDE), F32),
        ],
        cost_estimate=cost(5 * scores * WIDE * 2, 7 * images * keys * wide_heads * 2, scores),
        compiler_params=pltpu.CompilerParams(vmem_limit_bytes=VMEM_BYTES),
        name="attend_back",
    )(query, grad, qkv, qkv)


def project_back(grads, tokens, w_turned, gain, shift, narrow):
    images, count, length, width = tokens.shape
    parts = len(grads[0])
    part = grads[0][0].shape[-1]
    wide = parts * part
    own = narrow.shape[1]
    flat = [piece for kind in grads for piece in kind]
    last_image, last_block = images - 1, count - 1

    def kernel(*refs):
        ins = refs[: len(flat)]
        tok_ref, w_ref, g_ref, s_ref, n_ref = refs[len(flat) : len(flat) + 5]
        outs = refs[len(flat) + 5 : -1]
        held = refs[-1]
        dh_refs = outs[:count]
        weight_ref, norm_ref, bias_ref = outs[count:]
        block = pl.program_id(1)
        first = (pl.program_id(0) == 0) & (block == 0)

        @pl.when(first)
        def _():
            held[...] = jnp.zeros_like(held)
            norm_ref[...] = jnp.zeros_like(norm_ref)
            bias_ref[...] = jnp.zeros_like(bias_ref)

        normed, _ = norm_parts(tok_ref[0, 0].astype(F32))
        turned = (normed * g_ref[...] + s_ref[...]).astype(BF).T
        total = jnp.zeros((length, width), F32)
        for i, ref in enumerate(ins):
            piece = ref[0, 0]
            here = slice(i * part, (i + 1) * part)
            total = total + mm(piece, w_ref[here])
            held[:, here] += mm(turned, piece)
            bias_ref[:, here] += jnp.sum(piece.astype(F32), axis=0, keepdims=True)
        for j in range(count):

            @pl.when(block == j)
            def _():
                dh_refs[j][0] = total.astype(BF)

        norm_ref[0:1] += jnp.sum(total * normed, axis=0, keepdims=True)
        norm_ref[1:2] += jnp.sum(total, axis=0, keepdims=True)

        @pl.when((pl.program_id(0) == last_image) & (block == last_block))
        def _():
            for kind in range(3):
                whole = held[:, kind * wide : (kind + 1) * wide].astype(BF)
                weight_ref[kind] = mm(whole, n_ref[...]).astype(BF)

    piece_spec = pl.BlockSpec((1, 1, length, part), lambda im, b: (im, b, 0, 0))
    row_spec = pl.BlockSpec((1, 1, length, width), lambda im, b: (im, b, 0, 0))

    def whole_spec(shape):
        return pl.BlockSpec(shape, lambda im, b: (0,) * len(shape))

    shapes = [(3, width, own), (2, width), (1, 3 * wide)]
    kinds = [BF, F32, F32]
    all_rows = images * count * length
    return pl.pallas_call(
        kernel,
        grid=(images, count),
        in_specs=[piece_spec] * len(flat)
        + [row_spec]
        + [whole_spec(a.shape) for a in (w_turned, gain, shift, narrow)],
        out_specs=[pl.BlockSpec((1, length, width), lambda im, b: (im, 0, 0))] * count
        + [whole_spec(shape) for shape in shapes],
        out_shape=[jax.ShapeDtypeStruct((images, length, width), BF)] * count
        + [jax.ShapeDtypeStruct(shape, kind) for shape, kind in zip(shapes, kinds)],
        scratch_shapes=[pltpu.VMEM((width, 3 * wide), F32)],
        cost_estimate=cost(
            2 * all_rows * width * wide * 3,
            all_rows * (wide * 6 + width * 4) + w_turned.size * 2,
        ),
        compiler_params=pltpu.CompilerParams(vmem_limit_bytes=VMEM_BYTES),
        name="project_back",
    )(*flat, tokens, w_turned, gain, shift, narrow)


def local(
    tokens,
    patch_mask,
    gain_one,
    shift_one,
    w_query,
    b_query,
    w_key,
    w_value,
    b_value,
    w_output,
    b_output,
    gain_two,
    shift_two,
    w_up,
    b_up,
    w_down,
    b_down,
    cotangent,
):
    me = lax.axis_index("seq")
    count = lax.axis_size("seq")
    fcount = lax.axis_size("fsdp")
    images, length, width = tokens.shape
    own = w_query.shape[1]
    heads = own // HEAD
    wide_heads = heads * WIDE
    group = fcount // count
    rows = length // CHUNKS

    qkv_shard = jnp.concatenate([w_query, w_key, w_value], axis=1)
    small = jnp.concatenate(
        [patch_mask.astype(BF).reshape(-1)]
        + [gain_one, shift_one, b_output, gain_two, shift_two, b_down]
    )
    small = spread(small)
    qkv_blocks, qkv_index = ring_gather(qkv_shard, 0)
    tok_blocks, cot_blocks = None, None
    fast = images == 1 and count == 4
    if fast:
        near, across = swap(tokens, 1), swap(tokens, 2)
        across, cot_sent = together(across, cotangent)
        cot_across = swap(cot_sent, 2)
        across, cot_sent, qkv_blocks = together(across, cot_sent, qkv_blocks)
        tok_blocks = [tokens, near, across, swap(across, 1)]
    w_wide = place_wide(qkv_blocks, qkv_index, widen(3 * own, 3 * wide_heads))
    split = w_down.shape[0]
    lower = jnp.concatenate([w_down.T, w_output.T], axis=1)
    lower = lax.all_gather(lower, "fsdp", axis=0)
    if fast:
        down_sent, output_cols = cut_lower(lower, me, count, split)
    else:
        output_cols = lower[:, :, split:].transpose(1, 0, 2).reshape(own, width)
        down_sent = [
            lax.dynamic_slice_in_dim(lower[:, :, :split], (me ^ j) * group, group, 0)
            for j in range(count)
        ]
    up_mat = lax.all_gather(w_up, "fsdp", axis=0, tiled=True)

    patches = images * length
    valid = jnp.stack([block[:patches].reshape(images, length) for block in small], axis=1)
    bias_mask = jnp.where(valid > 0, 0.0, NEG).astype(F32)
    vectors = reorder([block[patches:].reshape(6, own) for block in small], me)
    vectors = jnp.concatenate(vectors, axis=1).astype(F32)
    g_one, s_one, b_out, g_two, s_two, b_dn = [vectors[i : i + 1] for i in range(6)]

    expand = widen(own, wide_heads)
    lane = np.arange(3 * wide_heads) % WIDE
    kind = np.arange(3 * wide_heads) // wide_heads
    factor = np.where(kind == 0, SCALE * LOG2E, 1.0).astype(np.float32)
    ones = (kind == 0) & (lane == MASK_AT)
    ones |= (kind == 1) & (lane >= LSE_AT) & (lane < LSE_AT + 3)
    ones |= (kind == 2) & (lane >= SUM_AT) & (lane < SUM_AT + 3)
    at_mask = ((kind == 1) & (lane == MASK_AT)).astype(np.float32)

    def widen_vector(vector):
        shaped = vector.astype(F32).reshape(heads, HEAD)
        return jnp.pad(shaped, ((0, 0), (0, WIDE - HEAD))).reshape(-1)

    def narrow(vector):
        return vector.reshape(heads, WIDE)[:, :HEAD].reshape(-1)

    bias_wide = jnp.concatenate(
        [widen_vector(b_query), jnp.zeros((wide_heads,), F32), widen_vector(b_value)]
    )
    bias_wide = bias_wide * factor + ones.astype(np.float32)

    single = images == 1
    down_exchanged = [down_sent[0]] + [swap(down_sent[j], j) for j in range(1, count)]
    cot_begun = (cot_sent, None, cot_across) if fast else None
    w_turned = w_wide.T

    def token_grads(tokens, residual, grad_norm):
        normed, inverse = norm_parts(tokens.astype(F32))
        return (residual + norm_back(grad_norm, normed, inverse, g_one)).astype(BF)

    def scatter_up(up_grad):
        blocks = up_grad if fast else up_grad.astype(BF).reshape(fcount, width // fcount, -1)
        return lax.psum_scatter(blocks, "fsdp", scatter_dimension=0)

    def send_down(down_grad):
        if fast:
            sent = cut_down(down_grad, me, count, group)
            return [sent[0]] + [swap(sent[j], j) for j in range(1, count)]
        shaped = down_grad.astype(BF).reshape(width, group, -1).transpose(1, 0, 2)

        def cols(j):
            return lax.dynamic_slice_in_dim(shaped, (me ^ j) * own, own, 1)

        return [cols(0)] + [swap(cols(j), j) for j in range(1, count)]

    def merge_down(got):
        if fast:
            return merge_blocks(got, me)
        return jnp.concatenate(reorder(got, me), axis=0)

    def run(tokens, bias_mask, cotangent, tok_blocks=None):
        images = tokens.shape[0]
        if tok_blocks is None:
            tok_blocks = spread(tokens)
        tok_all = jnp.stack(tok_blocks, axis=1)
        normed, _ = norm_parts(tok_all.astype(F32))
        h_one = (normed * g_one + s_one).astype(BF)
        product = jnp.einsum("ijld,de->ijle", h_one, w_wide, preferred_element_type=F32)
        qkv = (product * factor + bias_wide + bias_mask[..., None] * at_mask).astype(BF)
        if fast:
            qkv, cot_across, down_own, turned = together(
                qkv, cot_begun[2], down_sent[0], w_turned
            )
            down_parts = [down_own] + down_exchanged[1:]
            cot_blocks = [cotangent, swap(cot_begun[0], 1), cot_across, swap(cot_across, 1)]
        else:
            cot_blocks = spread(cotangent)
            down_parts, turned = down_exchanged, w_turned
        output_parts = spread(output_cols)
        up_turned = up_mat.T
        cot_all = jnp.stack(cot_blocks, axis=1)

        kept_middle = ()
        halves = 2 if heads % 2 == 0 else 1
        step = heads // halves
        mixed, *kept_attend = attend(qkv, wide_heads, 0, step, ())
        mixed_blocks = [[block] for block in spread(mixed)]
        if halves == 2:
            kept_attend, down_parts, output_parts = together(
                kept_attend, down_parts, output_parts
            )
            mixed, *kept_attend = attend(qkv, wide_heads, step, step, kept_attend)
            for pieces, block in zip(mixed_blocks, spread(mixed)):
                pieces.append(block)
        query_wide, mixed_exact = kept_attend
        down_in, output_in = down_parts, output_parts
        if fast:
            down_mat, down_turned, output_mat = build_weights(down_in, output_in, me)
        else:
            down_turned = jnp.stack(reorder(down_in, me)).transpose(0, 2, 1, 3)
            down_turned = down_turned.reshape(width, -1)
            down_mat = down_turned.T
            output_mat = jnp.concatenate(reorder(output_in, me), axis=0).T
            output_mat = output_mat.reshape(count, own, width)
        own_rows = lax.dynamic_index_in_dim(output_mat, me, 0, keepdims=False)
        output_wide = mm(own_rows.T, expand).astype(BF)
        weights = (
            me,
            output_mat,
            up_mat,
            up_turned,
            down_mat,
            down_turned,
            b_out,
            g_two,
            s_two,
            b_up.astype(F32)[None],
        )
        def grad_rows(c, hidden_grad, x_own):
            grad_norm = hidden_grad.astype(F32)
            normed_two, inverse_two = norm_parts(x_own)
            cot_own = cotangent[:, c * rows : (c + 1) * rows].astype(F32)
            residual = cot_own + norm_back(grad_norm, normed_two, inverse_two, g_two)
            grad_attn = residual.astype(BF)
            sums = jnp.stack(
                [
                    jnp.sum(grad_norm * normed_two, axis=(0, 1)),
                    jnp.sum(grad_norm, axis=(0, 1)),
                    jnp.sum(grad_attn.astype(F32), axis=(0, 1)),
                    jnp.sum(cot_own, axis=(0, 1)),
                ]
            )
            return residual, grad_attn, sums

        out_parts, x_parts = [], []
        grad_attn_all, grad_residual = [], []
        hidden_parts = []
        early, up_bias_grad = 0.0, 0.0
        for c in range(CHUNKS):
            result = middle(mixed_blocks, tok_all, cot_all, weights, c, kept_middle)
            kept_middle, x_own, gb = result[:4], result[4], result[5]
            hidden_parts.append(list(result[6 : 6 + count]))
            out_parts.append(result[6 + count :])
            x_parts.append(x_own)
            up_bias_grad = up_bias_grad + gb[0]
        h_two, activated, grad_hidden, mixed_all = kept_middle
        blocks = hidden_parts[0]
        if count == 4:
            near_sum, crossing = collect_pair(blocks)
            h_two, crossing = together(h_two, crossing)
            incoming = swap(crossing, 2)
        else:
            near_sum, incoming = collect(blocks), jnp.zeros((), F32)
        up_grad = jnp.einsum(
            "ijld,ijlf->df",
            h_two,
            grad_hidden,
            preferred_element_type=F32,
        ).astype(BF if single else F32)
        if fast:
            up_grad = hold_rows(up_grad, me, fcount)
        incoming, up_grad = together(incoming, up_grad)
        if single:
            up_grad = scatter_up(up_grad)
        hidden_grad = near_sum + incoming.astype(F32)
        residual, grad_attn, early = grad_rows(0, hidden_grad, x_parts[0])
        grad_attn, activated = together(grad_attn, activated)
        down_grad = jnp.einsum(
            "ijld,ijlf->df",
            cot_all,
            activated,
            preferred_element_type=F32,
        ).astype(BF if single else F32)
        grad_residual.append(residual)
        if fast:
            across = swap(grad_attn, 2)
            near = swap(grad_attn, 1)
            across, down_grad = together(across, down_grad)
            attn_blocks = [grad_attn, near, across, swap(across, 1)]
        else:
            attn_blocks = spread(grad_attn)
        grad_attn_all = jnp.stack(attn_blocks, axis=1)
        grad_mixed = mixed_back(grad_attn_all, output_wide, mixed_exact, 0, ())

        wide_shape = (images, count * length, wide_heads)
        query_in = query_wide.reshape(wide_shape)
        grad_in = grad_mixed.reshape(wide_shape)
        flat_qkv = qkv.reshape(images, count * length, 3 * wide_heads)
        grad_in, out_blocks, down_grad = together(grad_in, list(out_parts[0]), down_grad)
        if single:
            down_grad = send_down(down_grad)
            grad_in, up_grad = together(grad_in, up_grad)
        if count == 4:
            out_sum, out_across = collect_pair(out_blocks)
            grad_in, out_across = together(grad_in, out_across)
            out_incoming = swap(out_across, 2)
        else:
            out_sum, out_incoming = collect(out_blocks), jnp.zeros((), F32)
        first = attend_back(query_in, grad_in, flat_qkv, 0, step)
        pieces = [first]
        if halves == 2:
            first, down_grad = together(first, down_grad)
            if single:
                down_grad = merge_down(down_grad)
            query_in, down_grad = together(query_in, down_grad)
            pieces = [first, attend_back(query_in, grad_in, flat_qkv, step, step)]
            pieces, out_incoming = together(pieces, out_incoming)
        elif single:
            down_grad = merge_down(down_grad)
        out_sum = out_sum + out_incoming.astype(F32)
        grads = [
            [piece[k].reshape(images, count, length, -1) for piece in pieces] for k in range(3)
        ]
        grad_attn_cols = lax.dynamic_slice_in_dim(grad_attn_all, me * own, own, 3)
        output_grad = jnp.einsum(
            "ijle,ijld->ed", mixed_all, grad_attn_cols, preferred_element_type=F32
        )
        result = project_back(grads, tok_all, turned, g_one, s_one, expand.T)
        qkv_grad, late, bias_grads = result[count:]
        if fast:
            norm_near, norm_across = collect_pair(list(result[:count]))
            ends = (grad_residual[0], norm_near, swap(norm_across, 2))
        else:
            grad_norm = collect(list(result[:count])).astype(F32)
            ends = token_grads(tokens, grad_residual[0], grad_norm)

        layer_out = (jnp.concatenate(x_parts, axis=1) + out_sum.astype(F32) + b_dn).astype(BF)
        qkv_grad = qkv_grad if single else qkv_grad.astype(F32)
        sums = (down_grad, up_grad, output_grad, qkv_grad, early, up_bias_grad, late, bias_grads)
        return sums, (layer_out, ends)

    if images == 1:
        sums, (layer_out, ends) = run(tokens, bias_mask, cotangent, tok_blocks)
    else:
        items = (tokens[:, None], bias_mask[:, None], cotangent[:, None])
        shapes = jax.eval_shape(lambda item: run(*item)[0], jax.tree.map(lambda a: a[0], items))
        empty = jax.tree.map(lambda a: jnp.zeros(a.shape, a.dtype), shapes)

        def step(totals, item):
            sums, results = run(*item)
            return jax.tree.map(jnp.add, totals, sums), results

        sums, (layer_out, ends) = lax.scan(step, empty, items)
        layer_out = layer_out[:, 0]
        grad_tokens = ends[:, 0]
    down_grad, up_grad, output_grad, qkv_grad, early, up_bias_grad, late, bias_grads = sums

    down_pieces = down_grad if single else merge_down(send_down(down_grad))
    final_up = (up_grad if single else scatter_up(up_grad)).astype(F32)
    final_down = lax.psum_scatter(down_pieces, "fsdp", scatter_dimension=0)
    output_grad = reorder(jnp.split(output_grad.astype(BF), count, axis=0), me)
    output_grad = jnp.concatenate(output_grad, axis=0)
    qkv_grad = qkv_grad.astype(BF).reshape(3, fcount, width // fcount, own)
    output_grad = output_grad.reshape(fcount, width // fcount, own)

    def four_parts(f):
        parts = lax.dynamic_index_in_dim(qkv_grad, f, 1, keepdims=False)
        last = lax.dynamic_index_in_dim(output_grad, f, 0, keepdims=True)
        return jnp.concatenate([parts, last], axis=0)


    def to_owner(stack):
        kinds = stack.shape[0]
        parts = jnp.split(stack.reshape(kinds, count, own), count, axis=1)
        parts = reorder([part[:, 0] for part in parts], me)
        total = parts[0]
        for j in range(1, count):
            total = total + swap(parts[j], j)
        return jnp.concatenate(
            [total.reshape(-1)] + [narrow(g) for g in bias_grads] + [up_bias_grad]
        )

    bias_grads = [bias_grads[0, i * wide_heads : (i + 1) * wide_heads] for i in (0, 2)]
    four, final_down, vectors = ring_reduce(
        four_parts,
        0,
        final_down,
        jnp.concatenate([early, late], axis=0),
        [to_owner] + sum_steps(),
    )
    final_down = final_down.astype(F32).T
    if fast:
        ends, four = together(ends, four)
        residual, norm_near, norm_incoming = ends
        grad_tokens = token_grads(tokens, residual, norm_near + norm_incoming.astype(F32))
    (
        gain_two_grad,
        shift_two_grad,
        b_output_grad,
        b_down_grad,
        gain_one_grad,
        shift_one_grad,
        b_query_grad,
        b_value_grad,
    ) = [vectors[i * own : (i + 1) * own] for i in range(8)]
    b_up_grad = vectors[8 * own :]
    final_query, final_key, final_value, final_output = [four[i] for i in range(4)]
    return (
        layer_out,
        grad_tokens,
        gain_one_grad,
        shift_one_grad,
        final_query,
        b_query_grad,
        final_key,
        final_value,
        b_value_grad,
        final_output,
        b_output_grad,
        gain_two_grad,
        shift_two_grad,
        final_up,
        b_up_grad,
        final_down,
        b_down_grad,
    )


def solution(mesh):
    rows = P("fsdp", "seq", None)
    matrix = P("fsdp", "seq")
    vector = P("seq")
    return jax.shard_map(
        local,
        mesh=mesh,
        in_specs=(
            rows,
            matrix,
            vector,
            vector,
            matrix,
            vector,
            matrix,
            matrix,
            vector,
            matrix,
            vector,
            vector,
            vector,
            matrix,
            vector,
            matrix,
            vector,
            rows,
        ),
        out_specs=(
            rows,
            rows,
            vector,
            vector,
            matrix,
            vector,
            matrix,
            matrix,
            vector,
            matrix,
            vector,
            vector,
            vector,
            matrix,
            vector,
            matrix,
            vector,
        ),
        check_vma=False,
    )
```

```python
import functools
import math

import jax
import jax.numpy as jnp
import numpy as np
from jax import lax
from jax.experimental import pallas as pl
from jax.experimental.pallas import tpu as pltpu
from jax.sharding import PartitionSpec as P

HEAD = 72
WIDE = 128
MASK_AT = HEAD
LSE_AT = HEAD + 1
SUM_AT = HEAD
CHUNKS = 1
BESIDE_AT = 3

EPS = 1e-06
ROOT = 0.7978845608028654
CUBIC = 0.044715
NEG = -1e30
LOG2E = math.log2(math.e)
SCALE = HEAD ** (-0.5)

BF = jnp.bfloat16
F32 = jnp.float32
NT = (((1,), (1,)), ((), ()))
NN = (((1,), (0,)), ((), ()))
VMEM_BYTES = 56 << 20


def mm(left, right, dims=NN):
    return lax.dot_general(left, right, dims, preferred_element_type=F32)


def cost(macs, moved, special=0):
    return pl.CostEstimate(flops=macs // 64, bytes_accessed=moved // 64, transcendentals=special // 64)


def swap(value, bit):
    count = lax.axis_size("seq")
    return lax.ppermute(value, "seq", [(i, i ^ bit) for i in range(count)])


def spread(value):
    count = lax.axis_size("seq")
    blocks = [None] * count
    blocks[0] = value
    have = [0]
    bit = count // 2
    while bit:
        for j in list(have):
            blocks[j | bit] = swap(blocks[j], bit)
            have.append(j | bit)
        bit //= 2
    return blocks


def collect(blocks):
    blocks = list(blocks)
    kind = blocks[0].dtype
    count = len(blocks)
    alive = list(range(count))
    bit = 1
    while bit < count:
        for j in reversed(alive):
            if j & bit:
                incoming = swap(blocks[j].astype(kind), bit)
                blocks[j ^ bit] = blocks[j ^ bit].astype(F32) + incoming.astype(F32)
        alive = [j for j in alive if not j & bit]
        bit *= 2
    return blocks[0]


def together(*values):
    return lax.optimization_barrier(values)


def collect_pair(blocks):
    own, near, across, far = blocks
    far = swap(far, 1)
    near = swap(near, 1)
    across = (across.astype(F32) + far.astype(F32)).astype(BF)
    return own.astype(F32) + near.astype(F32), across


def reorder(blocks, me):
    blocks = list(blocks)
    bit = 1
    while bit < len(blocks):
        odd = (me & bit) > 0
        blocks = [jnp.where(odd, blocks[j ^ bit], blocks[j]) for j in range(len(blocks))]
        bit *= 2
    return blocks


def ring_order():
    count = lax.axis_size("fsdp")
    if count == 8:
        return [0, 2, 4, 6, 7, 5, 3, 1]
    return list(range(count))


def ring_place():
    device = lax.axis_index("fsdp")
    if lax.axis_size("fsdp") == 8:
        return jnp.where(device % 2 == 0, device // 2, (15 - device) // 2)
    return device


def ring_shift(value, step):
    order = ring_order()
    count = len(order)
    return lax.ppermute(
        value, "fsdp", [(order[i], order[(i + step) % count]) for i in range(count)]
    )


def ring_owner(offset):
    count = lax.axis_size("fsdp")
    at = lax.rem(ring_place() + (offset + count), count)
    if count == 8:
        return jnp.where(at < 4, 2 * at, 15 - 2 * at)
    return at


def ring_gather(value, flip):
    count = lax.axis_size("fsdp")
    found = [(0, value)]
    far = (count // 2, count - 1 - count // 2)
    moving = [value, value]
    for k in range(1, count // 2 + 1):
        for way, step in ((0, 1), (1, -1)):
            if k <= far[way ^ flip]:
                moving[way] = ring_shift(moving[way], step)
                found.append((-step * k, moving[way]))
        moving = list(lax.optimization_barrier(tuple(moving)))
    index = jnp.stack([ring_owner(offset) for offset, _ in found])
    return [block for _, block in found], index


def place_wide(blocks, index, wide):
    count = len(blocks)
    rows, cols = blocks[0].shape
    merged = rows % 16 == 0

    def kernel(index_ref, *refs):
        wide_ref, out_ref, held = refs[count:]
        for i in range(count):
            held[index_ref[i]] = refs[i][...]
        if merged:
            out_ref[...] = mm(held[...].reshape(count * rows, cols), wide_ref[...]).astype(BF)
        else:
            for i in range(count):
                out_ref[i] = mm(held[i], wide_ref[...]).astype(BF)

    shape = (count * rows, wide.shape[1]) if merged else (count, rows, wide.shape[1])
    out = pl.pallas_call(
        kernel,
        grid_spec=pltpu.PrefetchScalarGridSpec(
            num_scalar_prefetch=1,
            grid=(1,),
            in_specs=[pl.BlockSpec(a.shape, lambda i, index: (0, 0)) for a in [*blocks, wide]],
            out_specs=pl.BlockSpec(shape, lambda i, index: (0,) * len(shape)),
            scratch_shapes=[pltpu.VMEM((count, rows, cols), BF)],
        ),
        out_shape=jax.ShapeDtypeStruct(shape, BF),
        cost_estimate=cost(count * rows * cols * wide.shape[1], 4 * count * rows * cols),
        compiler_params=pltpu.CompilerParams(vmem_limit_bytes=VMEM_BYTES),
        name="place_wide",
    )(index, *blocks, wide)
    return out.reshape(count * rows, wide.shape[1])


def ring_reduce(take, flip, beside, side, side_steps):
    side_steps = list(side_steps)
    count = lax.axis_size("fsdp")
    far = (count // 2, count - 1 - count // 2)
    total = take(ring_owner(0)).astype(F32)
    incoming = [None, None]
    for k in range(count // 2, 0, -1):
        for way, step in ((0, 1), (1, -1)):
            if k <= far[way ^ flip]:
                part = take(ring_owner(step * k))
                if incoming[way] is not None:
                    part = (part.astype(F32) + incoming[way].astype(F32)).astype(BF)
                incoming[way] = ring_shift(part, step)
        if side_steps:
            side = side_steps.pop(0)(side)
        if incoming[1] is not None and incoming[0] is not None:
            incoming, side = together(incoming, side)
        if k == BESIDE_AT:
            incoming, beside = together(incoming, beside)
    return total + incoming[0].astype(F32) + incoming[1].astype(F32), beside, side


def sum_steps():
    count = lax.axis_size("fsdp")

    def step(bit, value):
        return value + lax.ppermute(value, "fsdp", [(i, i ^ bit) for i in range(count)])

    bits = [1 << i for i in range(count.bit_length() - 1)]
    return [functools.partial(step, bit) for bit in bits]


def norm_parts(value):
    mean = jnp.mean(value, axis=-1, keepdims=True)
    centered = value - mean
    inverse = lax.rsqrt(jnp.mean(centered * centered, axis=-1, keepdims=True) + EPS)
    return centered * inverse, inverse


def norm_back(grad_out, normed, inverse, gain):
    scaled = grad_out * gain
    first = jnp.mean(scaled, axis=-1, keepdims=True)
    second = jnp.mean(scaled * normed, axis=-1, keepdims=True)
    return inverse * (scaled - first - normed * second)


def three_parts(value):
    high = value.astype(BF).astype(F32)
    rest = value - high
    middle = rest.astype(BF).astype(F32)
    return high, middle, rest - middle


def put_parts(value, column, at):
    lane = lax.broadcasted_iota(jnp.int32, value.shape, 1)
    for i, part in enumerate(three_parts(column)):
        value = jnp.where(lane == at + i, -part, value)
    return value


def widen(rows, cols, dtype=BF):
    source = lax.broadcasted_iota(jnp.int32, (rows, cols), 0)
    target = lax.broadcasted_iota(jnp.int32, (rows, cols), 1)
    return ((source // HEAD) * WIDE + source % HEAD == target).astype(dtype)


def glue(kernel, me, inputs, shapes, name, scratch=()):
    def spec(shape):
        return pl.BlockSpec(shape, lambda i, me_ref: (0,) * len(shape))

    return pl.pallas_call(
        kernel,
        grid_spec=pltpu.PrefetchScalarGridSpec(
            num_scalar_prefetch=1,
            grid=(1,),
            in_specs=[spec(a.shape) for a in inputs],
            out_specs=[spec(shape) for shape in shapes],
            scratch_shapes=scratch,
        ),
        out_shape=[jax.ShapeDtypeStruct(shape, BF) for shape in shapes],
        cost_estimate=cost(0, 4 * sum(a.size for a in inputs)),
        compiler_params=pltpu.CompilerParams(vmem_limit_bytes=VMEM_BYTES),
        name=name,
    )(me.reshape(1), *inputs)


def cut_lower(lower, me, count, split):
    blocks, own, total = lower.shape
    group = blocks // count

    def kernel(me_ref, in_ref, *outs):
        for j in range(count):
            start = (me_ref[0] ^ j) * group
            for h in range(group):
                outs[j][h] = in_ref[start + h][:, :split]
        outs[count][...] = jnp.concatenate([in_ref[f][:, split:] for f in range(blocks)], axis=-1)

    shapes = [(group, own, split)] * count + [(own, blocks * (total - split))]
    *down, output = glue(kernel, me, [lower], shapes, "cut_lower")
    return down, output


def build_weights(down, output, me):
    count = len(down)
    group, own, split = down[0].shape
    width = count * own
    hidden_count = group * split

    def kernel(me_ref, *refs):
        down_refs, output_refs = refs[:count], refs[count : 2 * count]
        down_ref, turned_ref, output_ref, held_down, held_output = refs[2 * count :]
        for j in range(count):
            at = me_ref[0] ^ j
            parts = [down_refs[j][h] for h in range(group)]
            held_down[at] = jnp.concatenate(parts, axis=-1)
            held_output[at] = output_refs[j][...]
        turned = held_down[...].reshape(width, hidden_count)
        turned_ref[...] = turned
        down_ref[...] = turned.T
        output_ref[...] = held_output[...].reshape(width, width).T.reshape(count, own, width)

    shapes = [(hidden_count, width), (width, hidden_count), (count, own, width)]
    scratch = [pltpu.VMEM((count, own, hidden_count), BF), pltpu.VMEM((count, own, width), BF)]
    return glue(kernel, me, [*down, *output], shapes, "build_weights", scratch)


def cut_down(grad, me, count, group):
    width, hidden_count = grad.shape
    own, split = width // count, hidden_count // group

    def kernel(me_ref, in_ref, *outs):
        for j in range(count):
            start = pl.multiple_of((me_ref[0] ^ j) * own, own)
            rows = in_ref[pl.ds(start, own), :]
            for h in range(group):
                outs[j][h] = rows[:, h * split : (h + 1) * split]

    return glue(kernel, me, [grad], [(group, own, split)] * count, "cut_down")


def hold_rows(grad, me, blocks):
    rows = grad.shape[0] // blocks

    def kernel(me_ref, in_ref, out_ref):
        for f in range(blocks):
            out_ref[f] = in_ref[f * rows : (f + 1) * rows]

    return glue(kernel, me, [grad], [(blocks, rows, grad.shape[1])], "hold_rows")[0]


def merge_blocks(parts, me):
    count = len(parts)
    group, own, split = parts[0].shape

    def kernel(me_ref, *refs):
        out = refs[count]
        for j in range(count):
            for h in range(group):
                out[(me_ref[0] ^ j) * group + h] = refs[j][h]

    return glue(kernel, me, parts, [(count * group, own, split)], "merge_blocks")[0]


def attend(qkv, wide_heads, first, heads, kept):
    images, count, length, _ = qkv.shape
    rows = length
    half = first // heads
    keys = count * length
    flat = qkv.reshape(images, keys, 3 * wide_heads)

    def kernel(q_ref, kv_ref, *refs):
        mixed_ref, query_ref, exact_ref, turned = refs[-4:]

        @pl.when(pl.program_id(1) == 0)
        def _():
            for e in range(heads):
                at = wide_heads + (first + e) * WIDE
                turned[e] = kv_ref[0, :, at : at + WIDE].T

        total = jnp.zeros((rows, heads * HEAD), F32)
        for e in range(heads):
            here = slice(e * WIDE, (e + 1) * WIDE)
            query = q_ref[0, 0, :, here]
            at = 2 * wide_heads + (first + e) * WIDE
            v = kv_ref[0, :, at : at + WIDE]
            scores = mm(query, turned[e])
            top = jnp.max(scores, axis=-1, keepdims=True)
            weights = jnp.exp2(scores - top).astype(BF)
            mixed = mm(weights, v)
            summed = mixed[:, SUM_AT : SUM_AT + 1]
            mixed = mixed / summed
            log_total = top + jnp.log2(summed)
            exact_ref[0, 0, :, here] = mixed
            query_ref[0, 0, :, here] = put_parts(query.astype(F32), log_total, LSE_AT).astype(BF)
            source = lax.broadcasted_iota(jnp.int32, (WIDE, heads * HEAD), 0)
            target = lax.broadcasted_iota(jnp.int32, (WIDE, heads * HEAD), 1)
            pick = ((source < HEAD) & (source + e * HEAD == target)).astype(F32).astype(BF)
            total = total + mm(mixed.astype(BF), pick)
        mixed_ref[0, 0] = total.T.astype(BF)

    part = pl.BlockSpec((1, 1, rows, heads * WIDE), lambda i, b: (i, b, 0, half))
    shapes = [
        jax.ShapeDtypeStruct((images, count, heads * HEAD, rows), BF),
        jax.ShapeDtypeStruct((images, count, length, wide_heads), BF),
        jax.ShapeDtypeStruct((images, count, length, wide_heads), F32),
    ]
    outs = [pl.BlockSpec((1, 1, heads * HEAD, rows), lambda i, b: (i, b, 0, 0)), part, part]
    extra = list(kept)
    scores = images * count * rows * keys * heads
    return pl.pallas_call(
        kernel,
        grid=(images, count),
        in_specs=[part, pl.BlockSpec((1, keys, 3 * wide_heads), lambda i, b: (i, 0, 0))]
        + [pl.BlockSpec(memory_space=pl.ANY)] * len(extra),
        out_specs=outs,
        out_shape=shapes,
        input_output_aliases={2 + i: 1 + i for i in range(len(extra))},
        scratch_shapes=[pltpu.VMEM((heads, WIDE, keys), BF)],
        cost_estimate=cost(2 * scores * WIDE * 2, flat.size * 2 + 3 * images * keys * wide_heads, scores),
        compiler_params=pltpu.CompilerParams(vmem_limit_bytes=VMEM_BYTES),
        name="attend",
    )(qkv, flat, *extra)


def middle(mixed, tokens, cotangent, weights, chunk, kept):
    images, count, length, width = tokens.shape
    me, w_output, w_up, up_turned, w_down, down_turned, b_output, gain, shift, b_up = weights
    rows = length // CHUNKS
    halves = len(mixed[0])
    part_own = mixed[0][0].shape[-2]
    mixed = [piece for pieces in mixed for piece in pieces]
    hidden_count = w_up.shape[1]

    def kernel(me_ref, *refs):
        mixed_refs = refs[: count * halves]
        (
            tok_ref,
            cot_ref,
            wo_ref,
            up_ref,
            up_turned_ref,
            down_ref,
            down_turned_ref,
            bo_ref,
            g_ref,
            s_ref,
            bu_ref,
        ) = refs[count * halves : count * halves + 11]
        outs = refs[-(6 + 2 * count) :]
        h_ref, z_ref, du_ref, cat_ref, x_ref, gb_ref = outs[:6]
        dh_refs, y_refs = outs[6 : 6 + count], outs[6 + count :]
        block = pl.program_id(1)
        x_one = tok_ref[0, 0].astype(F32) + bo_ref[...]
        pieces = []
        for i in range(count):
            parts = [ref[0, 0] for ref in mixed_refs[i * halves : (i + 1) * halves]]
            piece = jnp.concatenate(parts, axis=0).T
            pieces.append(piece)
            x_one = x_one + mm(piece, wo_ref[me_ref[0] ^ i])
        cat_ref[0, 0] = jnp.concatenate(pieces, axis=-1)

        @pl.when(block == 0)
        def _():
            x_ref[0] = x_one

        normed, _ = norm_parts(x_one)
        h_two = (normed * g_ref[...] + s_ref[...]).astype(BF)
        h_ref[0, 0] = h_two
        hidden = mm(h_two, up_ref[...]) + bu_ref[...]
        grad_act = mm(cot_ref[0, 0], down_turned_ref[...])
        square = hidden * hidden
        inner = jnp.tanh(ROOT * (hidden + CUBIC * square * hidden))
        half = 0.5 * (1.0 + inner)
        z = (hidden * half).astype(BF)
        slope = half + 0.5 * hidden * (1.0 - inner * inner) * ROOT * (1.0 + 3.0 * CUBIC * square)
        wide_grad = grad_act * slope
        grad_hidden = wide_grad.astype(BF)
        z_ref[0, 0] = z
        du_ref[0, 0] = grad_hidden
        dh = mm(grad_hidden, up_turned_ref[...]).astype(BF)
        y = mm(z, down_ref[...]).astype(BF)
        for j in range(count):

            @pl.when(block == j)
            def _():
                dh_refs[j][0] = dh
                y_refs[j][0] = y

        summed = jnp.sum(grad_hidden.astype(F32), axis=0, keepdims=True)
        first = (pl.program_id(0) == 0) & (block == 0)

        @pl.when(first)
        def _():
            gb_ref[...] = summed

        @pl.when(jnp.logical_not(first))
        def _():
            gb_ref[...] += summed

    def piece_spec(i):
        return pl.BlockSpec((1, 1, part_own, rows), lambda im, b, me_ref: (im, b ^ i, 0, 0))

    def whole_spec(array):
        return pl.BlockSpec(array.shape, lambda im, b, me_ref: (0,) * array.ndim)

    full = pl.BlockSpec((1, 1, rows, width), lambda im, b, me_ref: (im, b, chunk, 0))
    full_hidden = pl.BlockSpec((1, 1, rows, hidden_count), lambda im, b, me_ref: (im, b, chunk, 0))
    part = pl.BlockSpec((1, rows, width), lambda im, b, me_ref: (im, 0, 0))
    constants = [w_output, w_up, up_turned, w_down, down_turned, b_output, gain, shift, b_up]
    extra = list(kept)
    inputs = [*mixed, tokens, cotangent, *constants, *extra]
    all_rows = images * count * rows
    return pl.pallas_call(
        kernel,
        grid_spec=pltpu.PrefetchScalarGridSpec(
            num_scalar_prefetch=1,
            grid=(images, count),
            in_specs=[piece_spec(i) for i in range(count) for _ in range(halves)]
            + [full, full]
            + [whole_spec(array) for array in constants]
            + [pl.BlockSpec(memory_space=pl.ANY)] * len(extra),
            out_specs=[
                full,
                full_hidden,
                full_hidden,
                full,
                part,
                pl.BlockSpec((1, hidden_count), lambda im, b, me_ref: (0, 0)),
            ]
            + [part] * (2 * count),
        ),
        out_shape=[
            jax.ShapeDtypeStruct(tokens.shape, BF),
            jax.ShapeDtypeStruct((images, count, length, hidden_count), BF),
            jax.ShapeDtypeStruct((images, count, length, hidden_count), BF),
            jax.ShapeDtypeStruct(tokens.shape, BF),
            jax.ShapeDtypeStruct((images, rows, width), F32),
            jax.ShapeDtypeStruct((1, hidden_count), F32),
        ]
        + [jax.ShapeDtypeStruct((images, rows, width), BF)] * (2 * count),
        input_output_aliases={1 + count * halves + 11 + i: i for i in range(len(extra))},
        cost_estimate=cost(
            all_rows * width * (width + 4 * hidden_count) * 2,
            all_rows * (width * 16 + hidden_count * 4) + (w_output.size + 2 * w_up.size) * 2,
        ),
        compiler_params=pltpu.CompilerParams(vmem_limit_bytes=VMEM_BYTES),
        name="middle",
    )(me.reshape(1), *inputs)


def mixed_back(grad, w_wide, exact, chunk, kept):
    images, count, rows, width = grad.shape
    _, _, length, wide_heads = exact.shape
    heads = wide_heads // WIDE

    def kernel(grad_ref, w_ref, exact_ref, *refs):
        out_ref = refs[-1]
        result = mm(grad_ref[0, 0], w_ref[...]).astype(BF).astype(F32)
        for e in range(heads):
            here = slice(e * WIDE, (e + 1) * WIDE)
            mine = result[:, here]
            exact = exact_ref[0, 0, :, here]
            delta = jnp.sum(mine * exact, axis=-1, keepdims=True)
            value = put_parts(mine, delta, SUM_AT).astype(BF)
            out_ref[0, 0, :, here] = value

    full = pl.BlockSpec((1, 1, rows, wide_heads), lambda im, b: (im, b, chunk, 0))
    extra = list(kept)
    return pl.pallas_call(
        kernel,
        grid=(images, count),
        in_specs=[
            pl.BlockSpec((1, 1, rows, width), lambda im, b: (im, b, 0, 0)),
            pl.BlockSpec(w_wide.shape, lambda im, b: (0, 0)),
            full,
        ]
        + [pl.BlockSpec(memory_space=pl.ANY)] * len(extra),
        out_specs=full,
        out_shape=jax.ShapeDtypeStruct(exact.shape, BF),
        input_output_aliases={3 + i: i for i in range(len(extra))},
        cost_estimate=cost(
            images * count * rows * width * wide_heads,
            images * count * rows * (width * 2 + wide_heads * 6) + w_wide.size * 2,
        ),
        compiler_params=pltpu.CompilerParams(vmem_limit_bytes=VMEM_BYTES),
        name="mixed_back",
    )(grad, w_wide, exact, *extra)


def attend_back(query, grad, qkv, first, heads):
    images, keys, wide_heads = query.shape
    every = wide_heads // WIDE
    rows = min(512, keys)
    span = min(512, keys)
    steps = keys // rows

    def kernel(q_ref, do_ref, k_ref, v_ref, dq_ref, dk_ref, dv_ref, kt, dk, dv):
        step = pl.program_id(2)

        @pl.when(step == 0)
        def _():
            kt[...] = k_ref[0].T
            dk[...] = jnp.zeros_like(dk)
            dv[...] = jnp.zeros_like(dv)

        q = q_ref[0]
        do = do_ref[0]
        turned = jnp.zeros((WIDE, rows), F32)
        for at in range(0, keys, span):
            here = slice(at, at + span)
            probs = jnp.exp2(mm(k_ref[0, here], q, NT))
            grad_scores = (probs * mm(v_ref[0, here], do, NT)).astype(BF)
            dv[here] += mm(probs.astype(BF), do)
            dk[here] += mm(grad_scores, q)
            turned = turned + mm(kt[:, here], grad_scores)
        dq_ref[0] = (turned.T * SCALE).astype(BF)

        @pl.when(step == steps - 1)
        def _():
            dk_ref[0] = (dk[...] * (1.0 / LOG2E)).astype(BF)
            dv_ref[0] = dv[...].astype(BF)

    row_in = pl.BlockSpec((1, rows, WIDE), lambda i, e, b: (i, b, e + first))
    row_out = pl.BlockSpec((1, rows, WIDE), lambda i, e, b: (i, b, e))

    def all_spec(shift):
        return pl.BlockSpec((1, keys, WIDE), lambda i, e, b: (i, 0, e + shift))

    shape = jax.ShapeDtypeStruct((images, keys, heads * WIDE), BF)
    scores = images * heads * keys * keys
    return pl.pallas_call(
        kernel,
        grid=(images, heads, steps),
        in_specs=[row_in, row_in, all_spec(every + first), all_spec(2 * every + first)],
        out_specs=[row_out, all_spec(0), all_spec(0)],
        out_shape=[shape] * 3,
        scratch_shapes=[
            pltpu.VMEM((WIDE, keys), BF),
            pltpu.VMEM((keys, WIDE), F32),
            pltpu.VMEM((keys, WIDE), F32),
        ],
        cost_estimate=cost(5 * scores * WIDE * 2, 7 * images * keys * wide_heads * 2, scores),
        compiler_params=pltpu.CompilerParams(vmem_limit_bytes=VMEM_BYTES),
        name="attend_back",
    )(query, grad, qkv, qkv)


def project_back(grads, tokens, w_turned, gain, shift, narrow):
    images, count, length, width = tokens.shape
    parts = len(grads[0])
    part = grads[0][0].shape[-1]
    wide = parts * part
    own = narrow.shape[1]
    flat = [piece for kind in grads for piece in kind]
    last_image, last_block = images - 1, count - 1

    def kernel(*refs):
        ins = refs[: len(flat)]
        tok_ref, w_ref, g_ref, s_ref, n_ref = refs[len(flat) : len(flat) + 5]
        outs = refs[len(flat) + 5 : -1]
        held = refs[-1]
        dh_refs = outs[:count]
        weight_ref, norm_ref, bias_ref = outs[count:]
        block = pl.program_id(1)
        first = (pl.program_id(0) == 0) & (block == 0)

        @pl.when(first)
        def _():
            held[...] = jnp.zeros_like(held)
            norm_ref[...] = jnp.zeros_like(norm_ref)
            bias_ref[...] = jnp.zeros_like(bias_ref)

        normed, _ = norm_parts(tok_ref[0, 0].astype(F32))
        turned = (normed * g_ref[...] + s_ref[...]).astype(BF).T
        total = jnp.zeros((length, width), F32)
        for i, ref in enumerate(ins):
            piece = ref[0, 0]
            here = slice(i * part, (i + 1) * part)
            total = total + mm(piece, w_ref[here])
            held[:, here] += mm(turned, piece)
            bias_ref[:, here] += jnp.sum(piece.astype(F32), axis=0, keepdims=True)
        for j in range(count):

            @pl.when(block == j)
            def _():
                dh_refs[j][0] = total.astype(BF)

        norm_ref[0:1] += jnp.sum(total * normed, axis=0, keepdims=True)
        norm_ref[1:2] += jnp.sum(total, axis=0, keepdims=True)

        @pl.when((pl.program_id(0) == last_image) & (block == last_block))
        def _():
            for kind in range(3):
                whole = held[:, kind * wide : (kind + 1) * wide].astype(BF)
                weight_ref[kind] = mm(whole, n_ref[...]).astype(BF)

    piece_spec = pl.BlockSpec((1, 1, length, part), lambda im, b: (im, b, 0, 0))
    row_spec = pl.BlockSpec((1, 1, length, width), lambda im, b: (im, b, 0, 0))

    def whole_spec(shape):
        return pl.BlockSpec(shape, lambda im, b: (0,) * len(shape))

    shapes = [(3, width, own), (2, width), (1, 3 * wide)]
    kinds = [BF, F32, F32]
    all_rows = images * count * length
    return pl.pallas_call(
        kernel,
        grid=(images, count),
        in_specs=[piece_spec] * len(flat)
        + [row_spec]
        + [whole_spec(a.shape) for a in (w_turned, gain, shift, narrow)],
        out_specs=[pl.BlockSpec((1, length, width), lambda im, b: (im, 0, 0))] * count
        + [whole_spec(shape) for shape in shapes],
        out_shape=[jax.ShapeDtypeStruct((images, length, width), BF)] * count
        + [jax.ShapeDtypeStruct(shape, kind) for shape, kind in zip(shapes, kinds)],
        scratch_shapes=[pltpu.VMEM((width, 3 * wide), F32)],
        cost_estimate=cost(
            2 * all_rows * width * wide * 3,
            all_rows * (wide * 6 + width * 4) + w_turned.size * 2,
        ),
        compiler_params=pltpu.CompilerParams(vmem_limit_bytes=VMEM_BYTES),
        name="project_back",
    )(*flat, tokens, w_turned, gain, shift, narrow)


def local(
    tokens,
    patch_mask,
    gain_one,
    shift_one,
    w_query,
    b_query,
    w_key,
    w_value,
    b_value,
    w_output,
    b_output,
    gain_two,
    shift_two,
    w_up,
    b_up,
    w_down,
    b_down,
    cotangent,
):
    me = lax.axis_index("seq")
    count = lax.axis_size("seq")
    fcount = lax.axis_size("fsdp")
    images, length, width = tokens.shape
    own = w_query.shape[1]
    heads = own // HEAD
    wide_heads = heads * WIDE
    group = fcount // count
    rows = length // CHUNKS

    qkv_shard = jnp.concatenate([w_query, w_key, w_value], axis=1)
    small = jnp.concatenate(
        [patch_mask.astype(BF).reshape(-1)]
        + [gain_one, shift_one, b_output, gain_two, shift_two, b_down]
    )
    small = spread(small)
    qkv_blocks, qkv_index = ring_gather(qkv_shard, 0)
    tok_blocks, cot_blocks = None, None
    fast = images == 1 and count == 4
    if fast:
        near, across = swap(tokens, 1), swap(tokens, 2)
        across, cot_sent = together(across, cotangent)
        cot_across = swap(cot_sent, 2)
        across, cot_sent, qkv_blocks = together(across, cot_sent, qkv_blocks)
        tok_blocks = [tokens, near, across, swap(across, 1)]
    w_wide = place_wide(qkv_blocks, qkv_index, widen(3 * own, 3 * wide_heads))
    split = w_down.shape[0]
    lower = jnp.concatenate([w_down.T, w_output.T], axis=1)
    lower = lax.all_gather(lower, "fsdp", axis=0)
    if fast:
        down_sent, output_cols = cut_lower(lower, me, count, split)
    else:
        output_cols = lower[:, :, split:].transpose(1, 0, 2).reshape(own, width)
        down_sent = [
            lax.dynamic_slice_in_dim(lower[:, :, :split], (me ^ j) * group, group, 0)
            for j in range(count)
        ]
    up_mat = lax.all_gather(w_up, "fsdp", axis=0, tiled=True)

    patches = images * length
    valid = jnp.stack([block[:patches].reshape(images, length) for block in small], axis=1)
    bias_mask = jnp.where(valid > 0, 0.0, NEG).astype(F32)
    vectors = reorder([block[patches:].reshape(6, own) for block in small], me)
    vectors = jnp.concatenate(vectors, axis=1).astype(F32)
    g_one, s_one, b_out, g_two, s_two, b_dn = [vectors[i : i + 1] for i in range(6)]

    expand = widen(own, wide_heads)
    lane = np.arange(3 * wide_heads) % WIDE
    kind = np.arange(3 * wide_heads) // wide_heads
    factor = np.where(kind == 0, SCALE * LOG2E, 1.0).astype(np.float32)
    ones = (kind == 0) & (lane == MASK_AT)
    ones |= (kind == 1) & (lane >= LSE_AT) & (lane < LSE_AT + 3)
    ones |= (kind == 2) & (lane >= SUM_AT) & (lane < SUM_AT + 3)
    at_mask = ((kind == 1) & (lane == MASK_AT)).astype(np.float32)

    def widen_vector(vector):
        shaped = vector.astype(F32).reshape(heads, HEAD)
        return jnp.pad(shaped, ((0, 0), (0, WIDE - HEAD))).reshape(-1)

    def narrow(vector):
        return vector.reshape(heads, WIDE)[:, :HEAD].reshape(-1)

    bias_wide = jnp.concatenate(
        [widen_vector(b_query), jnp.zeros((wide_heads,), F32), widen_vector(b_value)]
    )
    bias_wide = bias_wide * factor + ones.astype(np.float32)

    single = images == 1
    down_exchanged = [down_sent[0]] + [swap(down_sent[j], j) for j in range(1, count)]
    cot_begun = (cot_sent, None, cot_across) if fast else None
    w_turned = w_wide.T

    def absolute_rows(grad):
        parts = reorder(jnp.split(grad.astype(BF), count, axis=0), me)
        return jnp.concatenate(parts, axis=0)

    def token_grads(tokens, residual, grad_norm):
        normed, inverse = norm_parts(tokens.astype(F32))
        return (residual + norm_back(grad_norm, normed, inverse, g_one)).astype(BF)

    def scatter_up(up_grad):
        blocks = up_grad if fast else up_grad.astype(BF).reshape(fcount, width // fcount, -1)
        return lax.psum_scatter(blocks, "fsdp", scatter_dimension=0)

    def send_down(down_grad):
        if fast:
            sent = cut_down(down_grad, me, count, group)
            return [sent[0]] + [swap(sent[j], j) for j in range(1, count)]
        shaped = down_grad.astype(BF).reshape(width, group, -1).transpose(1, 0, 2)

        def cols(j):
            return lax.dynamic_slice_in_dim(shaped, (me ^ j) * own, own, 1)

        return [cols(0)] + [swap(cols(j), j) for j in range(1, count)]

    def merge_down(got):
        if fast:
            return merge_blocks(got, me)
        return jnp.concatenate(reorder(got, me), axis=0)

    def run(tokens, bias_mask, cotangent, tok_blocks=None):
        images = tokens.shape[0]
        if tok_blocks is None:
            tok_blocks = spread(tokens)
        tok_all = jnp.stack(tok_blocks, axis=1)
        normed, _ = norm_parts(tok_all.astype(F32))
        h_one = (normed * g_one + s_one).astype(BF)
        product = jnp.einsum("ijld,de->ijle", h_one, w_wide, preferred_element_type=F32)
        qkv = (product * factor + bias_wide + bias_mask[..., None] * at_mask).astype(BF)
        if fast:
            qkv, cot_across, down_own, turned = together(
                qkv, cot_begun[2], down_sent[0], w_turned
            )
            down_parts = [down_own] + down_exchanged[1:]
            cot_blocks = [cotangent, swap(cot_begun[0], 1), cot_across, swap(cot_across, 1)]
        else:
            cot_blocks = spread(cotangent)
            down_parts, turned = down_exchanged, w_turned
        output_parts = spread(output_cols)
        up_turned = up_mat.T
        cot_all = jnp.stack(cot_blocks, axis=1)

        kept_middle = ()
        halves = 2 if heads % 2 == 0 else 1
        step = heads // halves
        mixed, *kept_attend = attend(qkv, wide_heads, 0, step, ())
        mixed_blocks = [[block] for block in spread(mixed)]
        if halves == 2:
            kept_attend, down_parts, output_parts = together(
                kept_attend, down_parts, output_parts
            )
            mixed, *kept_attend = attend(qkv, wide_heads, step, step, kept_attend)
            for pieces, block in zip(mixed_blocks, spread(mixed)):
                pieces.append(block)
        query_wide, mixed_exact = kept_attend
        down_in, output_in = down_parts, output_parts
        if fast:
            down_mat, down_turned, output_mat = build_weights(down_in, output_in, me)
        else:
            down_turned = jnp.stack(reorder(down_in, me)).transpose(0, 2, 1, 3)
            down_turned = down_turned.reshape(width, -1)
            down_mat = down_turned.T
            output_mat = jnp.concatenate(reorder(output_in, me), axis=0).T
            output_mat = output_mat.reshape(count, own, width)
        own_rows = lax.dynamic_index_in_dim(output_mat, me, 0, keepdims=False)
        output_wide = mm(own_rows.T, expand).astype(BF)
        weights = (
            me,
            output_mat,
            up_mat,
            up_turned,
            down_mat,
            down_turned,
            b_out,
            g_two,
            s_two,
            b_up.astype(F32)[None],
        )
        def grad_rows(c, hidden_grad, x_own):
            grad_norm = hidden_grad.astype(F32)
            normed_two, inverse_two = norm_parts(x_own)
            cot_own = cotangent[:, c * rows : (c + 1) * rows].astype(F32)
            residual = cot_own + norm_back(grad_norm, normed_two, inverse_two, g_two)
            grad_attn = residual.astype(BF)
            sums = jnp.stack(
                [
                    jnp.sum(grad_norm * normed_two, axis=(0, 1)),
                    jnp.sum(grad_norm, axis=(0, 1)),
                    jnp.sum(grad_attn.astype(F32), axis=(0, 1)),
                    jnp.sum(cot_own, axis=(0, 1)),
                ]
            )
            return residual, grad_attn, sums

        out_parts, x_parts = [], []
        grad_attn_all, grad_residual = [], []
        hidden_parts = []
        early, up_bias_grad = 0.0, 0.0
        for c in range(CHUNKS):
            result = middle(mixed_blocks, tok_all, cot_all, weights, c, kept_middle)
            kept_middle, x_own, gb = result[:4], result[4], result[5]
            hidden_parts.append(list(result[6 : 6 + count]))
            out_parts.append(result[6 + count :])
            x_parts.append(x_own)
            up_bias_grad = up_bias_grad + gb[0]
        h_two, activated, grad_hidden, mixed_all = kept_middle
        blocks = hidden_parts[0]
        if count == 4:
            near_sum, crossing = collect_pair(blocks)
            h_two, crossing = together(h_two, crossing)
            incoming = swap(crossing, 2)
        else:
            near_sum, incoming = collect(blocks), jnp.zeros((), F32)
        up_grad = jnp.einsum(
            "ijld,ijlf->df",
            h_two,
            grad_hidden,
            preferred_element_type=F32,
        ).astype(BF if single else F32)
        if fast:
            up_grad = hold_rows(up_grad, me, fcount)
        incoming, up_grad = together(incoming, up_grad)
        if single:
            up_grad = scatter_up(up_grad)
        hidden_grad = near_sum + incoming.astype(F32)
        residual, grad_attn, early = grad_rows(0, hidden_grad, x_parts[0])
        grad_attn, activated = together(grad_attn, activated)
        down_grad = jnp.einsum(
            "ijld,ijlf->df",
            cot_all,
            activated,
            preferred_element_type=F32,
        ).astype(BF if single else F32)
        grad_residual.append(residual)
        if fast:
            across = swap(grad_attn, 2)
            near = swap(grad_attn, 1)
            across, down_grad = together(across, down_grad)
            attn_blocks = [grad_attn, near, across, swap(across, 1)]
        else:
            attn_blocks = spread(grad_attn)
        grad_attn_all = jnp.stack(attn_blocks, axis=1)
        grad_mixed = mixed_back(grad_attn_all, output_wide, mixed_exact, 0, ())

        wide_shape = (images, count * length, wide_heads)
        query_in = query_wide.reshape(wide_shape)
        grad_in = grad_mixed.reshape(wide_shape)
        flat_qkv = qkv.reshape(images, count * length, 3 * wide_heads)
        grad_attn_cols = lax.dynamic_slice_in_dim(grad_attn_all, me * own, own, 3)
        output_grad = jnp.einsum(
            "ijle,ijld->ed", mixed_all, grad_attn_cols, preferred_element_type=F32
        )
        grad_in, out_blocks, down_grad = together(grad_in, list(out_parts[0]), down_grad)
        if single:
            down_grad = send_down(down_grad)
            if fast:
                output_grad = absolute_rows(output_grad)
            grad_in, up_grad, output_grad, early = together(
                grad_in, up_grad, output_grad, early
            )
        if count == 4:
            out_sum, out_across = collect_pair(out_blocks)
            grad_in, out_across = together(grad_in, out_across)
            out_incoming = swap(out_across, 2)
        else:
            out_sum, out_incoming = collect(out_blocks), jnp.zeros((), F32)
        first = attend_back(query_in, grad_in, flat_qkv, 0, step)
        pieces = [first]
        if halves == 2:
            first, down_grad = together(first, down_grad)
            if single:
                down_grad = merge_down(down_grad)
            query_in, down_grad = together(query_in, down_grad)
            pieces = [first, attend_back(query_in, grad_in, flat_qkv, step, step)]
            pieces, out_incoming = together(pieces, out_incoming)
        elif single:
            down_grad = merge_down(down_grad)
        out_sum = out_sum + out_incoming.astype(F32)
        grads = [
            [piece[k].reshape(images, count, length, -1) for piece in pieces] for k in range(3)
        ]
        result = project_back(grads, tok_all, turned, g_one, s_one, expand.T)
        qkv_grad, late, bias_grads = result[count:]
        if fast:
            norm_near, norm_across = collect_pair(list(result[:count]))
            ends = (grad_residual[0], norm_near, swap(norm_across, 2))
        else:
            grad_norm = collect(list(result[:count])).astype(F32)
            ends = token_grads(tokens, grad_residual[0], grad_norm)

        layer_out = (jnp.concatenate(x_parts, axis=1) + out_sum.astype(F32) + b_dn).astype(BF)
        qkv_grad = qkv_grad if single else qkv_grad.astype(F32)
        sums = (down_grad, up_grad, output_grad, qkv_grad, early, up_bias_grad, late, bias_grads)
        return sums, (layer_out, ends)

    if images == 1:
        sums, (layer_out, ends) = run(tokens, bias_mask, cotangent, tok_blocks)
    else:
        items = (tokens[:, None], bias_mask[:, None], cotangent[:, None])
        shapes = jax.eval_shape(lambda item: run(*item)[0], jax.tree.map(lambda a: a[0], items))
        empty = jax.tree.map(lambda a: jnp.zeros(a.shape, a.dtype), shapes)

        def step(totals, item):
            sums, results = run(*item)
            return jax.tree.map(jnp.add, totals, sums), results

        sums, (layer_out, ends) = lax.scan(step, empty, items)
        layer_out = layer_out[:, 0]
        grad_tokens = ends[:, 0]
    down_grad, up_grad, output_grad, qkv_grad, early, up_bias_grad, late, bias_grads = sums

    down_pieces = down_grad if single else merge_down(send_down(down_grad))
    final_up = (up_grad if single else scatter_up(up_grad)).astype(F32)
    final_down = lax.psum_scatter(down_pieces, "fsdp", scatter_dimension=0)
    if not fast:
        output_grad = absolute_rows(output_grad)
    qkv_grad = qkv_grad.astype(BF).reshape(3, fcount, width // fcount, own)
    output_grad = output_grad.reshape(fcount, width // fcount, own)

    def four_parts(f):
        parts = lax.dynamic_index_in_dim(qkv_grad, f, 1, keepdims=False)
        last = lax.dynamic_index_in_dim(output_grad, f, 0, keepdims=True)
        return jnp.concatenate([parts, last], axis=0)


    def to_owner(stack):
        kinds = stack.shape[0]
        parts = jnp.split(stack.reshape(kinds, count, own), count, axis=1)
        parts = reorder([part[:, 0] for part in parts], me)
        total = parts[0]
        for j in range(1, count):
            total = total + swap(parts[j], j)
        return jnp.concatenate(
            [total.reshape(-1)] + [narrow(g) for g in bias_grads] + [up_bias_grad]
        )

    bias_grads = [bias_grads[0, i * wide_heads : (i + 1) * wide_heads] for i in (0, 2)]
    four, final_down, vectors = ring_reduce(
        four_parts,
        0,
        final_down,
        jnp.concatenate([early, late], axis=0),
        [to_owner] + sum_steps(),
    )
    final_down = final_down.astype(F32).T
    if fast:
        ends, four = together(ends, four)
        residual, norm_near, norm_incoming = ends
        grad_tokens = token_grads(tokens, residual, norm_near + norm_incoming.astype(F32))
    (
        gain_two_grad,
        shift_two_grad,
        b_output_grad,
        b_down_grad,
        gain_one_grad,
        shift_one_grad,
        b_query_grad,
        b_value_grad,
    ) = [vectors[i * own : (i + 1) * own] for i in range(8)]
    b_up_grad = vectors[8 * own :]
    final_query, final_key, final_value, final_output = [four[i] for i in range(4)]
    return (
        layer_out,
        grad_tokens,
        gain_one_grad,
        shift_one_grad,
        final_query,
        b_query_grad,
        final_key,
        final_value,
        b_value_grad,
        final_output,
        b_output_grad,
        gain_two_grad,
        shift_two_grad,
        final_up,
        b_up_grad,
        final_down,
        b_down_grad,
    )


def solution(mesh):
    rows = P("fsdp", "seq", None)
    matrix = P("fsdp", "seq")
    vector = P("seq")
    return jax.shard_map(
        local,
        mesh=mesh,
        in_specs=(
            rows,
            matrix,
            vector,
            vector,
            matrix,
            vector,
            matrix,
            matrix,
            vector,
            matrix,
            vector,
            vector,
            vector,
            matrix,
            vector,
            matrix,
            vector,
            rows,
        ),
        out_specs=(
            rows,
            rows,
            vector,
            vector,
            matrix,
            vector,
            matrix,
            matrix,
            vector,
            matrix,
            vector,
            vector,
            vector,
            matrix,
            vector,
            matrix,
            vector,
        ),
        check_vma=False,
    )
```
